768 devices in a mesh: curve: 24 (over x, z_lo), col: 32 (over y, z_hi, core).
Axes of the slice: x: 4, y: 8, z: 12 (z_hi: 2, z_lo: 6; z = z_hi * 6 + z_lo), core: 2. Of those that a mesh axis runs over, the one named last changes fastest.
Arguments:
- evolving_state_array: float32 [5, 8, 589824], P(None, None, ('curve', 'col')), may hold values from -6 to 6
- point_id: int32 [589824], P(('curve', 'col')), may hold values from 0 to 143, as said below
- neighbours: int32 [8, 36864], P(None, ('curve', 'col')), may hold values from -1 to 36863, as said below
- jacobian: float32 [589824], P(('curve', 'col')), may hold values from 0.7 to 1.4
- inverse_metric: float32 [4, 589824], P(None, ('curve', 'col')), may hold values from -0.3 to 0.3
- coriolis: float32 [589824], P(('curve', 'col')), may hold values from -2 to 2
- column_slot: int32 [589824], P(('curve', 'col')), may hold values from 0 to 24575, as said below
Outputs:
- updated: float32 [5, 8, 589824], P(None, None, ('curve', 'col'))
- physics: float32 [5, 8, 589824], P(None, None, ('curve', 'col'))
The draws below stay inside these ranges and needn't reach their ends.
Inputs may be any that keep to these rules, and one draw needn't show every extreme that they name: `point_id`: the points lie on a lattice around the band of 96 rows and 384 elements around. Among the points of one element and its listed neighbours, coinciding points of different elements share one number and all other points have distinct numbers; numbers repeat farther away. neighbours[k, e] names the element beside e toward the lower and the higher position around the band, the lower and the higher row, then the diagonal ones (lower row and lower position, lower row and higher position, higher row and lower position, higher row and higher position); -1 where the band ends. The lists are symmetric, the band closes around, and an element shares points only with itself and its listed ones. Element g lies on device g // 48 of curve+col; device d holds exactly the elements of rows 4 (d // 32) to 4 (d // 32) + 3 at positions 12 (d % 32) to 12 (d % 32) + 11 around the band, in some order. Within each group of rows, column_slot maps the group's columns one to one onto the slots; slot s belongs to device s // 768 of the group's col axis. Every device receives 768 columns and sends at most 72 to any one device of its group; that count is reached.
All inputs are finite; a program needn't handle non-finite values.
Results may differ from the reference program's by a relative error of at most 0.0003.
Values sent between devices are 32-bit elements; how exact they have to be, the bound alone decides.
No kernel may reach another device: no remote copies, remote signals or barrier semaphores. Data moves between devices by JAX's collectives and lax.ppermute only.
A program may use at most 32 MiB of HBM per device.

```python
import math
import jax
import jax.numpy as jnp
import numpy as np
from jax import lax

ROWS_DEV = 4
CYCLE_DEV = 12
LEV = 8
FIELDS = 5
E_DEV = 48
POINTS_DEV = 768
ELEMS = 36864
POINTS = 589824
CAP_PHYS = 72
N_CURVE = 24
N_COL = 32
DEVICES = 768


def band_geometry(key):
    rows_total = ROWS_DEV * N_CURVE
    cycle_total = CYCLE_DEV * N_COL
    scores = jax.random.randint(key, (DEVICES, E_DEV), 0, 1 << 16) * E_DEV + jnp.arange(E_DEV, dtype=jnp.int32)[None, :]
    placement_order = jnp.argsort(scores, axis=1).astype(jnp.int32)
    row_index = jnp.arange(rows_total, dtype=jnp.int32)[:, None]
    cycle_index = jnp.arange(cycle_total, dtype=jnp.int32)[None, :]
    device = row_index // ROWS_DEV * N_COL + cycle_index // CYCLE_DEV
    within = row_index % ROWS_DEV * CYCLE_DEV + cycle_index % CYCLE_DEV
    global_index = device * E_DEV + placement_order[device, within]
    local_row = jnp.arange(4, dtype=jnp.int32)[:, None]
    local_cycle = jnp.arange(4, dtype=jnp.int32)[None, :]
    vertical = (3 * row_index[:, :, None, None] + local_row) % 12
    beside_all = (3 * cycle_index[:, :, None, None] + local_cycle) % 12
    numbers = vertical * 12 + beside_all
    places = global_index[:, :, None, None] * 16 + local_row * 4 + local_cycle
    point_id = jnp.zeros((ELEMS * 16,), jnp.int32).at[places.reshape(-1)].set(numbers.reshape(-1))
    step_pairs = ((0, -1), (0, 1), (-1, 0), (1, 0), (-1, -1), (-1, 1), (1, -1), (1, 1))
    neighbour_rows = []
    for row_step, cycle_step in step_pairs:
        other_row = row_index + row_step
        present = (other_row >= 0) & (other_row < rows_total)
        other_cycle = (cycle_index + cycle_step) % cycle_total
        found_index = global_index[jnp.clip(other_row, 0, rows_total - 1), other_cycle]
        entry_value = jnp.where(present, found_index, -1)
        neighbour_rows.append(jnp.zeros((ELEMS,), jnp.int32).at[global_index.reshape(-1)].set(entry_value.reshape(-1)))
    return (point_id, jnp.stack(neighbour_rows))


def draw_point_id(key, part):
    geometry = band_geometry(key)
    return geometry[0]


def draw_neighbours(key, part):
    geometry = band_geometry(key)
    return geometry[1]


def draw_column_slot(key, part):
    key = jax.random.fold_in(key, 23)
    key_peak, key_spread, key_source, key_target = jax.random.split(key, 4)
    remaining = POINTS_DEV - CAP_PHYS
    base_share = remaining // (N_COL - 1)
    remainder = remaining - base_share * (N_COL - 1)
    spread = max(base_share // 2, 1)
    wobble = jax.random.randint(key_spread, (N_CURVE, N_COL - 1), 0, spread)
    shares = base_share + wobble - jnp.roll(wobble, 1, axis=1) + (jnp.arange(N_COL - 1, dtype=jnp.int32) < remainder).astype(jnp.int32)[None, :]
    extended = jnp.concatenate([shares, jnp.full((N_CURVE, 1), CAP_PHYS, jnp.int32)], axis=1)
    peak_offset = jax.random.randint(key_peak, (N_CURVE, 1), 0, N_COL)
    offsets = jnp.arange(N_COL, dtype=jnp.int32)[None, :]
    amounts = jnp.take_along_axis(extended, (offsets - peak_offset - 1) % N_COL, axis=1)
    pair_offset = (jnp.arange(N_COL, dtype=jnp.int32)[None, :] - jnp.arange(N_COL, dtype=jnp.int32)[:, None]) % N_COL
    sent_counts = amounts[:, pair_offset]
    boundaries = jnp.cumsum(sent_counts, axis=2)
    before = boundaries - sent_counts
    rank_position = jnp.arange(POINTS_DEV, dtype=jnp.int32)
    target = jnp.sum((rank_position[None, None, :, None] >= boundaries[:, :, None, :]).astype(jnp.int32), axis=3)
    within = rank_position[None, None, :] - jnp.take_along_axis(before, target, axis=2)
    incoming_start = jnp.cumsum(sent_counts, axis=1) - sent_counts
    start_here = jnp.take_along_axis(incoming_start, target, axis=2)
    target_scores = jax.random.randint(key_target, (N_CURVE, N_COL, POINTS_DEV), 0, 1 << 16) * POINTS_DEV + rank_position[None, None, :]
    target_order = jnp.argsort(target_scores, axis=2).astype(jnp.int32)
    flat_place = target * POINTS_DEV + start_here + within
    slot_within = jnp.take_along_axis(target_order.reshape(N_CURVE, N_COL * POINTS_DEV), flat_place.reshape(N_CURVE, N_COL * POINTS_DEV), axis=1).reshape(N_CURVE, N_COL, POINTS_DEV)
    slot_value = target * POINTS_DEV + slot_within
    source_scores = jax.random.randint(key_source, (N_CURVE, N_COL, POINTS_DEV), 0, 1 << 16) * POINTS_DEV + rank_position[None, None, :]
    source_order = jnp.argsort(source_scores, axis=2).astype(jnp.int32)
    inverse_order = jnp.argsort(source_order, axis=2).astype(jnp.int32)
    return jnp.take_along_axis(slot_value, inverse_order, axis=2).reshape(POINTS)


def block_levels(key, shape, pieces, least, largest):
    factor_of = 1.0
    for dim, parts in pieces:
        draws = jax.random.uniform(jax.random.fold_in(jax.random.fold_in(key, 6), dim), (parts,), jnp.float32, least / len(pieces), largest / len(pieces))
        factor_of = factor_of * jnp.repeat(jnp.exp(draws), shape[dim] // parts).reshape((-1,) + (1,) * (len(shape) - 1 - dim))
    return factor_of


def noise(stream_key, extent, deviation, most, cuts=(), kind=jnp.bfloat16):
    entries = jax.random.normal(stream_key, extent, jnp.float32) * deviation
    if len(cuts) > 0:
        entries = block_levels(stream_key, extent, cuts, -0.22, 0.18) * entries
    return jnp.clip(entries, min=-most, max=most).astype(kind)


def setup_inputs(seed: int = 0) -> dict:
    splits = jax.random.split(jax.random.key(seed), 8)
    return {
        "evolving_state_array": noise(splits[0], (FIELDS, LEV, POINTS), 1.0, 6.0, ((2, 768),), jnp.float32),
        "point_id": draw_point_id(jax.random.fold_in(splits[7], 71), 0),
        "neighbours": draw_neighbours(jax.random.fold_in(splits[7], 71), 0),
        "jacobian": jnp.clip(jnp.exp(math.log(1.4) - 0.6931472 * jax.random.uniform(splits[3], (POINTS,), jnp.float32) ** block_levels(splits[3], (POINTS,), ((0, 768),), -0.2, 0.2)), 0.7, 1.4),
        "inverse_metric": jnp.clip(jax.random.uniform(splits[4], (4, POINTS), jnp.float32, -0.3, 0.3) * block_levels(splits[4], (4, POINTS), ((1, 768),), -0.4, 0.0), -0.3, 0.3),
        "coriolis": jnp.clip(jax.random.uniform(splits[5], (POINTS,), jnp.float32, -2.0, 2.0) * block_levels(splits[5], (POINTS,), ((0, 768),), -0.4, 0.0), -2.0, 2.0),
        "column_slot": draw_column_slot(jax.random.fold_in(splits[7], 71), 0),
    }


TIME_STEP = 0.1
HYPER_NU = 0.002

def gll_tables():
    root_fifth = 1.0 / math.sqrt(5.0)
    gll_nodes = np.array([-1.0, -root_fifth, root_fifth, 1.0])
    weights = np.array([1.0, 5.0, 5.0, 1.0]) / 6.0
    diff_table = np.zeros((4, 4))
    for target in range(4):
        for source in range(4):
            if target == source:
                diff_table[target, source] = sum((1.0 / (gll_nodes[target] - gll_nodes[other_node]) for other_node in range(4) if other_node != target))
            else:
                numerator_part = np.prod([gll_nodes[target] - gll_nodes[other_node] for other_node in range(4) if other_node != target])
                denominator_part = np.prod([gll_nodes[source] - gll_nodes[other_node] for other_node in range(4) if other_node != source])
                diff_table[target, source] = numerator_part / (denominator_part * (gll_nodes[target] - gll_nodes[source]))
    return (diff_table, weights)

def cycle_derivative(values, nodal_slope_operator):
    return jnp.einsum('im,...jm->...ji', nodal_slope_operator, values, precision=lax.Precision.HIGHEST)

def row_derivative(values, nodal_slope_operator):
    return jnp.einsum('jm,...mi->...ji', nodal_slope_operator, values, precision=lax.Precision.HIGHEST)

def spatial_slope_values(values, surface_distance_form, nodal_slope_operator):
    along_cycle = cycle_derivative(values, nodal_slope_operator)
    along_rows = row_derivative(values, nodal_slope_operator)
    return (surface_distance_form[0] * along_cycle + surface_distance_form[2] * along_rows, surface_distance_form[1] * along_cycle + surface_distance_form[3] * along_rows)

def divergence(first_part, second_part, surface_distance_form, jacobian, nodal_slope_operator):
    cycle_flux = jacobian * (surface_distance_form[0] * first_part + surface_distance_form[1] * second_part)
    row_flux = jacobian * (surface_distance_form[2] * first_part + surface_distance_form[3] * second_part)
    return (cycle_derivative(cycle_flux, nodal_slope_operator) + row_derivative(row_flux, nodal_slope_operator)) / jacobian

def laplacian(values, surface_distance_form, jacobian, nodal_slope_operator):
    first_part, second_part = spatial_slope_values(values, surface_distance_form, nodal_slope_operator)
    return divergence(first_part, second_part, surface_distance_form, jacobian, nodal_slope_operator)

def tendencies(evolving_state_array, surface_distance_form, jacobian, coriolis, nodal_slope_operator):
    eastward_wind_speed = evolving_state_array[0]
    northward_wind_speed = evolving_state_array[1]
    thermal_state_values = evolving_state_array[2]
    thickness = evolving_state_array[3]
    tracer = evolving_state_array[4]
    motion_work_density = 0.5 * (eastward_wind_speed * eastward_wind_speed + northward_wind_speed * northward_wind_speed) + thermal_state_values
    first_grad, second_grad = spatial_slope_values(motion_work_density, surface_distance_form, nodal_slope_operator)
    initial_thermal_addend, latter_thermal_addend = spatial_slope_values(thermal_state_values, surface_distance_form, nodal_slope_operator)
    tendency = jnp.stack([-first_grad + coriolis * northward_wind_speed, -second_grad - coriolis * eastward_wind_speed, -(eastward_wind_speed * initial_thermal_addend + northward_wind_speed * latter_thermal_addend), -divergence(thickness * eastward_wind_speed, thickness * northward_wind_speed, surface_distance_form, jacobian, nodal_slope_operator), -divergence(tracer * eastward_wind_speed, tracer * northward_wind_speed, surface_distance_form, jacobian, nodal_slope_operator)])
    smoothing = jnp.stack([laplacian(evolving_state_array[component], surface_distance_form, jacobian, nodal_slope_operator) for component in range(FIELDS)])
    return (tendency, smoothing)

def sum_shared(fields, point_id, neighbours, point_mass):
    field_count = fields.shape[0]
    element_ids = point_id.reshape(ELEMS, 16)
    element_mass = point_mass.reshape(ELEMS, 16)
    weighted = (fields * point_mass).reshape(field_count, ELEMS, 16)
    group_size = E_DEV * N_COL

    def one_group(first_element):
        elements = first_element + jnp.arange(group_size, dtype=jnp.int32)
        listed = neighbours[:, elements].T
        present = listed >= 0
        clipped = jnp.maximum(listed, 0)
        own_ids = element_ids[elements]
        far_ids = element_ids[clipped]
        matched = ((own_ids[:, None, :, None] == far_ids[:, :, None, :]) & present[:, :, None, None]).astype(jnp.float32)
        numerator = weighted[:, elements] + jnp.einsum('ekim,fekm->fei', matched, weighted[:, clipped], precision=lax.Precision.HIGHEST)
        denominator = element_mass[elements] + jnp.einsum('ekim,ekm->ei', matched, element_mass[clipped], precision=lax.Precision.HIGHEST)
        return numerator / denominator
    starts = jnp.arange(N_CURVE, dtype=jnp.int32) * group_size
    results = lax.map(one_group, starts)
    return jnp.transpose(results, (1, 0, 2, 3)).reshape(field_count, POINTS)

def reference(evolving_state_array, point_id, neighbours, jacobian, inverse_metric, coriolis, column_slot):
    diff_table, weights = gll_tables()
    nodal_slope_operator = jnp.asarray(diff_table, dtype=jnp.float32)
    point_weight = jnp.asarray(np.outer(weights, weights).reshape(16), dtype=jnp.float32)
    point_mass = jacobian * jnp.tile(point_weight, ELEMS)
    shape_elements = (ELEMS, 4, 4)
    surface_distance_form = jnp.stack([1.0 + inverse_metric[0], inverse_metric[1], inverse_metric[2], 1.0 + inverse_metric[3]]).reshape((4,) + shape_elements)
    element_jacobian = jacobian.reshape(shape_elements)
    element_coriolis = coriolis.reshape(shape_elements)
    element_state = evolving_state_array.reshape((FIELDS, LEV) + shape_elements)
    tendency, smoothing = tendencies(element_state, surface_distance_form, element_jacobian, element_coriolis, nodal_slope_operator)
    joined = jnp.concatenate([tendency, smoothing]).reshape(2 * FIELDS * LEV, POINTS)
    summed = sum_shared(joined, point_id, neighbours, point_mass)
    tendency_sum = summed[:FIELDS * LEV].reshape(FIELDS, LEV, POINTS)
    smoothing_sum = summed[FIELDS * LEV:].reshape((FIELDS, LEV) + shape_elements)
    damping_local = jnp.stack([laplacian(smoothing_sum[component], surface_distance_form, element_jacobian, nodal_slope_operator) for component in range(FIELDS)]).reshape(FIELDS * LEV, POINTS)
    damping = sum_shared(damping_local, point_id, neighbours, point_mass).reshape(FIELDS, LEV, POINTS)
    midway = evolving_state_array + TIME_STEP * tendency_sum
    updated = midway - TIME_STEP * HYPER_NU * damping
    group_base = jnp.arange(POINTS, dtype=jnp.int32) // (N_COL * POINTS_DEV) * (N_COL * POINTS_DEV)
    physics = jnp.zeros_like(updated).at[:, :, group_base + column_slot].set(updated)
    return (updated, physics)
```

```python
import functools
import math

import jax
import jax.numpy as jnp
import numpy as np
from jax import lax
from jax.experimental import pallas as pl
from jax.experimental.pallas import tpu as pltpu
from jax.sharding import PartitionSpec as P

FIELDS = 5
LEV = 8
STATE = FIELDS * LEV
TILE = 48
LANES = 128
ELEMS_DEV = 48
POINTS_DEV = 768
N_COL = 32
CAP = 72
CAP_ROWS = CAP // 3
TIME_STEP = 0.1
HYPER_NU = 0.002
F32 = jnp.float32
BF16 = jnp.bfloat16
VMEM_LIMIT = 48 * 1024 * 1024


def gll_tables():
    root_fifth = 1.0 / math.sqrt(5.0)
    nodes = np.array([-1.0, -root_fifth, root_fifth, 1.0])
    weights = np.array([1.0, 5.0, 5.0, 1.0]) / 6.0
    table = np.zeros((4, 4))
    for i in range(4):
        for m in range(4):
            if i == m:
                table[i, m] = sum(1.0 / (nodes[i] - nodes[o]) for o in range(4) if o != i)
            else:
                upper = np.prod([nodes[i] - nodes[o] for o in range(4) if o != i])
                lower = np.prod([nodes[m] - nodes[o] for o in range(4) if o != m])
                table[i, m] = upper / (lower * (nodes[i] - nodes[m]))
    return table, weights


def two_parts(matrix):
    upper = matrix.astype(np.float32).astype(jnp.bfloat16)
    lower = (matrix - upper.astype(np.float64)).astype(np.float32).astype(jnp.bfloat16)
    return upper, lower


@functools.lru_cache(maxsize=None)
def operators():
    table, weights = gll_tables()
    eye4, eye8 = np.eye(4), np.eye(8)
    along_cycle = np.kron(eye4, table.T)
    along_rows = np.kron(table.T, eye4)
    grad = np.concatenate([np.kron(eye8, along_cycle), np.kron(eye8, along_rows)], axis=1)
    weight = np.diag(np.outer(weights, weights).reshape(16))
    div = np.concatenate(
        [np.kron(eye8, along_cycle @ weight), np.kron(eye8, along_rows @ weight)], axis=0
    )
    join = np.eye(256)
    for place in range(15):
        for j in range(4):
            low, high = place * 16 + 4 * j + 3, place * 16 + 16 + 4 * j
            join[low, high] = 1.0
            join[high, low] = 1.0
    both = np.zeros((512, 256))
    both[:256, :128] = div
    both[256:, 128:] = div
    div_join = both @ join
    grad_hi, grad_lo = two_parts(grad)
    div_hi, div_lo = two_parts(div_join)
    mass_weight = np.tile(np.outer(weights, weights).reshape(16), 8).astype(np.float32)
    return (
        np.concatenate([grad_hi, grad_hi], axis=0),
        grad_lo,
        div_hi,
        div_lo,
        join.astype(jnp.bfloat16),
        np.broadcast_to(mass_weight, (8, 128)).copy(),
    )


def dot(left, right):
    return jnp.dot(left, right, preferred_element_type=F32)


def dot_last(left, right):
    return lax.dot_general(left, right, (((1,), (1,)), ((), ())), preferred_element_type=F32)


def halves(value):
    upper = value.astype(BF16)
    lower = (value - upper.astype(F32)).astype(BF16)
    return upper, lower


def lane_iota(shape):
    return lax.broadcasted_iota(jnp.int32, shape, 1)


def row_iota(shape):
    return lax.broadcasted_iota(jnp.int32, shape, 0)


def chain_length(local, index, doublings):
    present = jnp.broadcast_to(local.astype(F32), (8, ELEMS_DEV))
    hit = (row_iota((ELEMS_DEV, ELEMS_DEV)) == index) & local
    step = hit.astype(F32).astype(BF16)
    length = present
    for k in range(doublings):
        length = length + dot(length.astype(BF16), step)
        if k + 1 < doublings:
            step = dot(step, step).astype(BF16)
    return length


def arrange_kernel(state_ref, geo_ref, near_ref, low_ref, high_ref, right_ref, left_ref, place_ref):
    base = (lax.axis_index("curve") * N_COL + lax.axis_index("col")) * ELEMS_DEV
    index = near_ref[...] - base
    local = (index >= 0) & (index < ELEMS_DEV)
    place = chain_length(local[0:1], index[0:1], 4)
    row = chain_length(local[2:3], index[2:3], 2)
    spot = row * 16.0 + place + 2.0
    points = (ELEMS_DEV, POINTS_DEV)
    spread = (lane_iota(points) // 16 == row_iota(points)).astype(F32).astype(BF16)
    spot_of_point = dot(spot.astype(BF16), spread)[0:1].astype(jnp.int32)
    target = spot_of_point * 16 + lane_iota((1, POINTS_DEV)) % 16
    place_ref[...] = jnp.broadcast_to(target, (8, POINTS_DEV))
    hits = (row_iota((1024, POINTS_DEV)) == target).astype(F32).astype(BF16)
    values = jnp.concatenate([state_ref[...], geo_ref[...]], axis=0)
    first = values.astype(BF16)
    rest = values - first.astype(F32)
    second = rest.astype(BF16)
    third = (rest - second.astype(F32)).astype(BF16)
    parts = dot_last(jnp.concatenate([first, second, third], axis=0), hits)
    ordered = parts[0:TILE] + parts[TILE : 2 * TILE] + parts[2 * TILE :]
    lane = lane_iota((TILE, LANES))
    to_right = jnp.zeros((TILE, LANES), F32)
    to_left = jnp.zeros((TILE, LANES), F32)
    for r in range(4):
        for g in range(2):
            block = ordered[:, (2 * r + g) * LANES : (2 * r + g + 1) * LANES]
            ref = low_ref if r < 2 else high_ref
            start = ((r % 2) * 2 + g) * TILE
            ref[start : start + TILE, :] = block
            inside = (lane >= 32 * r) & (lane < 32 * r + 32)
            if g == 1:
                to_right = jnp.where(inside, turned(block, 32 * r - 64), to_right)
            else:
                to_left = jnp.where(inside, turned(block, 32 * r - 32), to_left)
    right_ref[...] = to_right
    left_ref[...] = to_left


def turned(block, by):
    by = by % LANES
    return block if by == 0 else pltpu.roll(block, by, 1)


def margin_kernel(low_in, high_in, from_left, from_right, low_ref, high_ref):
    lane = lane_iota((TILE, LANES))
    for r in range(4):
        source = low_in if r < 2 else high_in
        ref = low_ref if r < 2 else high_ref
        start = (r % 2) * 2 * TILE
        first = source[start : start + TILE, :]
        ref[start : start + TILE, :] = jnp.where(lane < 32, turned(from_left[...], -32 * r), first)
        start += TILE
        second = source[start : start + TILE, :]
        ref[start : start + TILE, :] = jnp.where(
            lane >= 96, turned(from_right[...], 96 - 32 * r), second
        )


def send_kernel(slot_ref, map_ref):
    slot = slot_ref[...]
    slot_value = slot.astype(F32)
    device = jnp.floor((slot_value + 0.5) * (1.0 / POINTS_DEV))
    within = slot_value - device * POINTS_DEV
    wanted = jnp.broadcast_to(device.astype(jnp.int32), (N_COL, POINTS_DEV))
    chosen = (wanted == row_iota((N_COL, POINTS_DEV))).astype(F32)
    square = (LANES, LANES)
    upto = (row_iota(square) <= lane_iota(square)).astype(F32)
    count = jnp.concatenate([upto, jnp.ones(square, F32)], axis=1).astype(BF16)
    groups = POINTS_DEV // LANES
    stacked = jnp.concatenate(
        [chosen[:, i * LANES : (i + 1) * LANES] for i in range(groups)], axis=0
    )
    counted = dot(stacked.astype(BF16), count)
    before = jnp.zeros((N_COL, LANES), F32)
    ranks = []
    for i in range(groups):
        rows = counted[i * N_COL : (i + 1) * N_COL]
        here = (rows[:, :LANES] + before) * stacked[i * N_COL : (i + 1) * N_COL]
        ranks.append(jnp.sum(here, axis=0, keepdims=True))
        before = before + rows[:, LANES:]
    rank = jnp.concatenate(ranks, axis=1) - 1.0
    third = (rank >= CAP_ROWS).astype(F32) + (rank >= 2 * CAP_ROWS).astype(F32)
    line = device * CAP_ROWS + rank - third * CAP_ROWS
    lists = [jnp.where(third == float(k), line, -1.0) for k in range(3)]
    filler = jnp.zeros((4, POINTS_DEV), F32)
    map_ref[...] = jnp.concatenate(lists + [within + 1.0, filler], axis=0)


def fluxes(slope, coefficients):
    along_cycle, along_rows = slope[:, :LANES], slope[:, LANES:]
    caa, cab, cbb = coefficients
    return caa * along_cycle + cab * along_rows, cab * along_cycle + cbb * along_rows


def gradient(values, grad2_ref, grad_lo_ref):
    upper, lower = halves(values)
    return dot(jnp.concatenate([upper, lower], axis=1), grad2_ref[...]) + dot(
        upper, grad_lo_ref[...]
    )


def divergence_joined(values, div_hi_ref, div_lo_ref):
    upper, lower = halves(values)
    return dot(upper, div_hi_ref[...]) + dot(lower, div_hi_ref[...]) + dot(upper, div_lo_ref[...])


def rows_joined(below, here, above, low_mask, high_mask):
    parts = []
    for g in range(2):
        part = slice(g * LANES, (g + 1) * LANES)
        parts.append(
            here[:, part]
            + low_mask * turned(below[:, part], -12)
            + high_mask * turned(above[:, part], 12)
        )
    return parts


def section_kernel(
    below_ref,
    low_ref,
    high_ref,
    above_ref,
    place_ref,
    map_ref,
    grad2_ref,
    grad_lo_ref,
    div_hi_ref,
    div_lo_ref,
    join_ref,
    weight_ref,
    updated_ref,
    send_ref,
    slopes,
    flux,
    plain,
    coefs,
):
    quarters = (below_ref, low_ref, high_ref, above_ref)

    def tile(r, g, start=0, size=TILE):
        offset = ((r % 2) * 2 + g) * TILE + start
        return quarters[r // 2][offset : offset + size, :]

    cells = [(r, g) for r in range(8) for g in range(2)]
    stacked = []
    for r, g in cells:
        zonal, meridional = tile(r, g, 0, 8), tile(r, g, 8, 8)
        energy = 0.5 * (zonal * zonal + meridional * meridional) + tile(r, g, 16, 8)
        stacked += [tile(r, g, 0, STATE), energy]
    slopes[...] = gradient(jnp.concatenate(stacked, axis=0), grad2_ref, grad_lo_ref)

    for r, g in cells:
        def line(k):
            return jnp.broadcast_to(tile(r, g, STATE + k, 1), (8, LANES))

        jacobian, coriolis = line(0), line(1)
        m11, m12, m21, m22 = 1.0 + line(2), line(3), line(4), 1.0 + line(5)
        caa = jacobian * (m11 * m11 + m12 * m12)
        cab = jacobian * (m11 * m21 + m12 * m22)
        cbb = jacobian * (m21 * m21 + m22 * m22)
        at = (2 * r + g) * 24
        coefs[at : at + 8, :] = caa
        coefs[at + 8 : at + 16, :] = cab
        coefs[at + 16 : at + 24, :] = cbb
        mass = jacobian * weight_ref[...]
        at = (2 * r + g) * TILE
        first = slice(g * 2 * LANES, (g * 2 + 1) * LANES)
        second = slice((g * 2 + 1) * LANES, (g * 2 + 2) * LANES)
        for f in range(FIELDS):
            one, two = fluxes(slopes[at + 8 * f : at + 8 * f + 8, :], (caa, cab, cbb))
            flux[r * 56 + 8 * f : r * 56 + 8 * f + 8, first] = one
            flux[r * 56 + 8 * f : r * 56 + 8 * f + 8, second] = two
        zonal, meridional = tile(r, g, 0, 8), tile(r, g, 8, 8)
        flow1 = jacobian * (m11 * zonal + m12 * meridional)
        flow2 = jacobian * (m21 * zonal + m22 * meridional)
        for k in range(2):
            carried = tile(r, g, 24 + 8 * k, 8)
            flux[r * 56 + 40 + 8 * k : r * 56 + 48 + 8 * k, first] = carried * flow1
            flux[r * 56 + 40 + 8 * k : r * 56 + 48 + 8 * k, second] = carried * flow2
        ea, eb = slopes[at + 40 : at + 48, :LANES], slopes[at + 40 : at + 48, LANES:]
        ta, tb = slopes[at + 16 : at + 24, :LANES], slopes[at + 16 : at + 24, LANES:]
        part = slice(g * LANES, (g + 1) * LANES)
        plain[r * 32 : r * 32 + 8, part] = mass * (
            coriolis * meridional - (m11 * ea + m21 * eb)
        )
        plain[r * 32 + 8 : r * 32 + 16, part] = -mass * (
            coriolis * zonal + (m12 * ea + m22 * eb)
        )
        plain[r * 32 + 16 : r * 32 + 24, part] = -mass * (
            zonal * (m11 * ta + m21 * tb) + meridional * (m12 * ta + m22 * tb)
        )
        plain[r * 32 + 24 : r * 32 + 32, part] = mass

    spread = divergence_joined(flux[...], div_hi_ref, div_lo_ref)
    upper, lower = halves(plain[...])
    direct = dot(upper, join_ref[...]) + dot(lower, join_ref[...])

    lane = lane_iota((1, LANES)) % 16
    low_mask = (lane < 4).astype(F32)
    high_mask = (lane >= 12).astype(F32)

    def joined(value, size, r, start, count):
        def rows(k):
            return value[k * size + start : k * size + start + count, :]

        return rows_joined(rows(r - 1), rows(r), rows(r + 1), low_mask, high_mask)

    inverse = {}
    smooth = []
    for r in range(1, 7):
        mass_sum = joined(direct, 32, r, 24, 8)
        smoothing = joined(spread, 56, r, 0, STATE)
        for g in range(2):
            inverse[r, g] = 1.0 / jnp.where(mass_sum[g] > 0.0, mass_sum[g], 1.0)
            smooth.append(smoothing[g] * jnp.concatenate([inverse[r, g]] * FIELDS, axis=0))
    again = gradient(jnp.concatenate(smooth, axis=0), grad2_ref, grad_lo_ref)
    flat = []
    for r in range(1, 7):
        parts = []
        for g in range(2):
            at = (2 * r + g) * 24
            triple = tuple(
                jnp.concatenate([coefs[at + 8 * k : at + 8 * k + 8, :]] * FIELDS, axis=0)
                for k in range(3)
            )
            start = (2 * (r - 1) + g) * STATE
            parts += list(fluxes(again[start : start + STATE, :], triple))
        flat.append(jnp.concatenate(parts, axis=1))
    damped = divergence_joined(jnp.concatenate(flat, axis=0), div_hi_ref, div_lo_ref)

    ordered = []
    for r in range(2, 6):
        straight = joined(direct, 32, r, 0, 24)
        carried = joined(spread, 56, r, STATE, 16)
        damping = rows_joined(
            damped[(r - 2) * STATE : (r - 1) * STATE, :],
            damped[(r - 1) * STATE : r * STATE, :],
            damped[r * STATE : (r + 1) * STATE, :],
            low_mask,
            high_mask,
        )
        for g in range(2):
            change = (
                TIME_STEP * jnp.concatenate([straight[g], -carried[g]], axis=0)
                - (TIME_STEP * HYPER_NU) * damping[g]
            )
            scale = jnp.concatenate([inverse[r, g]] * FIELDS, axis=0)
            ordered.append(tile(r, g, 0, STATE) + change * scale)
    whole = jnp.concatenate(ordered, axis=1)
    upper, lower = halves(whole)
    hits = (row_iota((1024, POINTS_DEV)) == place_ref[0:1, :]).astype(F32).astype(BF16)
    updated = dot(upper, hits) + dot(lower, hits)
    updated_ref[...] = updated

    columns = []
    picks = []
    for k in range(3):
        pieces = []
        if k > 0:
            pieces.append(jnp.zeros((STATE * k, POINTS_DEV), F32))
        pieces.append(updated)
        if k < 2:
            pieces.append(jnp.zeros((STATE * (2 - k), POINTS_DEV), F32))
        slot_row = jnp.where(
            row_iota((8, POINTS_DEV)) == k, jnp.broadcast_to(map_ref[3:4, :], (8, POINTS_DEV)), 0.0
        )
        columns.append(jnp.concatenate(pieces + [slot_row], axis=0))
        line = map_ref[k : k + 1, :].astype(jnp.int32)
        picks.append((row_iota((POINTS_DEV, POINTS_DEV)) == line).astype(F32).astype(BF16))
    upper, lower = halves(jnp.concatenate(columns, axis=1))
    sent = dot_last(jnp.concatenate(picks, axis=1), jnp.concatenate([upper, lower], axis=0))
    send_ref[...] = sent[:, :LANES] + sent[:, LANES:]


def receive_kernel(received_ref, physics_ref):
    turned_over = received_ref[...].T
    values = jnp.concatenate(
        [turned_over[STATE * k : STATE * (k + 1), :] for k in range(3)], axis=1
    )
    first = values.astype(BF16).astype(F32)
    both = jnp.concatenate([first, values - first], axis=0).astype(BF16)
    hits = []
    for k in range(3):
        slot = turned_over[3 * STATE + k : 3 * STATE + k + 1, :].astype(jnp.int32) - 1
        hits.append((row_iota((POINTS_DEV, POINTS_DEV)) == slot).astype(F32).astype(BF16))
    placed = dot_last(both, jnp.concatenate(hits, axis=1))
    physics_ref[...] = placed[:STATE] + placed[STATE:]


def call(kernel, shapes, scratch=(), flops=0, moved=0):
    single = not isinstance(shapes, list)
    outs = [jax.ShapeDtypeStruct(s, d) for s, d in ([shapes] if single else shapes)]
    return pl.pallas_call(
        kernel,
        out_shape=outs[0] if single else outs,
        scratch_shapes=list(scratch),
        compiler_params=pltpu.CompilerParams(vmem_limit_bytes=VMEM_LIMIT),
        cost_estimate=pl.CostEstimate(flops=flops, bytes_accessed=moved, transcendentals=0),
    )


def ring(axis, by):
    count = lax.axis_size(axis)
    return [(i, (i + by) % count) for i in range(count)]


def open_line(axis, by):
    count = lax.axis_size(axis)
    return [(i, i + by) for i in range(count) if 0 <= i + by < count]


def body(
    evolving_state_array, point_id, neighbours, jacobian, inverse_metric, coriolis, column_slot
):
    state = evolving_state_array.reshape(STATE, POINTS_DEV)
    geo = jnp.concatenate(
        [jacobian[None], coriolis[None], inverse_metric, jnp.zeros((2, POINTS_DEV), F32)], axis=0
    )
    half = ((4 * TILE, LANES), F32)
    strip = ((TILE, LANES), F32)
    low, high, to_right, to_left, place = call(
        arrange_kernel, [half, half, strip, strip, ((8, POINTS_DEV), jnp.int32)]
    )(state, geo, neighbours)
    from_left = lax.ppermute(to_right, "col", ring("col", 1))
    from_right = lax.ppermute(to_left, "col", ring("col", -1))
    sends = call(send_kernel, ((8, POINTS_DEV), F32))(column_slot[None])
    low, high = call(margin_kernel, [half, half])(low, high, from_left, from_right)
    below = lax.ppermute(high, "curve", open_line("curve", 1))
    above = lax.ppermute(low, "curve", open_line("curve", -1))
    updated, sent = call(
        section_kernel,
        [((STATE, POINTS_DEV), F32), ((POINTS_DEV, LANES), F32)],
        scratch=[
            pltpu.VMEM((16 * TILE, 2 * LANES), F32),
            pltpu.VMEM((8 * 56, 4 * LANES), F32),
            pltpu.VMEM((8 * 32, 2 * LANES), F32),
            pltpu.VMEM((16 * 24, LANES), F32),
        ],
    )(below, low, high, above, place, sends, *[jnp.asarray(m) for m in operators()])
    received = lax.all_to_all(sent, "col", split_axis=0, concat_axis=0, tiled=True)
    physics = call(receive_kernel, ((STATE, POINTS_DEV), F32))(received)
    shape = evolving_state_array.shape
    return updated.reshape(shape), physics.reshape(shape)


def solution(mesh):
    split = ("curve", "col")
    return jax.shard_map(
        body,
        mesh=mesh,
        in_specs=(
            P(None, None, split),
            P(split),
            P(None, split),
            P(split),
            P(None, split),
            P(split),
            P(split),
        ),
        out_specs=(P(None, None, split), P(None, None, split)),
        check_vma=False,
    )
```

```python
import functools
import math

import jax
import jax.numpy as jnp
import numpy as np
from jax import lax
from jax.experimental import pallas as pl
from jax.experimental.pallas import tpu as pltpu
from jax.sharding import PartitionSpec as P

FIELDS = 5
LEV = 8
STATE = FIELDS * LEV
TILE = 48
LANES = 128
ELEMS_DEV = 48
POINTS_DEV = 768
N_COL = 32
CAP = 72
CAP_ROWS = CAP // 3
TIME_STEP = 0.1
HYPER_NU = 0.002
F32 = jnp.float32
BF16 = jnp.bfloat16
VMEM_LIMIT = 32 * 1024 * 1024


def gll_tables():
    root_fifth = 1.0 / math.sqrt(5.0)
    nodes = np.array([-1.0, -root_fifth, root_fifth, 1.0])
    weights = np.array([1.0, 5.0, 5.0, 1.0]) / 6.0
    table = np.zeros((4, 4))
    for i in range(4):
        for m in range(4):
            if i == m:
                table[i, m] = sum(1.0 / (nodes[i] - nodes[o]) for o in range(4) if o != i)
            else:
                upper = np.prod([nodes[i] - nodes[o] for o in range(4) if o != i])
                lower = np.prod([nodes[m] - nodes[o] for o in range(4) if o != m])
                table[i, m] = upper / (lower * (nodes[i] - nodes[m]))
    return table, weights


def two_parts(matrix):
    upper = matrix.astype(np.float32).astype(jnp.bfloat16)
    lower = (matrix - upper.astype(np.float64)).astype(np.float32).astype(jnp.bfloat16)
    return upper, lower


@functools.lru_cache(maxsize=None)
def operators():
    table, weights = gll_tables()
    eye4, eye8 = np.eye(4), np.eye(8)
    along_cycle = np.kron(eye4, table.T)
    along_rows = np.kron(table.T, eye4)
    grad = np.concatenate([np.kron(eye8, along_cycle), np.kron(eye8, along_rows)], axis=1)
    weight = np.diag(np.outer(weights, weights).reshape(16))
    div = np.concatenate(
        [np.kron(eye8, along_cycle @ weight), np.kron(eye8, along_rows @ weight)], axis=0
    )
    join = np.eye(256)
    for place in range(15):
        for j in range(4):
            low, high = place * 16 + 4 * j + 3, place * 16 + 16 + 4 * j
            join[low, high] = 1.0
            join[high, low] = 1.0
    both = np.zeros((512, 256))
    both[:256, :128] = div
    both[256:, 128:] = div
    div_join = both @ join
    grad_hi, grad_lo = two_parts(grad)
    div_hi, div_lo = two_parts(div_join)
    mass_weight = np.tile(np.outer(weights, weights).reshape(16), 8).astype(np.float32)
    return (
        np.concatenate([grad_hi, grad_hi], axis=0),
        grad_lo,
        div_hi,
        div_lo,
        join.astype(jnp.bfloat16),
        np.broadcast_to(mass_weight, (8, 128)).copy(),
    )


def dot(left, right):
    return jnp.dot(left, right, preferred_element_type=F32)


def dot_last(left, right):
    return lax.dot_general(left, right, (((1,), (1,)), ((), ())), preferred_element_type=F32)


def halves(value):
    upper = value.astype(BF16)
    lower = (value - upper.astype(F32)).astype(BF16)
    return upper, lower


def lane_iota(shape):
    return lax.broadcasted_iota(jnp.int32, shape, 1)


def row_iota(shape):
    return lax.broadcasted_iota(jnp.int32, shape, 0)


def one_step(local, index):
    hit = (row_iota((ELEMS_DEV, ELEMS_DEV)) == index) & local
    return hit.astype(F32).astype(BF16)


def wide(local):
    return jnp.broadcast_to(local.astype(F32), (8, ELEMS_DEV))


def chain_length(local, index, doublings):
    length = wide(local)
    step = one_step(local, index)
    for k in range(doublings):
        length = length + dot(length.astype(BF16), step)
        if k + 1 < doublings:
            step = dot(step, step).astype(BF16)
    return length


def local_lists(near):
    base = (lax.axis_index("curve") * N_COL + lax.axis_index("col")) * ELEMS_DEV
    index = near - base
    return index, (index >= 0) & (index < ELEMS_DEV)


def over_points(element_values):
    shape = (ELEMS_DEV, POINTS_DEV)
    spread = (lane_iota(shape) // 16 == row_iota(shape)).astype(F32).astype(BF16)
    return dot(element_values.astype(BF16), spread)[0:1].astype(jnp.int32)


def three_parts(value):
    first = value.astype(BF16)
    rest = value - first.astype(F32)
    second = rest.astype(BF16)
    return first, second, (rest - second.astype(F32)).astype(BF16)


def strip_kernel(
    state_ref, jacobian_ref, coriolis_ref, metric_ref, near_ref, far_ref, close_ref, values_ref,
    near, jac, cor, metric, state, sems
):
    copies = [
        pltpu.make_async_copy(source, target, sems.at[i])
        for i, (source, target) in enumerate(
            [
                (near_ref, near),
                (state_ref, state),
                (jacobian_ref, jac),
                (coriolis_ref, cor),
                (metric_ref, metric),
            ]
        )
    ]
    for copy in copies:
        copy.start()
    copies[0].wait()
    index, local = local_lists(near[...])
    row = chain_length(local[2:3], index[2:3], 2)
    sides = []
    for side in range(2):
        here, there = local[side : side + 1], index[side : side + 1]
        second = dot(wide(here).astype(BF16), one_step(here, there))
        edge = wide(~here)
        sides.append((edge, wide(here) * (1.0 - second)))
    (first, second), (last, second_last) = sides
    unit = (first + second) * (2.0 * row + 1.0 + second)
    unit = unit + (last + second_last) * (2.0 * row + 9.0 + last)
    lane = (over_points(unit) - 1) * 16 + lane_iota((1, POINTS_DEV)) % 16
    hits = (row_iota((2 * LANES, POINTS_DEV)) == lane).astype(F32).astype(BF16)
    for copy in copies[1:]:
        copy.wait()
    values = jnp.concatenate(
        [
            state[...].reshape(STATE, POINTS_DEV),
            jac[...].reshape(1, POINTS_DEV),
            cor[...].reshape(1, POINTS_DEV),
            metric[...],
            jnp.zeros((2, POINTS_DEV), F32),
        ],
        axis=0,
    )
    values_ref[...] = values
    parts = dot_last(jnp.concatenate(three_parts(values), axis=0), hits)
    strips = parts[0:TILE] + parts[TILE : 2 * TILE] + parts[2 * TILE :]
    even = lax.rem(lax.axis_index("col"), 2) == 0
    to_left, to_right = strips[:, :LANES], strips[:, LANES:]
    far_ref[...] = jnp.where(even, to_left, to_right)
    close_ref[...] = jnp.where(even, to_right, to_left)


def arrange_kernel(values_ref, near_ref, slot_ref, low_ref, high_ref, place_ref, lists_ref):
    index, local = local_lists(near_ref[...])
    place = chain_length(local[0:1], index[0:1], 4)
    row = chain_length(local[2:3], index[2:3], 2)
    target = over_points(row * 16.0 + place + 2.0) * 16 + lane_iota((1, POINTS_DEV)) % 16
    place_ref[...] = jnp.broadcast_to(target, (8, POINTS_DEV))
    hits = (row_iota((1024, POINTS_DEV)) == target).astype(F32).astype(BF16)
    columns = send_lists(slot_ref[...])
    left = jnp.concatenate(three_parts(values_ref[...]), axis=0)
    upper, rest = halves(columns)
    left = jnp.concatenate([left, jnp.concatenate([columns, columns - upper.astype(F32)], axis=0).astype(BF16)], axis=0)
    parts = dot_last(left, hits)
    ordered = parts[0:TILE] + parts[TILE : 2 * TILE] + parts[2 * TILE : 3 * TILE]
    for r in range(4):
        for g in range(2):
            block = ordered[:, (2 * r + g) * LANES : (2 * r + g + 1) * LANES]
            ref = low_ref if r < 2 else high_ref
            start = ((r % 2) * 2 + g) * TILE
            ref[start : start + TILE, :] = block
    lists_ref[...] = parts[3 * TILE : 3 * TILE + 8] + parts[3 * TILE + 8 :]


def turned(block, by):
    by = by % LANES
    return block if by == 0 else pltpu.roll(block, by, 1)


def margin_kernel(low_in, high_in, from_far, from_close, first_ref, second_ref):
    lane = lane_iota((TILE, LANES))
    even = lax.rem(lax.axis_index("col"), 2) == 0
    from_left = jnp.where(even, from_far[...], from_close[...])
    from_right = jnp.where(even, from_close[...], from_far[...])
    halves_of_rows = []
    for source, start_row in ((low_in, 0), (high_in, 2)):
        blocks = []
        for r in range(2):
            turn = start_row + r
            start = r * 2 * TILE
            blocks.append(
                jnp.where(lane < 32, turned(from_left, -32 * turn), source[start : start + TILE, :])
            )
            start += TILE
            blocks.append(
                jnp.where(
                    lane >= 96, turned(from_right, 96 - 32 * turn), source[start : start + TILE, :]
                )
            )
        halves_of_rows.append(jnp.concatenate(blocks, axis=0))
    low, high = halves_of_rows
    even = lax.rem(lax.axis_index("curve"), 2) == 0
    first_ref[...] = jnp.where(even, high, low)
    second_ref[...] = jnp.where(even, low, high)


def send_lists(slot):
    slot_value = slot.astype(F32)
    device = jnp.floor((slot_value + 0.5) * (1.0 / POINTS_DEV))
    within = slot_value - device * POINTS_DEV
    wanted = jnp.broadcast_to(device.astype(jnp.int32), (N_COL, POINTS_DEV))
    chosen = (wanted == row_iota((N_COL, POINTS_DEV))).astype(F32)
    square = (LANES, LANES)
    upto = (row_iota(square) <= lane_iota(square)).astype(F32)
    count = jnp.concatenate([upto, jnp.ones(square, F32)], axis=1).astype(BF16)
    groups = POINTS_DEV // LANES
    stacked = jnp.concatenate(
        [chosen[:, i * LANES : (i + 1) * LANES] for i in range(groups)], axis=0
    )
    counted = dot(stacked.astype(BF16), count)
    before = jnp.zeros((N_COL, LANES), F32)
    ranks = []
    for i in range(groups):
        rows = counted[i * N_COL : (i + 1) * N_COL]
        here = (rows[:, :LANES] + before) * stacked[i * N_COL : (i + 1) * N_COL]
        ranks.append(jnp.sum(here, axis=0, keepdims=True))
        before = before + rows[:, LANES:]
    rank = jnp.concatenate(ranks, axis=1) - 1.0
    third = (rank >= CAP_ROWS).astype(F32) + (rank >= 2 * CAP_ROWS).astype(F32)
    line = device * CAP_ROWS + rank - third * CAP_ROWS
    lists = [jnp.where(third == float(k), line + 1.0, 0.0) for k in range(3)]
    filler = jnp.zeros((4, POINTS_DEV), F32)
    return jnp.concatenate(lists + [within + 1.0, filler], axis=0)


def pick_kernel(lists_ref, *refs):
    count = len(refs) // 2
    sources, (picks_ref, *targets), sems = refs[: count - 1], refs[count - 1 : -1], refs[-1]
    copies = [
        pltpu.make_async_copy(source, target, sems.at[i])
        for i, (source, target) in enumerate(zip(sources, targets))
    ]
    for copy in copies:
        copy.start()
    shape = (POINTS_DEV, 1024)
    for k in range(3):
        line = lists_ref[k : k + 1, :].astype(jnp.int32) - 1
        picks_ref[:, k * 1024 : (k + 1) * 1024] = (row_iota(shape) == line).astype(F32).astype(BF16)
    for copy in copies:
        copy.wait()


def fluxes(slope, coefficients):
    along_cycle, along_rows = slope[:, :LANES], slope[:, LANES:]
    caa, cab, cbb = coefficients
    return caa * along_cycle + cab * along_rows, cab * along_cycle + cbb * along_rows


def gradient(values, grad2_ref, grad_lo_ref):
    upper, lower = halves(values)
    return dot(jnp.concatenate([upper, lower], axis=1), grad2_ref[...]) + dot(
        upper, grad_lo_ref[...]
    )


def divergence_joined(values, div_hi_ref, div_lo_ref):
    upper, lower = halves(values)
    return dot(upper, div_hi_ref[...]) + dot(lower, div_hi_ref[...]) + dot(upper, div_lo_ref[...])


def rows_joined(below, here, above, low_mask, high_mask):
    parts = []
    for g in range(2):
        part = slice(g * LANES, (g + 1) * LANES)
        parts.append(
            here[:, part]
            + low_mask * turned(below[:, part], -12)
            + high_mask * turned(above[:, part], 12)
        )
    return parts


def section_kernel(
    first_far_ref,
    first_ref,
    second_ref,
    second_far_ref,
    lists_ref,
    picks_ref,
    grad2_ref,
    grad_lo_ref,
    div_hi_ref,
    div_lo_ref,
    join_ref,
    weight_ref,
    whole_ref,
    send_ref,
    quarters,
    slopes,
    flux,
    plain,
    coefs,
):
    even = lax.rem(lax.axis_index("curve"), 2) == 0
    quarters[0] = jnp.where(even, second_far_ref[...], first_far_ref[...])
    quarters[1] = jnp.where(even, second_ref[...], first_ref[...])
    quarters[2] = jnp.where(even, first_ref[...], second_ref[...])
    quarters[3] = jnp.where(even, first_far_ref[...], second_far_ref[...])

    def tile(r, g, start=0, size=TILE):
        offset = ((r % 2) * 2 + g) * TILE + start
        return quarters[r // 2, offset : offset + size, :]

    cells = [(r, g) for r in range(8) for g in range(2)]
    stacked = []
    for r, g in cells:
        zonal, meridional = tile(r, g, 0, 8), tile(r, g, 8, 8)
        energy = 0.5 * (zonal * zonal + meridional * meridional) + tile(r, g, 16, 8)
        stacked += [tile(r, g, 0, STATE), energy]
    slopes[...] = gradient(jnp.concatenate(stacked, axis=0), grad2_ref, grad_lo_ref)

    for r, g in cells:
        def line(k):
            return jnp.broadcast_to(tile(r, g, STATE + k, 1), (8, LANES))

        jacobian, coriolis = line(0), line(1)
        m11, m12, m21, m22 = 1.0 + line(2), line(3), line(4), 1.0 + line(5)
        caa = jacobian * (m11 * m11 + m12 * m12)
        cab = jacobian * (m11 * m21 + m12 * m22)
        cbb = jacobian * (m21 * m21 + m22 * m22)
        at = (2 * r + g) * 24
        coefs[at : at + 8, :] = caa
        coefs[at + 8 : at + 16, :] = cab
        coefs[at + 16 : at + 24, :] = cbb
        mass = jacobian * weight_ref[...]
        at = (2 * r + g) * TILE
        first = slice(g * 2 * LANES, (g * 2 + 1) * LANES)
        second = slice((g * 2 + 1) * LANES, (g * 2 + 2) * LANES)
        for f in range(FIELDS):
            one, two = fluxes(slopes[at + 8 * f : at + 8 * f + 8, :], (caa, cab, cbb))
            flux[r * 56 + 8 * f : r * 56 + 8 * f + 8, first] = one
            flux[r * 56 + 8 * f : r * 56 + 8 * f + 8, second] = two
        zonal, meridional = tile(r, g, 0, 8), tile(r, g, 8, 8)
        flow1 = jacobian * (m11 * zonal + m12 * meridional)
        flow2 = jacobian * (m21 * zonal + m22 * meridional)
        for k in range(2):
            carried = tile(r, g, 24 + 8 * k, 8)
            flux[r * 56 + 40 + 8 * k : r * 56 + 48 + 8 * k, first] = carried * flow1
            flux[r * 56 + 40 + 8 * k : r * 56 + 48 + 8 * k, second] = carried * flow2
        ea, eb = slopes[at + 40 : at + 48, :LANES], slopes[at + 40 : at + 48, LANES:]
        ta, tb = slopes[at + 16 : at + 24, :LANES], slopes[at + 16 : at + 24, LANES:]
        part = slice(g * LANES, (g + 1) * LANES)
        plain[r * 32 : r * 32 + 8, part] = mass * (
            coriolis * meridional - (m11 * ea + m21 * eb)
        )
        plain[r * 32 + 8 : r * 32 + 16, part] = -mass * (
            coriolis * zonal + (m12 * ea + m22 * eb)
        )
        plain[r * 32 + 16 : r * 32 + 24, part] = -mass * (
            zonal * (m11 * ta + m21 * tb) + meridional * (m12 * ta + m22 * tb)
        )
        plain[r * 32 + 24 : r * 32 + 32, part] = mass

    spread = divergence_joined(flux[...], div_hi_ref, div_lo_ref)
    upper, lower = halves(plain[...])
    direct = dot(upper, join_ref[...]) + dot(lower, join_ref[...])

    lane = lane_iota((1, LANES)) % 16
    low_mask = (lane < 4).astype(F32)
    high_mask = (lane >= 12).astype(F32)

    def joined(value, size, r, start, count):
        def rows(k):
            return value[k * size + start : k * size + start + count, :]

        return rows_joined(rows(r - 1), rows(r), rows(r + 1), low_mask, high_mask)

    inverse = {}
    smooth = []
    for r in range(1, 7):
        mass_sum = joined(direct, 32, r, 24, 8)
        smoothing = joined(spread, 56, r, 0, STATE)
        for g in range(2):
            inverse[r, g] = 1.0 / jnp.where(mass_sum[g] > 0.0, mass_sum[g], 1.0)
            smooth.append(smoothing[g] * jnp.concatenate([inverse[r, g]] * FIELDS, axis=0))
    again = gradient(jnp.concatenate(smooth, axis=0), grad2_ref, grad_lo_ref)
    flat = []
    for r in range(1, 7):
        parts = []
        for g in range(2):
            at = (2 * r + g) * 24
            triple = tuple(
                jnp.concatenate([coefs[at + 8 * k : at + 8 * k + 8, :]] * FIELDS, axis=0)
                for k in range(3)
            )
            start = (2 * (r - 1) + g) * STATE
            parts += list(fluxes(again[start : start + STATE, :], triple))
        flat.append(jnp.concatenate(parts, axis=1))
    damped = divergence_joined(jnp.concatenate(flat, axis=0), div_hi_ref, div_lo_ref)

    ordered = []
    for r in range(2, 6):
        straight = joined(direct, 32, r, 0, 24)
        carried = joined(spread, 56, r, STATE, 16)
        damping = rows_joined(
            damped[(r - 2) * STATE : (r - 1) * STATE, :],
            damped[(r - 1) * STATE : r * STATE, :],
            damped[r * STATE : (r + 1) * STATE, :],
            low_mask,
            high_mask,
        )
        for g in range(2):
            change = (
                TIME_STEP * jnp.concatenate([straight[g], -carried[g]], axis=0)
                - (TIME_STEP * HYPER_NU) * damping[g]
            )
            scale = jnp.concatenate([inverse[r, g]] * FIELDS, axis=0)
            ordered.append(tile(r, g, 0, STATE) + change * scale)
    whole = jnp.concatenate(ordered, axis=1)
    whole_ref[...] = whole
    columns = []
    for k in range(3):
        pieces = []
        if k > 0:
            pieces.append(jnp.zeros((STATE * k, 1024), F32))
        pieces.append(whole)
        if k < 2:
            pieces.append(jnp.zeros((STATE * (2 - k), 1024), F32))
        slot_row = jnp.where(
            row_iota((8, 1024)) == k, jnp.broadcast_to(lists_ref[3:4, :], (8, 1024)), 0.0
        )
        columns.append(jnp.concatenate(pieces + [slot_row], axis=0))
    upper, lower = halves(jnp.concatenate(columns, axis=1))
    sent = dot_last(picks_ref[...], jnp.concatenate([upper, lower], axis=0))
    send_ref[...] = sent[:, :LANES] + sent[:, LANES:]


def restore_kernel(whole_ref, place_ref, updated_ref):
    first, second, third = three_parts(whole_ref[...])
    hits = (row_iota((1024, POINTS_DEV)) == place_ref[0:1, :]).astype(F32).astype(BF16)
    updated_ref[...] = dot(first, hits) + dot(second, hits) + dot(third, hits)


def receive_kernel(received_ref, physics_ref):
    turned_over = received_ref[...].T
    values = jnp.concatenate(
        [turned_over[STATE * k : STATE * (k + 1), :] for k in range(3)], axis=1
    )
    first = values.astype(BF16).astype(F32)
    both = jnp.concatenate([first, values - first], axis=0).astype(BF16)
    hits = []
    for k in range(3):
        slot = turned_over[3 * STATE + k : 3 * STATE + k + 1, :].astype(jnp.int32) - 1
        hits.append((row_iota((POINTS_DEV, POINTS_DEV)) == slot).astype(F32).astype(BF16))
    placed = dot_last(both, jnp.concatenate(hits, axis=1))
    physics_ref[...] = placed[:STATE] + placed[STATE:]


def call(kernel, shapes, scratch=(), flops=0, moved=0, vmem=VMEM_LIMIT, **specs):
    return pl.pallas_call(
        kernel,
        out_shape=[jax.ShapeDtypeStruct(s, d) for s, d in shapes],
        scratch_shapes=list(scratch),
        **specs,
        compiler_params=pltpu.CompilerParams(vmem_limit_bytes=vmem),
        cost_estimate=pl.CostEstimate(flops=flops, bytes_accessed=moved, transcendentals=0),
    )


def swaps(count, pairs_from):
    route = []
    for i in range(pairs_from, count - 1, 2):
        route += [(i, i + 1), (i + 1, i)]
    return route


def body(
    evolving_state_array, point_id, neighbours, jacobian, inverse_metric, coriolis, column_slot
):
    anywhere = pl.BlockSpec(memory_space=pltpu.HBM)
    vmem = pl.BlockSpec(memory_space=pltpu.VMEM)
    half = ((4 * TILE, LANES), F32)
    strip = ((TILE, LANES), F32)
    values_shape = ((TILE, POINTS_DEV), F32)
    far, close, values = call(
        strip_kernel,
        [strip, strip, values_shape],
        scratch=[
            pltpu.VMEM((8, ELEMS_DEV), jnp.int32),
            pltpu.VMEM((POINTS_DEV,), F32),
            pltpu.VMEM((POINTS_DEV,), F32),
            pltpu.VMEM((4, POINTS_DEV), F32),
            pltpu.VMEM((FIELDS, LEV, POINTS_DEV), F32),
            pltpu.SemaphoreType.DMA((5,)),
        ],
        in_specs=[anywhere] * 5,
        vmem=64 * 1024 * 1024 - 524288,
    )(evolving_state_array, jacobian, coriolis, inverse_metric, neighbours)
    cols, rows = lax.axis_size("col"), lax.axis_size("curve")
    from_far = lax.ppermute(far, "col", swaps(cols, 1) + [(cols - 1, 0), (0, cols - 1)])
    from_close = lax.ppermute(close, "col", swaps(cols, 0))
    low, high, place, lists = call(
        arrange_kernel,
        [half, half, ((8, POINTS_DEV), jnp.int32), ((8, 1024), F32)],
        flops=400_000_000,
        moved=1_000_000,
    )(values, neighbours, column_slot[None])
    first, second = call(margin_kernel, [half, half])(low, high, from_far, from_close)
    second_far = lax.ppermute(second, "curve", swaps(rows, 1))
    first_far = lax.ppermute(first, "curve", swaps(rows, 0))
    matrices = [jnp.asarray(m) for m in operators()]
    picks, *matrices = call(
        pick_kernel,
        [((POINTS_DEV, 3 * 1024), BF16)] + [(m.shape, m.dtype) for m in matrices],
        scratch=[pltpu.SemaphoreType.DMA((len(matrices),))],
        in_specs=[vmem] + [anywhere] * len(matrices),
        flops=400_000_000,
        moved=1_000_000,
    )(lists, *matrices)
    whole, sent = call(
        section_kernel,
        [((STATE, 1024), F32), ((POINTS_DEV, LANES), F32)],
        scratch=[
            pltpu.VMEM((4, 4 * TILE, LANES), F32),
            pltpu.VMEM((16 * TILE, 2 * LANES), F32),
            pltpu.VMEM((8 * 56, 4 * LANES), F32),
            pltpu.VMEM((8 * 32, 2 * LANES), F32),
            pltpu.VMEM((16 * 24, LANES), F32),
        ],
    )(first_far, first, second, second_far, lists, picks, *matrices)
    received = lax.all_to_all(sent, "col", split_axis=0, concat_axis=0, tiled=True)
    (updated,) = call(
        restore_kernel, [((STATE, POINTS_DEV), F32)], flops=400_000_000, moved=1_000_000
    )(whole, place)
    (physics,) = call(receive_kernel, [((STATE, POINTS_DEV), F32)])(received)
    shape = evolving_state_array.shape
    return updated.reshape(shape), physics.reshape(shape)


def solution(mesh):
    split = ("curve", "col")
    return jax.shard_map(
        body,
        mesh=mesh,
        in_specs=(
            P(None, None, split),
            P(split),
            P(None, split),
            P(split),
            P(None, split),
            P(split),
            P(split),
        ),
        out_specs=(P(None, None, split), P(None, None, split)),
        check_vma=False,
    )
```

```python
import functools
import math

import jax
import jax.numpy as jnp
import numpy as np
from jax import lax
from jax.experimental import pallas as pl
from jax.experimental.pallas import tpu as pltpu
from jax.sharding import PartitionSpec as P

FIELDS = 5
LEV = 8
STATE = FIELDS * LEV
TILE = 48
LANES = 128
ELEMS_DEV = 48
POINTS_DEV = 768
N_COL = 32
CAP = 72
CAP_ROWS = CAP // 3
TIME_STEP = 0.1
HYPER_NU = 0.002
F32 = jnp.float32
BF16 = jnp.bfloat16
VMEM_LIMIT = 32 * 1024 * 1024


def gll_tables():
    root_fifth = 1.0 / math.sqrt(5.0)
    nodes = np.array([-1.0, -root_fifth, root_fifth, 1.0])
    weights = np.array([1.0, 5.0, 5.0, 1.0]) / 6.0
    table = np.zeros((4, 4))
    for i in range(4):
        for m in range(4):
            if i == m:
                table[i, m] = sum(1.0 / (nodes[i] - nodes[o]) for o in range(4) if o != i)
            else:
                upper = np.prod([nodes[i] - nodes[o] for o in range(4) if o != i])
                lower = np.prod([nodes[m] - nodes[o] for o in range(4) if o != m])
                table[i, m] = upper / (lower * (nodes[i] - nodes[m]))
    return table, weights


def two_parts(matrix):
    upper = matrix.astype(np.float32).astype(jnp.bfloat16)
    lower = (matrix - upper.astype(np.float64)).astype(np.float32).astype(jnp.bfloat16)
    return upper, lower


@functools.lru_cache(maxsize=None)
def operators():
    table, weights = gll_tables()
    eye4, eye8 = np.eye(4), np.eye(8)
    along_cycle = np.kron(eye4, table.T)
    along_rows = np.kron(table.T, eye4)
    grad = np.concatenate([np.kron(eye8, along_cycle), np.kron(eye8, along_rows)], axis=1)
    weight = np.diag(np.outer(weights, weights).reshape(16))
    div = np.concatenate(
        [np.kron(eye8, along_cycle @ weight), np.kron(eye8, along_rows @ weight)], axis=0
    )
    join = np.eye(256)
    for place in range(15):
        for j in range(4):
            low, high = place * 16 + 4 * j + 3, place * 16 + 16 + 4 * j
            join[low, high] = 1.0
            join[high, low] = 1.0
    both = np.zeros((512, 256))
    both[:256, :128] = div
    both[256:, 128:] = div
    div_join = both @ join
    grad_hi, grad_lo = two_parts(grad)
    div_hi, div_lo = two_parts(div_join)
    return np.concatenate(
        [grad_hi, grad_hi, grad_lo, div_hi, div_lo, join.astype(jnp.bfloat16)], axis=0
    )


def dot(left, right):
    return jnp.dot(left, right, preferred_element_type=F32)


def dot_last(left, right):
    return lax.dot_general(left, right, (((1,), (1,)), ((), ())), preferred_element_type=F32)


def halves(value):
    upper = value.astype(BF16)
    lower = (value - upper.astype(F32)).astype(BF16)
    return upper, lower


def lane_iota(shape):
    return lax.broadcasted_iota(jnp.int32, shape, 1)


def row_iota(shape):
    return lax.broadcasted_iota(jnp.int32, shape, 0)


def one_step(local, index):
    hit = (row_iota((ELEMS_DEV, ELEMS_DEV)) == index) & local
    return hit.astype(F32).astype(BF16)


def wide(local):
    return jnp.broadcast_to(local.astype(F32), (8, ELEMS_DEV))


def chain_length(local, index, doublings):
    length = wide(local)
    step = one_step(local, index)
    for k in range(doublings):
        length = length + dot(length.astype(BF16), step)
        if k + 1 < doublings:
            step = dot(step, step).astype(BF16)
    return length


def local_lists(near):
    base = (lax.axis_index("curve") * N_COL + lax.axis_index("col")) * ELEMS_DEV
    index = near - base
    return index, (index >= 0) & (index < ELEMS_DEV)


def over_points(element_values):
    shape = (ELEMS_DEV, POINTS_DEV)
    spread = (lane_iota(shape) // 16 == row_iota(shape)).astype(F32).astype(BF16)
    return dot(element_values.astype(BF16), spread)[0:1].astype(jnp.int32)


def three_parts(value):
    first = value.astype(BF16)
    rest = value - first.astype(F32)
    second = rest.astype(BF16)
    return first, second, (rest - second.astype(F32)).astype(BF16)


def strip_kernel(
    state_ref, jacobian_ref, coriolis_ref, metric_ref, near_ref, far_ref, close_ref, values_ref,
    near, jac, cor, metric, state, sems
):
    copies = [
        pltpu.make_async_copy(source, target, sems.at[i])
        for i, (source, target) in enumerate(
            [
                (near_ref, near),
                (state_ref, state),
                (jacobian_ref, jac),
                (coriolis_ref, cor),
                (metric_ref, metric),
            ]
        )
    ]
    for copy in copies:
        copy.start()
    copies[0].wait()
    index, local = local_lists(near[...])
    row = chain_length(local[2:3], index[2:3], 2)
    sides = []
    for side in range(2):
        here, there = local[side : side + 1], index[side : side + 1]
        second = dot(wide(here).astype(BF16), one_step(here, there))
        edge = wide(~here)
        sides.append((edge, wide(here) * (1.0 - second)))
    (first, second), (last, second_last) = sides
    unit = (first + second) * (2.0 * row + 1.0 + second)
    unit = unit + (last + second_last) * (2.0 * row + 9.0 + last)
    lane = (over_points(unit) - 1) * 16 + lane_iota((1, POINTS_DEV)) % 16
    hits = (row_iota((2 * LANES, POINTS_DEV)) == lane).astype(F32).astype(BF16)
    for copy in copies[1:]:
        copy.wait()
    values = jnp.concatenate(
        [
            state[...].reshape(STATE, POINTS_DEV),
            jac[...].reshape(1, POINTS_DEV),
            cor[...].reshape(1, POINTS_DEV),
            metric[...],
            jnp.zeros((2, POINTS_DEV), F32),
        ],
        axis=0,
    )
    values_ref[...] = values
    parts = dot_last(jnp.concatenate(three_parts(values), axis=0), hits)
    strips = parts[0:TILE] + parts[TILE : 2 * TILE] + parts[2 * TILE :]
    even = lax.rem(lax.axis_index("col"), 2) == 0
    to_left, to_right = strips[:, :LANES], strips[:, LANES:]
    far_ref[...] = jnp.where(even, to_left, to_right)
    close_ref[...] = jnp.where(even, to_right, to_left)


def arrange_kernel(values_ref, near_ref, slot_ref, low_ref, high_ref, place_ref, lists_ref):
    index, local = local_lists(near_ref[...])
    place = chain_length(local[0:1], index[0:1], 4)
    row = chain_length(local[2:3], index[2:3], 2)
    target = over_points(row * 16.0 + place + 2.0) * 16 + lane_iota((1, POINTS_DEV)) % 16
    place_ref[...] = jnp.broadcast_to(target, (8, POINTS_DEV))
    hits = (row_iota((1024, POINTS_DEV)) == target).astype(F32).astype(BF16)
    columns = send_lists(slot_ref[...])
    left = jnp.concatenate(three_parts(values_ref[...]), axis=0)
    upper, rest = halves(columns)
    left = jnp.concatenate([left, jnp.concatenate([columns, columns - upper.astype(F32)], axis=0).astype(BF16)], axis=0)
    parts = dot_last(left, hits)
    ordered = parts[0:TILE] + parts[TILE : 2 * TILE] + parts[2 * TILE : 3 * TILE]
    for r in range(4):
        for g in range(2):
            block = ordered[:, (2 * r + g) * LANES : (2 * r + g + 1) * LANES]
            ref = low_ref if r < 2 else high_ref
            start = ((r % 2) * 2 + g) * TILE
            ref[start : start + TILE, :] = block
    lists_ref[...] = parts[3 * TILE : 3 * TILE + 8] + parts[3 * TILE + 8 :]


def turned(block, by):
    by = by % LANES
    return block if by == 0 else pltpu.roll(block, by, 1)


def margin_kernel(
    low_in, high_in, from_far, from_close, first_ref, second_ref, low_ref, high_ref
):
    lane = lane_iota((TILE, LANES))
    even = lax.rem(lax.axis_index("col"), 2) == 0
    from_left = jnp.where(even, from_far[...], from_close[...])
    from_right = jnp.where(even, from_close[...], from_far[...])
    halves_of_rows = []
    for source, start_row in ((low_in, 0), (high_in, 2)):
        blocks = []
        for r in range(2):
            turn = start_row + r
            start = r * 2 * TILE
            blocks.append(
                jnp.where(lane < 32, turned(from_left, -32 * turn), source[start : start + TILE, :])
            )
            start += TILE
            blocks.append(
                jnp.where(
                    lane >= 96, turned(from_right, 96 - 32 * turn), source[start : start + TILE, :]
                )
            )
        halves_of_rows.append(jnp.concatenate(blocks, axis=0))
    low, high = halves_of_rows
    low_ref[...] = low
    high_ref[...] = high
    even = lax.rem(lax.axis_index("curve"), 2) == 0
    first_ref[...] = jnp.where(even, high, low)
    second_ref[...] = jnp.where(even, low, high)


def send_lists(slot):
    slot_value = slot.astype(F32)
    device = jnp.floor((slot_value + 0.5) * (1.0 / POINTS_DEV))
    within = slot_value - device * POINTS_DEV
    wanted = jnp.broadcast_to(device.astype(jnp.int32), (N_COL, POINTS_DEV))
    chosen = (wanted == row_iota((N_COL, POINTS_DEV))).astype(F32)
    square = (LANES, LANES)
    upto = (row_iota(square) <= lane_iota(square)).astype(F32)
    count = jnp.concatenate([upto, jnp.ones(square, F32)], axis=1).astype(BF16)
    groups = POINTS_DEV // LANES
    stacked = jnp.concatenate(
        [chosen[:, i * LANES : (i + 1) * LANES] for i in range(groups)], axis=0
    )
    counted = dot(stacked.astype(BF16), count)
    before = jnp.zeros((N_COL, LANES), F32)
    ranks = []
    for i in range(groups):
        rows = counted[i * N_COL : (i + 1) * N_COL]
        here = (rows[:, :LANES] + before) * stacked[i * N_COL : (i + 1) * N_COL]
        ranks.append(jnp.sum(here, axis=0, keepdims=True))
        before = before + rows[:, LANES:]
    rank = jnp.concatenate(ranks, axis=1) - 1.0
    third = (rank >= CAP_ROWS).astype(F32) + (rank >= 2 * CAP_ROWS).astype(F32)
    line = device * CAP_ROWS + rank - third * CAP_ROWS
    lists = [jnp.where(third == float(k), line + 1.0, 0.0) for k in range(3)]
    filler = jnp.zeros((4, POINTS_DEV), F32)
    return jnp.concatenate(lists + [within + 1.0, filler], axis=0)


def fluxes(slope, coefficients):
    along_cycle, along_rows = slope[:, :LANES], slope[:, LANES:]
    caa, cab, cbb = coefficients
    return caa * along_cycle + cab * along_rows, cab * along_cycle + cbb * along_rows


def gradient(values, matrices):
    upper, lower = halves(values)
    return dot(jnp.concatenate([upper, lower], axis=1), matrices[0:256, :]) + dot(
        upper, matrices[256:384, :]
    )


def divergence_joined(values, matrices):
    upper, lower = halves(values)
    first = matrices[384:896, :]
    return dot(upper, first) + dot(lower, first) + dot(upper, matrices[896:1408, :])


def local_terms(rows, tile, matrices, slopes, flux, plain, coefs, coefs_at):
    cells = [(n, r, g) for n, r in enumerate(rows) for g in range(2)]
    stacked = []
    for _, r, g in cells:
        zonal, meridional = tile(r, g, 0, 8), tile(r, g, 8, 8)
        energy = 0.5 * (zonal * zonal + meridional * meridional) + tile(r, g, 16, 8)
        stacked += [tile(r, g, 0, STATE), energy]
    slopes[...] = gradient(jnp.concatenate(stacked, axis=0), matrices)
    lane = lane_iota((8, LANES))
    inner_i = (lane % 4 == 1) | (lane % 4 == 2)
    inner_j = (lane // 4 % 4 == 1) | (lane // 4 % 4 == 2)
    weight = jnp.where(inner_i, 5.0 / 6.0, 1.0 / 6.0) * jnp.where(inner_j, 5.0 / 6.0, 1.0 / 6.0)
    for n, r, g in cells:

        def line(k):
            return jnp.broadcast_to(tile(r, g, STATE + k, 1), (8, LANES))

        jacobian, coriolis = line(0), line(1)
        m11, m12, m21, m22 = 1.0 + line(2), line(3), line(4), 1.0 + line(5)
        caa = jacobian * (m11 * m11 + m12 * m12)
        cab = jacobian * (m11 * m21 + m12 * m22)
        cbb = jacobian * (m21 * m21 + m22 * m22)
        at = coefs_at(r, g)
        if at is not None:
            coefs[at : at + 8, :] = caa
            coefs[at + 8 : at + 16, :] = cab
            coefs[at + 16 : at + 24, :] = cbb
        mass = jacobian * weight
        at = (2 * n + g) * TILE
        first = slice(g * 2 * LANES, (g * 2 + 1) * LANES)
        second = slice((g * 2 + 1) * LANES, (g * 2 + 2) * LANES)
        for f in range(FIELDS):
            one, two = fluxes(slopes[at + 8 * f : at + 8 * f + 8, :], (caa, cab, cbb))
            flux[n * 56 + 8 * f : n * 56 + 8 * f + 8, first] = one
            flux[n * 56 + 8 * f : n * 56 + 8 * f + 8, second] = two
        zonal, meridional = tile(r, g, 0, 8), tile(r, g, 8, 8)
        flow1 = jacobian * (m11 * zonal + m12 * meridional)
        flow2 = jacobian * (m21 * zonal + m22 * meridional)
        for k in range(2):
            carried = tile(r, g, 24 + 8 * k, 8)
            flux[n * 56 + 40 + 8 * k : n * 56 + 48 + 8 * k, first] = carried * flow1
            flux[n * 56 + 40 + 8 * k : n * 56 + 48 + 8 * k, second] = carried * flow2
        ea, eb = slopes[at + 40 : at + 48, :LANES], slopes[at + 40 : at + 48, LANES:]
        ta, tb = slopes[at + 16 : at + 24, :LANES], slopes[at + 16 : at + 24, LANES:]
        part = slice(g * LANES, (g + 1) * LANES)
        plain[n * 32 : n * 32 + 8, part] = mass * (coriolis * meridional - (m11 * ea + m21 * eb))
        plain[n * 32 + 8 : n * 32 + 16, part] = -mass * (coriolis * zonal + (m12 * ea + m22 * eb))
        plain[n * 32 + 16 : n * 32 + 24, part] = -mass * (
            zonal * (m11 * ta + m21 * tb) + meridional * (m12 * ta + m22 * tb)
        )
        plain[n * 32 + 24 : n * 32 + 32, part] = mass
    spread = divergence_joined(flux[...], matrices)
    upper, lower = halves(plain[...])
    join = matrices[1408:1664, :]
    return spread, dot(upper, join) + dot(lower, join)


def inner_kernel(
    low_ref, high_ref, lists_ref, matrices, spread_ref, direct_ref, coefs, picks_ref, slopes, flux, plain
):
    def tile(r, g, start=0, size=TILE):
        offset = ((r % 2) * 2 + g) * TILE + start
        return (low_ref if r < 2 else high_ref)[offset : offset + size, :]

    spread, direct = local_terms(
        range(4), tile, matrices, slopes, flux, plain, coefs, lambda r, g: (2 * r + g) * 24
    )
    spread_ref[...] = spread
    direct_ref[...] = direct
    line = (lists_ref[0:1, :] + lists_ref[1:2, :] + lists_ref[2:3, :]).astype(jnp.int32) - 1
    picks_ref[...] = (row_iota((POINTS_DEV, 1024)) == line).astype(F32).astype(BF16)


def rows_joined(below, here, above, low_mask, high_mask):
    parts = []
    for g in range(2):
        part = slice(g * LANES, (g + 1) * LANES)
        parts.append(
            here[:, part]
            + low_mask * turned(below[:, part], -12)
            + high_mask * turned(above[:, part], 12)
        )
    return parts


def section_kernel(
    first_far_ref,
    second_far_ref,
    low_ref,
    high_ref,
    lists_ref,
    picks_ref,
    matrices,
    inner_spread,
    inner_direct,
    inner_coefs,
    whole_ref,
    send_ref,
    outside,
    slopes,
    flux,
    plain,
    outer_coefs,
):
    even = lax.rem(lax.axis_index("curve"), 2) == 0
    outside[0] = jnp.where(even, second_far_ref[...], first_far_ref[...])
    outside[1] = jnp.where(even, first_far_ref[...], second_far_ref[...])

    def tile(r, g, start=0, size=TILE):
        offset = ((r % 2) * 2 + g) * TILE + start
        if r in (0, 1, 6, 7):
            return outside[r // 6, offset : offset + size, :]
        return (low_ref if r < 4 else high_ref)[offset : offset + size, :]

    outer_rows = (0, 1, 6, 7)
    outer_spread, outer_direct = local_terms(
        outer_rows,
        tile,
        matrices,
        slopes,
        flux,
        plain,
        outer_coefs,
        lambda r, g: {1: 24 * g, 6: 48 + 24 * g}.get(r),
    )

    lane = lane_iota((1, LANES)) % 16
    low_mask = (lane < 4).astype(F32)
    high_mask = (lane >= 12).astype(F32)

    def joined(outer, inner, size, r, start, count):
        def rows(k):
            if k in outer_rows:
                at = outer_rows.index(k) * size + start
                return outer[at : at + count, :]
            at = (k - 2) * size + start
            return inner[at : at + count, :]

        return rows_joined(rows(r - 1), rows(r), rows(r + 1), low_mask, high_mask)

    def coefficients(r, g, k):
        if r in outer_rows:
            at = (0 if r == 1 else 48) + 24 * g + 8 * k
            return outer_coefs[at : at + 8, :]
        at = (2 * (r - 2) + g) * 24 + 8 * k
        return inner_coefs[at : at + 8, :]

    inverse = {}
    smooth = []
    for r in range(1, 7):
        mass_sum = joined(outer_direct, inner_direct, 32, r, 24, 8)
        smoothing = joined(outer_spread, inner_spread, 56, r, 0, STATE)
        for g in range(2):
            inverse[r, g] = 1.0 / jnp.where(mass_sum[g] > 0.0, mass_sum[g], 1.0)
            smooth.append(smoothing[g] * jnp.concatenate([inverse[r, g]] * FIELDS, axis=0))
    again = gradient(jnp.concatenate(smooth, axis=0), matrices)
    flat = []
    for r in range(1, 7):
        parts = []
        for g in range(2):
            triple = tuple(
                jnp.concatenate([coefficients(r, g, k)] * FIELDS, axis=0) for k in range(3)
            )
            start = (2 * (r - 1) + g) * STATE
            parts += list(fluxes(again[start : start + STATE, :], triple))
        flat.append(jnp.concatenate(parts, axis=1))
    damped = divergence_joined(jnp.concatenate(flat, axis=0), matrices)

    ordered = []
    for r in range(2, 6):
        straight = joined(outer_direct, inner_direct, 32, r, 0, 24)
        carried = joined(outer_spread, inner_spread, 56, r, STATE, 16)
        damping = rows_joined(
            damped[(r - 2) * STATE : (r - 1) * STATE, :],
            damped[(r - 1) * STATE : r * STATE, :],
            damped[r * STATE : (r + 1) * STATE, :],
            low_mask,
            high_mask,
        )
        for g in range(2):
            change = (
                TIME_STEP * jnp.concatenate([straight[g], -carried[g]], axis=0)
                - (TIME_STEP * HYPER_NU) * damping[g]
            )
            scale = jnp.concatenate([inverse[r, g]] * FIELDS, axis=0)
            ordered.append(tile(r, g, 0, STATE) + change * scale)
    whole = jnp.concatenate(ordered, axis=1)
    whole_ref[...] = whole
    shares = [(lists_ref[k : k + 1, :] > 0.0).astype(F32) for k in range(3)]
    slots = [jnp.broadcast_to(lists_ref[3:4, :] * shares[k], (8, 1024)) for k in range(3)]
    row = row_iota((8, 1024))
    slot_rows = sum(jnp.where(row == k, slots[k], 0.0) for k in range(3))
    columns = jnp.concatenate([whole * share for share in shares] + [slot_rows], axis=0)
    upper, lower = halves(columns)
    sent = dot_last(picks_ref[...], jnp.concatenate([upper, lower], axis=0))
    send_ref[...] = sent[:, :LANES] + sent[:, LANES:]


def restore_kernel(whole_ref, place_ref, updated_ref):
    first, second, third = three_parts(whole_ref[...])
    hits = (row_iota((1024, POINTS_DEV)) == place_ref[0:1, :]).astype(F32).astype(BF16)
    updated_ref[...] = dot(first, hits) + dot(second, hits) + dot(third, hits)


def receive_kernel(received_ref, physics_ref):
    turned_over = received_ref[...].T
    upper, lower = halves(turned_over)
    places = slice(3 * STATE, 3 * STATE + 3)
    slot = turned_over[places, :].astype(jnp.int32) - 1
    row = row_iota((POINTS_DEV, POINTS_DEV))
    hits = (row == slot[0:1]) | (row == slot[1:2]) | (row == slot[2:3])
    rows = dot_last(jnp.concatenate([upper, lower], axis=0), hits.astype(F32).astype(BF16))
    rows = rows[:LANES] + rows[LANES:]
    own = rows[places, :] == (lane_iota((3, POINTS_DEV)) + 1).astype(F32)
    physics_ref[...] = jnp.where(
        own[0:1],
        rows[:STATE],
        jnp.where(own[1:2], rows[STATE : 2 * STATE], rows[2 * STATE : 3 * STATE]),
    )


def call(kernel, shapes, scratch=(), flops=0, moved=0, vmem=VMEM_LIMIT, **specs):
    return pl.pallas_call(
        kernel,
        out_shape=[jax.ShapeDtypeStruct(s, d) for s, d in shapes],
        scratch_shapes=list(scratch),
        **specs,
        compiler_params=pltpu.CompilerParams(vmem_limit_bytes=vmem),
        cost_estimate=pl.CostEstimate(flops=flops, bytes_accessed=moved, transcendentals=0),
    )


def swaps(count, pairs_from):
    route = []
    for i in range(pairs_from, count - 1, 2):
        route += [(i, i + 1), (i + 1, i)]
    return route


def body(
    evolving_state_array, point_id, neighbours, jacobian, inverse_metric, coriolis, column_slot
):
    anywhere = pl.BlockSpec(memory_space=pltpu.HBM)
    half = ((4 * TILE, LANES), F32)
    strip = ((TILE, LANES), F32)
    values_shape = ((TILE, POINTS_DEV), F32)
    far, close, values = call(
        strip_kernel,
        [strip, strip, values_shape],
        scratch=[
            pltpu.VMEM((8, ELEMS_DEV), jnp.int32),
            pltpu.VMEM((POINTS_DEV,), F32),
            pltpu.VMEM((POINTS_DEV,), F32),
            pltpu.VMEM((4, POINTS_DEV), F32),
            pltpu.VMEM((FIELDS, LEV, POINTS_DEV), F32),
            pltpu.SemaphoreType.DMA((5,)),
        ],
        in_specs=[anywhere] * 5,
        vmem=64 * 1024 * 1024 - 524288,
    )(evolving_state_array, jacobian, coriolis, inverse_metric, neighbours)
    cols, rows = lax.axis_size("col"), lax.axis_size("curve")
    from_far = lax.ppermute(far, "col", swaps(cols, 1) + [(cols - 1, 0), (0, cols - 1)])
    from_close = lax.ppermute(close, "col", swaps(cols, 0))
    low, high, place, lists = call(
        arrange_kernel,
        [half, half, ((8, POINTS_DEV), jnp.int32), ((8, 1024), F32)],
        flops=400_000_000,
        moved=1_000_000,
    )(values, neighbours, column_slot[None])
    first, second, low, high = call(margin_kernel, [half] * 4)(low, high, from_far, from_close)
    second_far = lax.ppermute(second, "curve", swaps(rows, 1))
    first_far = lax.ppermute(first, "curve", swaps(rows, 0))
    matrices = jnp.asarray(operators())
    scratch = [
        pltpu.VMEM((8 * TILE, 2 * LANES), F32),
        pltpu.VMEM((4 * 56, 4 * LANES), F32),
        pltpu.VMEM((4 * 32, 2 * LANES), F32),
    ]
    spread, direct, coefs, picks = call(
        inner_kernel,
        [
            ((4 * 56, 2 * LANES), F32),
            ((4 * 32, 2 * LANES), F32),
            ((8 * 24, LANES), F32),
            ((POINTS_DEV, 1024), BF16),
        ],
        scratch=scratch,
        flops=400_000_000,
        moved=1_000_000,
    )(low, high, lists, matrices)
    whole, sent = call(
        section_kernel,
        [((STATE, 1024), F32), ((POINTS_DEV, LANES), F32)],
        scratch=[pltpu.VMEM((2, 4 * TILE, LANES), F32)]
        + scratch
        + [pltpu.VMEM((4 * 24, LANES), F32)],
    )(first_far, second_far, low, high, lists, picks, matrices, spread, direct, coefs)
    received = lax.all_to_all(sent, "col", split_axis=0, concat_axis=0, tiled=True)
    (updated,) = call(
        restore_kernel, [((STATE, POINTS_DEV), F32)], flops=400_000_000, moved=1_000_000
    )(whole, place)
    (physics,) = call(receive_kernel, [((STATE, POINTS_DEV), F32)])(received)
    shape = evolving_state_array.shape
    return updated.reshape(shape), physics.reshape(shape)


def solution(mesh):
    split = ("curve", "col")
    return jax.shard_map(
        body,
        mesh=mesh,
        in_specs=(
            P(None, None, split),
            P(split),
            P(None, split),
            P(split),
            P(None, split),
            P(split),
            P(split),
        ),
        out_specs=(P(None, None, split), P(None, None, split)),
        check_vma=False,
    )
```

```python
import functools
import math

import jax
import jax.numpy as jnp
import numpy as np
from jax import lax
from jax.experimental import pallas as pl
from jax.experimental.pallas import tpu as pltpu
from jax.sharding import PartitionSpec as P

FIELDS = 5
LEV = 8
STATE = FIELDS * LEV
TILE = 48
LANES = 128
ELEMS_DEV = 48
POINTS_DEV = 768
N_COL = 32
CAP = 72
CAP_ROWS = CAP // 3
TIME_STEP = 0.1
HYPER_NU = 0.002
F32 = jnp.float32
BF16 = jnp.bfloat16
VMEM_LIMIT = 32 * 1024 * 1024


def gll_tables():
    root_fifth = 1.0 / math.sqrt(5.0)
    nodes = np.array([-1.0, -root_fifth, root_fifth, 1.0])
    weights = np.array([1.0, 5.0, 5.0, 1.0]) / 6.0
    table = np.zeros((4, 4))
    for i in range(4):
        for m in range(4):
            if i == m:
                table[i, m] = sum(1.0 / (nodes[i] - nodes[o]) for o in range(4) if o != i)
            else:
                upper = np.prod([nodes[i] - nodes[o] for o in range(4) if o != i])
                lower = np.prod([nodes[m] - nodes[o] for o in range(4) if o != m])
                table[i, m] = upper / (lower * (nodes[i] - nodes[m]))
    return table, weights


def two_parts(matrix):
    upper = matrix.astype(np.float32).astype(jnp.bfloat16)
    lower = (matrix - upper.astype(np.float64)).astype(np.float32).astype(jnp.bfloat16)
    return upper, lower


@functools.lru_cache(maxsize=None)
def operators():
    table, weights = gll_tables()
    eye4, eye8 = np.eye(4), np.eye(8)
    along_cycle = np.kron(eye4, table.T)
    along_rows = np.kron(table.T, eye4)
    grad = np.concatenate([np.kron(eye8, along_cycle), np.kron(eye8, along_rows)], axis=1)
    weight = np.diag(np.outer(weights, weights).reshape(16))
    div = np.concatenate(
        [np.kron(eye8, along_cycle @ weight), np.kron(eye8, along_rows @ weight)], axis=0
    )
    join = np.eye(256)
    for place in range(15):
        for j in range(4):
            low, high = place * 16 + 4 * j + 3, place * 16 + 16 + 4 * j
            join[low, high] = 1.0
            join[high, low] = 1.0
    both = np.zeros((512, 256))
    both[:256, :128] = div
    both[256:, 128:] = div
    div_join = both @ join
    grad_hi, grad_lo = two_parts(grad)
    div_hi, div_lo = two_parts(div_join)
    return np.concatenate(
        [grad_hi, grad_hi, grad_lo, div_hi, div_lo, join.astype(jnp.bfloat16)], axis=0
    )


def dot(left, right):
    return jnp.dot(left, right, preferred_element_type=F32)


def dot_last(left, right):
    return lax.dot_general(left, right, (((1,), (1,)), ((), ())), preferred_element_type=F32)


def halves(value):
    upper = value.astype(BF16)
    lower = (value - upper.astype(F32)).astype(BF16)
    return upper, lower


def lane_iota(shape):
    return lax.broadcasted_iota(jnp.int32, shape, 1)


def row_iota(shape):
    return lax.broadcasted_iota(jnp.int32, shape, 0)


def one_step(local, index):
    hit = (row_iota((ELEMS_DEV, ELEMS_DEV)) == index) & local
    return hit.astype(F32).astype(BF16)


def wide(local):
    return jnp.broadcast_to(local.astype(F32), (8, ELEMS_DEV))


def chain_length(local, index, doublings):
    length = wide(local)
    step = one_step(local, index)
    for k in range(doublings):
        length = length + dot(length.astype(BF16), step)
        if k + 1 < doublings:
            step = dot(step, step).astype(BF16)
    return length


def local_lists(near):
    base = (lax.axis_index("curve") * N_COL + lax.axis_index("col")) * ELEMS_DEV
    index = near - base
    return index, (index >= 0) & (index < ELEMS_DEV)


def over_points(element_values):
    shape = (ELEMS_DEV, POINTS_DEV)
    spread = (lane_iota(shape) // 16 == row_iota(shape)).astype(F32).astype(BF16)
    return dot(element_values.astype(BF16), spread)[0:1].astype(jnp.int32)


def three_parts(value):
    first = value.astype(BF16)
    rest = value - first.astype(F32)
    second = rest.astype(BF16)
    return first, second, (rest - second.astype(F32)).astype(BF16)


def strip_kernel(
    state_ref, jacobian_ref, coriolis_ref, metric_ref, near_ref, far_ref, close_ref, values_ref,
    near, jac, cor, metric, state, sems
):
    copies = [
        pltpu.make_async_copy(source, target, sems.at[i])
        for i, (source, target) in enumerate(
            [
                (near_ref, near),
                (state_ref, state),
                (jacobian_ref, jac),
                (coriolis_ref, cor),
                (metric_ref, metric),
            ]
        )
    ]
    for copy in copies:
        copy.start()
    copies[0].wait()
    index, local = local_lists(near[...])
    row = chain_length(local[2:3], index[2:3], 2)
    sides = []
    for side in range(2):
        here, there = local[side : side + 1], index[side : side + 1]
        second = dot(wide(here).astype(BF16), one_step(here, there))
        edge = wide(~here)
        sides.append((edge, wide(here) * (1.0 - second)))
    (first, second), (last, second_last) = sides
    unit = (first + second) * (2.0 * row + 1.0 + second)
    unit = unit + (last + second_last) * (2.0 * row + 9.0 + last)
    lane = (over_points(unit) - 1) * 16 + lane_iota((1, POINTS_DEV)) % 16
    hits = (row_iota((2 * LANES, POINTS_DEV)) == lane).astype(F32).astype(BF16)
    for copy in copies[1:]:
        copy.wait()
    values = jnp.concatenate(
        [
            state[...].reshape(STATE, POINTS_DEV),
            jac[...].reshape(1, POINTS_DEV),
            cor[...].reshape(1, POINTS_DEV),
            metric[...],
            jnp.zeros((2, POINTS_DEV), F32),
        ],
        axis=0,
    )
    values_ref[...] = values
    parts = dot_last(jnp.concatenate(three_parts(values), axis=0), hits)
    strips = parts[0:TILE] + parts[TILE : 2 * TILE] + parts[2 * TILE :]
    even = lax.rem(lax.axis_index("col"), 2) == 0
    to_left, to_right = strips[:, :LANES], strips[:, LANES:]
    far_ref[...] = jnp.where(even, to_left, to_right)
    close_ref[...] = jnp.where(even, to_right, to_left)


def arrange_kernel(values_ref, near_ref, slot_ref, low_ref, high_ref, place_ref, lists_ref):
    index, local = local_lists(near_ref[...])
    place = chain_length(local[0:1], index[0:1], 4)
    row = chain_length(local[2:3], index[2:3], 2)
    target = over_points(row * 16.0 + place + 2.0) * 16 + lane_iota((1, POINTS_DEV)) % 16
    place_ref[...] = jnp.broadcast_to(target, (8, POINTS_DEV))
    hits = (row_iota((1024, POINTS_DEV)) == target).astype(F32).astype(BF16)
    columns = send_lists(slot_ref[...])
    left = jnp.concatenate(three_parts(values_ref[...]), axis=0)
    upper, rest = halves(columns)
    left = jnp.concatenate([left, jnp.concatenate([columns, columns - upper.astype(F32)], axis=0).astype(BF16)], axis=0)
    parts = dot_last(left, hits)
    ordered = parts[0:TILE] + parts[TILE : 2 * TILE] + parts[2 * TILE : 3 * TILE]
    for r in range(4):
        for g in range(2):
            block = ordered[:, (2 * r + g) * LANES : (2 * r + g + 1) * LANES]
            ref = low_ref if r < 2 else high_ref
            start = ((r % 2) * 2 + g) * TILE
            ref[start : start + TILE, :] = block
    lists_ref[...] = parts[3 * TILE : 3 * TILE + 8] + parts[3 * TILE + 8 :]


def turned(block, by):
    by = by % LANES
    return block if by == 0 else pltpu.roll(block, by, 1)


def margin_kernel(
    low_in, high_in, from_far, from_close, first_ref, second_ref, low_ref, high_ref
):
    lane = lane_iota((TILE, LANES))
    even = lax.rem(lax.axis_index("col"), 2) == 0
    from_left = jnp.where(even, from_far[...], from_close[...])
    from_right = jnp.where(even, from_close[...], from_far[...])
    halves_of_rows = []
    for source, start_row in ((low_in, 0), (high_in, 2)):
        blocks = []
        for r in range(2):
            turn = start_row + r
            start = r * 2 * TILE
            blocks.append(
                jnp.where(lane < 32, turned(from_left, -32 * turn), source[start : start + TILE, :])
            )
            start += TILE
            blocks.append(
                jnp.where(
                    lane >= 96, turned(from_right, 96 - 32 * turn), source[start : start + TILE, :]
                )
            )
        halves_of_rows.append(jnp.concatenate(blocks, axis=0))
    low, high = halves_of_rows
    low_ref[...] = low
    high_ref[...] = high
    even = lax.rem(lax.axis_index("curve"), 2) == 0
    first_ref[...] = jnp.where(even, high, low)
    second_ref[...] = jnp.where(even, low, high)


def send_lists(slot):
    slot_value = slot.astype(F32)
    device = jnp.floor((slot_value + 0.5) * (1.0 / POINTS_DEV))
    within = slot_value - device * POINTS_DEV
    wanted = jnp.broadcast_to(device.astype(jnp.int32), (N_COL, POINTS_DEV))
    chosen = (wanted == row_iota((N_COL, POINTS_DEV))).astype(F32)
    square = (LANES, LANES)
    upto = (row_iota(square) <= lane_iota(square)).astype(F32)
    count = jnp.concatenate([upto, jnp.ones(square, F32)], axis=1).astype(BF16)
    groups = POINTS_DEV // LANES
    stacked = jnp.concatenate(
        [chosen[:, i * LANES : (i + 1) * LANES] for i in range(groups)], axis=0
    )
    counted = dot(stacked.astype(BF16), count)
    before = jnp.zeros((N_COL, LANES), F32)
    ranks = []
    for i in range(groups):
        rows = counted[i * N_COL : (i + 1) * N_COL]
        here = (rows[:, :LANES] + before) * stacked[i * N_COL : (i + 1) * N_COL]
        ranks.append(jnp.sum(here, axis=0, keepdims=True))
        before = before + rows[:, LANES:]
    rank = jnp.concatenate(ranks, axis=1) - 1.0
    third = (rank >= CAP_ROWS).astype(F32) + (rank >= 2 * CAP_ROWS).astype(F32)
    line = device * CAP_ROWS + rank - third * CAP_ROWS
    lists = [jnp.where(third == float(k), line + 1.0, 0.0) for k in range(3)]
    filler = jnp.zeros((4, POINTS_DEV), F32)
    return jnp.concatenate(lists + [within + 1.0, filler], axis=0)


def fluxes(slope, coefficients):
    along_cycle, along_rows = slope[:, :LANES], slope[:, LANES:]
    caa, cab, cbb = coefficients
    return caa * along_cycle + cab * along_rows, cab * along_cycle + cbb * along_rows


def gradient(values, matrices):
    upper, lower = halves(values)
    return dot(jnp.concatenate([upper, lower], axis=1), matrices[0:256, :]) + dot(
        upper, matrices[256:384, :]
    )


def divergence_joined(values, matrices):
    upper, lower = halves(values)
    first = matrices[384:896, :]
    return dot(upper, first) + dot(lower, first) + dot(upper, matrices[896:1408, :])


def local_terms(rows, tile, matrices, slopes, flux, plain, coefs, coefs_at):
    cells = [(n, r, g) for n, r in enumerate(rows) for g in range(2)]
    stacked = []
    for _, r, g in cells:
        zonal, meridional = tile(r, g, 0, 8), tile(r, g, 8, 8)
        energy = 0.5 * (zonal * zonal + meridional * meridional) + tile(r, g, 16, 8)
        stacked += [tile(r, g, 0, STATE), energy]
    slopes[...] = gradient(jnp.concatenate(stacked, axis=0), matrices)
    lane = lane_iota((8, LANES))
    inner_i = (lane % 4 == 1) | (lane % 4 == 2)
    inner_j = (lane // 4 % 4 == 1) | (lane // 4 % 4 == 2)
    weight = jnp.where(inner_i, 5.0 / 6.0, 1.0 / 6.0) * jnp.where(inner_j, 5.0 / 6.0, 1.0 / 6.0)
    for n, r, g in cells:

        def line(k):
            return jnp.broadcast_to(tile(r, g, STATE + k, 1), (8, LANES))

        jacobian, coriolis = line(0), line(1)
        m11, m12, m21, m22 = 1.0 + line(2), line(3), line(4), 1.0 + line(5)
        caa = jacobian * (m11 * m11 + m12 * m12)
        cab = jacobian * (m11 * m21 + m12 * m22)
        cbb = jacobian * (m21 * m21 + m22 * m22)
        at = coefs_at(r, g)
        if at is not None:
            coefs[at : at + 8, :] = caa
            coefs[at + 8 : at + 16, :] = cab
            coefs[at + 16 : at + 24, :] = cbb
        mass = jacobian * weight
        at = (2 * n + g) * TILE
        first = slice(g * 2 * LANES, (g * 2 + 1) * LANES)
        second = slice((g * 2 + 1) * LANES, (g * 2 + 2) * LANES)
        for f in range(FIELDS):
            one, two = fluxes(slopes[at + 8 * f : at + 8 * f + 8, :], (caa, cab, cbb))
            flux[n * 56 + 8 * f : n * 56 + 8 * f + 8, first] = one
            flux[n * 56 + 8 * f : n * 56 + 8 * f + 8, second] = two
        zonal, meridional = tile(r, g, 0, 8), tile(r, g, 8, 8)
        flow1 = jacobian * (m11 * zonal + m12 * meridional)
        flow2 = jacobian * (m21 * zonal + m22 * meridional)
        for k in range(2):
            carried = tile(r, g, 24 + 8 * k, 8)
            flux[n * 56 + 40 + 8 * k : n * 56 + 48 + 8 * k, first] = carried * flow1
            flux[n * 56 + 40 + 8 * k : n * 56 + 48 + 8 * k, second] = carried * flow2
        ea, eb = slopes[at + 40 : at + 48, :LANES], slopes[at + 40 : at + 48, LANES:]
        ta, tb = slopes[at + 16 : at + 24, :LANES], slopes[at + 16 : at + 24, LANES:]
        part = slice(g * LANES, (g + 1) * LANES)
        plain[n * 32 : n * 32 + 8, part] = mass * (coriolis * meridional - (m11 * ea + m21 * eb))
        plain[n * 32 + 8 : n * 32 + 16, part] = -mass * (coriolis * zonal + (m12 * ea + m22 * eb))
        plain[n * 32 + 16 : n * 32 + 24, part] = -mass * (
            zonal * (m11 * ta + m21 * tb) + meridional * (m12 * ta + m22 * tb)
        )
        plain[n * 32 + 24 : n * 32 + 32, part] = mass
    spread = divergence_joined(flux[...], matrices)
    upper, lower = halves(plain[...])
    join = matrices[1408:1664, :]
    return spread, dot(upper, join) + dot(lower, join)


def inner_kernel(
    low_ref, high_ref, lists_ref, matrices, spread_ref, direct_ref, coefs, picks_ref, slopes, flux, plain
):
    def tile(r, g, start=0, size=TILE):
        offset = ((r % 2) * 2 + g) * TILE + start
        return (low_ref if r < 2 else high_ref)[offset : offset + size, :]

    spread, direct = local_terms(
        range(4), tile, matrices, slopes, flux, plain, coefs, lambda r, g: (2 * r + g) * 24
    )
    spread_ref[...] = spread
    direct_ref[...] = direct
    line = (lists_ref[0:1, :] + lists_ref[1:2, :] + lists_ref[2:3, :]).astype(jnp.int32) - 1
    picks_ref[...] = (row_iota((POINTS_DEV, 1024)) == line).astype(F32).astype(BF16)


def rows_joined(below, here, above, low_mask, high_mask):
    parts = []
    for g in range(2):
        part = slice(g * LANES, (g + 1) * LANES)
        parts.append(
            here[:, part]
            + low_mask * turned(below[:, part], -12)
            + high_mask * turned(above[:, part], 12)
        )
    return parts


def section_kernel(
    second_far_ref,
    first_far_ref,
    low_ref,
    high_ref,
    lists_ref,
    picks_ref,
    matrices,
    inner_spread,
    inner_direct,
    inner_coefs,
    whole_ref,
    send_ref,
    outside,
    slopes,
    flux,
    plain,
    outer_coefs,
):
    even = lax.rem(lax.axis_index("curve"), 2) == 0
    outside[0] = jnp.where(even, second_far_ref[...], first_far_ref[...])
    outside[1] = jnp.where(even, first_far_ref[...], second_far_ref[...])

    def tile(r, g, start=0, size=TILE):
        offset = ((r % 2) * 2 + g) * TILE + start
        if r in (0, 1, 6, 7):
            return outside[r // 6, offset : offset + size, :]
        return (low_ref if r < 4 else high_ref)[offset : offset + size, :]

    outer_rows = (0, 1, 6, 7)
    outer_spread, outer_direct = local_terms(
        outer_rows,
        tile,
        matrices,
        slopes,
        flux,
        plain,
        outer_coefs,
        lambda r, g: {1: 24 * g, 6: 48 + 24 * g}.get(r),
    )

    lane = lane_iota((1, LANES)) % 16
    low_mask = (lane < 4).astype(F32)
    high_mask = (lane >= 12).astype(F32)

    def joined(outer, inner, size, r, start, count):
        def rows(k):
            if k in outer_rows:
                at = outer_rows.index(k) * size + start
                return outer[at : at + count, :]
            at = (k - 2) * size + start
            return inner[at : at + count, :]

        return rows_joined(rows(r - 1), rows(r), rows(r + 1), low_mask, high_mask)

    def coefficients(r, g, k):
        if r in outer_rows:
            at = (0 if r == 1 else 48) + 24 * g + 8 * k
            return outer_coefs[at : at + 8, :]
        at = (2 * (r - 2) + g) * 24 + 8 * k
        return inner_coefs[at : at + 8, :]

    inverse = {}
    smooth = []
    for r in range(1, 7):
        mass_sum = joined(outer_direct, inner_direct, 32, r, 24, 8)
        smoothing = joined(outer_spread, inner_spread, 56, r, 0, STATE)
        for g in range(2):
            inverse[r, g] = 1.0 / jnp.where(mass_sum[g] > 0.0, mass_sum[g], 1.0)
            smooth.append(smoothing[g] * jnp.concatenate([inverse[r, g]] * FIELDS, axis=0))
    again = gradient(jnp.concatenate(smooth, axis=0), matrices)
    flat = []
    for r in range(1, 7):
        parts = []
        for g in range(2):
            triple = tuple(
                jnp.concatenate([coefficients(r, g, k)] * FIELDS, axis=0) for k in range(3)
            )
            start = (2 * (r - 1) + g) * STATE
            parts += list(fluxes(again[start : start + STATE, :], triple))
        flat.append(jnp.concatenate(parts, axis=1))
    damped = divergence_joined(jnp.concatenate(flat, axis=0), matrices)

    ordered = []
    for r in range(2, 6):
        straight = joined(outer_direct, inner_direct, 32, r, 0, 24)
        carried = joined(outer_spread, inner_spread, 56, r, STATE, 16)
        damping = rows_joined(
            damped[(r - 2) * STATE : (r - 1) * STATE, :],
            damped[(r - 1) * STATE : r * STATE, :],
            damped[r * STATE : (r + 1) * STATE, :],
            low_mask,
            high_mask,
        )
        for g in range(2):
            change = (
                TIME_STEP * jnp.concatenate([straight[g], -carried[g]], axis=0)
                - (TIME_STEP * HYPER_NU) * damping[g]
            )
            scale = jnp.concatenate([inverse[r, g]] * FIELDS, axis=0)
            ordered.append(tile(r, g, 0, STATE) + change * scale)
    whole = jnp.concatenate(ordered, axis=1)
    whole_ref[...] = whole
    shares = [(lists_ref[k : k + 1, :] > 0.0).astype(F32) for k in range(3)]
    slots = [jnp.broadcast_to(lists_ref[3:4, :] * shares[k], (8, 1024)) for k in range(3)]
    row = row_iota((8, 1024))
    slot_rows = sum(jnp.where(row == k, slots[k], 0.0) for k in range(3))
    columns = jnp.concatenate([whole * share for share in shares] + [slot_rows], axis=0)
    upper, lower = halves(columns)
    sent = dot_last(picks_ref[...], jnp.concatenate([upper, lower], axis=0))
    send_ref[...] = sent[:, :LANES] + sent[:, LANES:]


def restore_kernel(whole_ref, place_ref, updated_ref):
    first, second, third = three_parts(whole_ref[...])
    hits = (row_iota((1024, POINTS_DEV)) == place_ref[0:1, :]).astype(F32).astype(BF16)
    updated_ref[...] = dot(first, hits) + dot(second, hits) + dot(third, hits)


def receive_kernel(received_ref, physics_ref):
    turned_over = received_ref[...].T
    upper, lower = halves(turned_over)
    places = slice(3 * STATE, 3 * STATE + 3)
    slot = turned_over[places, :].astype(jnp.int32) - 1
    row = row_iota((POINTS_DEV, POINTS_DEV))
    hits = (row == slot[0:1]) | (row == slot[1:2]) | (row == slot[2:3])
    rows = dot_last(jnp.concatenate([upper, lower], axis=0), hits.astype(F32).astype(BF16))
    rows = rows[:LANES] + rows[LANES:]
    own = rows[places, :] == (lane_iota((3, POINTS_DEV)) + 1).astype(F32)
    physics_ref[...] = jnp.where(
        own[0:1],
        rows[:STATE],
        jnp.where(own[1:2], rows[STATE : 2 * STATE], rows[2 * STATE : 3 * STATE]),
    )


def call(kernel, shapes, scratch=(), flops=0, moved=0, vmem=VMEM_LIMIT, **specs):
    return pl.pallas_call(
        kernel,
        out_shape=[jax.ShapeDtypeStruct(s, d) for s, d in shapes],
        scratch_shapes=list(scratch),
        **specs,
        compiler_params=pltpu.CompilerParams(vmem_limit_bytes=vmem),
        cost_estimate=pl.CostEstimate(flops=flops, bytes_accessed=moved, transcendentals=0),
    )


def swaps(count, pairs_from):
    route = []
    for i in range(pairs_from, count - 1, 2):
        route += [(i, i + 1), (i + 1, i)]
    return route


def body(
    evolving_state_array, point_id, neighbours, jacobian, inverse_metric, coriolis, column_slot
):
    anywhere = pl.BlockSpec(memory_space=pltpu.HBM)
    half = ((4 * TILE, LANES), F32)
    strip = ((TILE, LANES), F32)
    values_shape = ((TILE, POINTS_DEV), F32)
    far, close, values = call(
        strip_kernel,
        [strip, strip, values_shape],
        scratch=[
            pltpu.VMEM((8, ELEMS_DEV), jnp.int32),
            pltpu.VMEM((POINTS_DEV,), F32),
            pltpu.VMEM((POINTS_DEV,), F32),
            pltpu.VMEM((4, POINTS_DEV), F32),
            pltpu.VMEM((FIELDS, LEV, POINTS_DEV), F32),
            pltpu.SemaphoreType.DMA((5,)),
        ],
        in_specs=[anywhere] * 5,
        vmem=64 * 1024 * 1024 - 524288,
    )(evolving_state_array, jacobian, coriolis, inverse_metric, neighbours)
    cols, rows = lax.axis_size("col"), lax.axis_size("curve")
    from_far = lax.ppermute(far, "col", swaps(cols, 1) + [(cols - 1, 0), (0, cols - 1)])
    from_close = lax.ppermute(close, "col", swaps(cols, 0))
    low, high, place, lists = call(
        arrange_kernel,
        [half, half, ((8, POINTS_DEV), jnp.int32), ((8, 1024), F32)],
        flops=400_000_000,
        moved=1_000_000,
    )(values, neighbours, column_slot[None])
    first, second, low, high = call(margin_kernel, [half] * 4)(low, high, from_far, from_close)
    second_far = lax.ppermute(second, "curve", swaps(rows, 1))
    first_far = lax.ppermute(first, "curve", swaps(rows, 0))
    matrices = jnp.asarray(operators())
    scratch = [
        pltpu.VMEM((8 * TILE, 2 * LANES), F32),
        pltpu.VMEM((4 * 56, 4 * LANES), F32),
        pltpu.VMEM((4 * 32, 2 * LANES), F32),
    ]
    spread, direct, coefs, picks = call(
        inner_kernel,
        [
            ((4 * 56, 2 * LANES), F32),
            ((4 * 32, 2 * LANES), F32),
            ((8 * 24, LANES), F32),
            ((POINTS_DEV, 1024), BF16),
        ],
        scratch=scratch,
        flops=400_000_000,
        moved=1_000_000,
    )(low, high, lists, matrices)
    whole, sent = call(
        section_kernel,
        [((STATE, 1024), F32), ((POINTS_DEV, LANES), F32)],
        scratch=[pltpu.VMEM((2, 4 * TILE, LANES), F32)]
        + scratch
        + [pltpu.VMEM((4 * 24, LANES), F32)],
    )(second_far, first_far, low, high, lists, picks, matrices, spread, direct, coefs)
    received = lax.all_to_all(sent, "col", split_axis=0, concat_axis=0, tiled=True)
    (updated,) = call(
        restore_kernel, [((STATE, POINTS_DEV), F32)], flops=400_000_000, moved=1_000_000
    )(whole, place)
    (physics,) = call(receive_kernel, [((STATE, POINTS_DEV), F32)])(received)
    shape = evolving_state_array.shape
    return updated.reshape(shape), physics.reshape(shape)


def solution(mesh):
    split = ("curve", "col")
    return jax.shard_map(
        body,
        mesh=mesh,
        in_specs=(
            P(None, None, split),
            P(split),
            P(None, split),
            P(split),
            P(None, split),
            P(split),
            P(split),
        ),
        out_specs=(P(None, None, split), P(None, None, split)),
        check_vma=False,
    )
```

```python
import functools
import math

import jax
import jax.numpy as jnp
import numpy as np
from jax import lax
from jax.experimental import pallas as pl
from jax.experimental.pallas import tpu as pltpu
from jax.sharding import PartitionSpec as P

FIELDS = 5
LEV = 8
STATE = FIELDS * LEV
TILE = 48
LANES = 128
ELEMS_DEV = 48
POINTS_DEV = 768
N_COL = 32
CAP = 72
CAP_ROWS = CAP // 3
TIME_STEP = 0.1
HYPER_NU = 0.002
F32 = jnp.float32
BF16 = jnp.bfloat16
VMEM_LIMIT = 32 * 1024 * 1024


def gll_tables():
    root_fifth = 1.0 / math.sqrt(5.0)
    nodes = np.array([-1.0, -root_fifth, root_fifth, 1.0])
    weights = np.array([1.0, 5.0, 5.0, 1.0]) / 6.0
    table = np.zeros((4, 4))
    for i in range(4):
        for m in range(4):
            if i == m:
                table[i, m] = sum(1.0 / (nodes[i] - nodes[o]) for o in range(4) if o != i)
            else:
                upper = np.prod([nodes[i] - nodes[o] for o in range(4) if o != i])
                lower = np.prod([nodes[m] - nodes[o] for o in range(4) if o != m])
                table[i, m] = upper / (lower * (nodes[i] - nodes[m]))
    return table, weights


def two_parts(matrix):
    upper = matrix.astype(np.float32).astype(jnp.bfloat16)
    lower = (matrix - upper.astype(np.float64)).astype(np.float32).astype(jnp.bfloat16)
    return upper, lower


@functools.lru_cache(maxsize=None)
def operators():
    table, weights = gll_tables()
    eye4, eye8 = np.eye(4), np.eye(8)
    along_cycle = np.kron(eye4, table.T)
    along_rows = np.kron(table.T, eye4)
    grad = np.concatenate([np.kron(eye8, along_cycle), np.kron(eye8, along_rows)], axis=1)
    weight = np.diag(np.outer(weights, weights).reshape(16))
    div = np.concatenate(
        [np.kron(eye8, along_cycle @ weight), np.kron(eye8, along_rows @ weight)], axis=0
    )
    join = np.eye(256)
    for place in range(15):
        for j in range(4):
            low, high = place * 16 + 4 * j + 3, place * 16 + 16 + 4 * j
            join[low, high] = 1.0
            join[high, low] = 1.0
    both = np.zeros((512, 256))
    both[:256, :128] = div
    both[256:, 128:] = div
    div_join = both @ join
    grad_hi, grad_lo = two_parts(grad)
    div_hi, div_lo = two_parts(div_join)
    return np.concatenate(
        [grad_hi, grad_hi, grad_lo, div_hi, div_lo, join.astype(jnp.bfloat16)], axis=0
    )


def dot(left, right):
    return jnp.dot(left, right, preferred_element_type=F32)


def dot_last(left, right):
    return lax.dot_general(left, right, (((1,), (1,)), ((), ())), preferred_element_type=F32)


def halves(value):
    upper = value.astype(BF16)
    lower = (value - upper.astype(F32)).astype(BF16)
    return upper, lower


def lane_iota(shape):
    return lax.broadcasted_iota(jnp.int32, shape, 1)


def row_iota(shape):
    return lax.broadcasted_iota(jnp.int32, shape, 0)


def one_step(local, index):
    hit = (row_iota((ELEMS_DEV, ELEMS_DEV)) == index) & local
    return hit.astype(F32).astype(BF16)


def wide(local):
    return jnp.broadcast_to(local.astype(F32), (8, ELEMS_DEV))


def chain_length(local, index, doublings):
    length = wide(local)
    step = one_step(local, index)
    for k in range(doublings):
        length = length + dot(length.astype(BF16), step)
        if k + 1 < doublings:
            step = dot(step, step).astype(BF16)
    return length


def local_lists(near):
    base = (lax.axis_index("curve") * N_COL + lax.axis_index("col")) * ELEMS_DEV
    index = near - base
    return index, (index >= 0) & (index < ELEMS_DEV)


def over_points(element_values):
    shape = (ELEMS_DEV, POINTS_DEV)
    spread = (lane_iota(shape) // 16 == row_iota(shape)).astype(F32).astype(BF16)
    return dot(element_values.astype(BF16), spread)[0:1].astype(jnp.int32)


def three_parts(value):
    first = value.astype(BF16)
    rest = value - first.astype(F32)
    second = rest.astype(BF16)
    return first, second, (rest - second.astype(F32)).astype(BF16)


def strip_kernel(
    state_ref, jacobian_ref, coriolis_ref, metric_ref, near_ref, slot_ref, far_ref, close_ref,
    values_ref, near, jac, cor, metric, slot, state, sems
):
    copies = [
        pltpu.make_async_copy(source, target, sems.at[i])
        for i, (source, target) in enumerate(
            [
                (near_ref, near),
                (state_ref, state),
                (jacobian_ref, jac),
                (coriolis_ref, cor),
                (metric_ref, metric),
                (slot_ref, slot),
            ]
        )
    ]
    for copy in copies:
        copy.start()
    copies[0].wait()
    index, local = local_lists(near[...])
    row = chain_length(local[2:3], index[2:3], 2)
    sides = []
    for side in range(2):
        here, there = local[side : side + 1], index[side : side + 1]
        second = dot(wide(here).astype(BF16), one_step(here, there))
        edge = wide(~here)
        sides.append((edge, wide(here) * (1.0 - second)))
    (first, second), (last, second_last) = sides
    unit = (first + second) * (2.0 * row + 1.0 + second)
    unit = unit + (last + second_last) * (2.0 * row + 9.0 + last)
    lane = (over_points(unit) - 1) * 16 + lane_iota((1, POINTS_DEV)) % 16
    hits = (row_iota((2 * LANES, POINTS_DEV)) == lane).astype(F32).astype(BF16)
    for copy in copies[1:]:
        copy.wait()
    values = jnp.concatenate(
        [
            state[...].reshape(STATE, POINTS_DEV),
            jac[...].reshape(1, POINTS_DEV),
            cor[...].reshape(1, POINTS_DEV),
            metric[...],
            slot[...].astype(F32).reshape(1, POINTS_DEV),
            jnp.zeros((1, POINTS_DEV), F32),
        ],
        axis=0,
    )
    values_ref[0:TILE, :] = values
    values_ref[TILE:, 0:ELEMS_DEV] = jnp.where(local, index, -1).astype(F32)
    parts = dot_last(jnp.concatenate(three_parts(values), axis=0), hits)
    strips = parts[0:TILE] + parts[TILE : 2 * TILE] + parts[2 * TILE :]
    even = lax.rem(lax.axis_index("col"), 2) == 0
    to_left, to_right = strips[:, :LANES], strips[:, LANES:]
    far_ref[...] = jnp.where(even, to_left, to_right)
    close_ref[...] = jnp.where(even, to_right, to_left)


def arrange_kernel(values_ref, low_ref, high_ref, place_ref):
    index = values_ref[TILE:, 0:ELEMS_DEV].astype(jnp.int32)
    local = index >= 0
    place = chain_length(local[0:1], index[0:1], 4)
    row = chain_length(local[2:3], index[2:3], 2)
    target = over_points(row * 16.0 + place + 2.0) * 16 + lane_iota((1, POINTS_DEV)) % 16
    place_ref[...] = jnp.broadcast_to(target, (8, POINTS_DEV))
    hits = (row_iota((1024, POINTS_DEV)) == target).astype(F32).astype(BF16)
    parts = dot_last(jnp.concatenate(three_parts(values_ref[0:TILE, :]), axis=0), hits)
    ordered = parts[0:TILE] + parts[TILE : 2 * TILE] + parts[2 * TILE :]
    for r in range(4):
        for g in range(2):
            block = ordered[:, (2 * r + g) * LANES : (2 * r + g + 1) * LANES]
            ref = low_ref if r < 2 else high_ref
            start = ((r % 2) * 2 + g) * TILE
            ref[start : start + TILE, :] = block


def turned(block, by):
    by = by % LANES
    return block if by == 0 else pltpu.roll(block, by, 1)


def margin_kernel(
    low_in, high_in, from_far, from_close, first_ref, second_ref, low_ref, high_ref
):
    lane = lane_iota((TILE, LANES))
    even = lax.rem(lax.axis_index("col"), 2) == 0
    from_left = jnp.where(even, from_far[...], from_close[...])
    from_right = jnp.where(even, from_close[...], from_far[...])
    halves_of_rows = []
    for source, start_row in ((low_in, 0), (high_in, 2)):
        blocks = []
        for r in range(2):
            turn = start_row + r
            start = r * 2 * TILE
            blocks.append(
                jnp.where(lane < 32, turned(from_left, -32 * turn), source[start : start + TILE, :])
            )
            start += TILE
            blocks.append(
                jnp.where(
                    lane >= 96, turned(from_right, 96 - 32 * turn), source[start : start + TILE, :]
                )
            )
        halves_of_rows.append(jnp.concatenate(blocks, axis=0))
    low, high = halves_of_rows
    low_ref[...] = low
    high_ref[...] = high
    even = lax.rem(lax.axis_index("curve"), 2) == 0
    first_ref[...] = jnp.where(even, high, low)
    second_ref[...] = jnp.where(even, low, high)


def send_lists(slots):
    square = (LANES, LANES)
    upto = (row_iota(square) <= lane_iota(square)).astype(F32)
    count = jnp.concatenate([upto, jnp.ones(square, F32)], axis=1).astype(BF16)
    lane = lane_iota((1, LANES))
    chosen, devices, withins, owns = [], [], [], []
    for i, slot in enumerate(slots):
        own = lane >= 32 if i % 2 == 0 else lane < 96
        device = jnp.where(own, jnp.floor((slot + 0.5) * (1.0 / POINTS_DEV)), -1.0)
        wanted = jnp.broadcast_to(device.astype(jnp.int32), (N_COL, LANES))
        chosen.append((wanted == row_iota((N_COL, LANES))).astype(F32))
        devices.append(device)
        withins.append(slot - device * POINTS_DEV)
        owns.append(own)
    counted = dot(jnp.concatenate(chosen, axis=0).astype(BF16), count)
    before = jnp.zeros((N_COL, LANES), F32)
    lists = []
    for i, (device, within, own) in enumerate(zip(devices, withins, owns)):
        rows = counted[i * N_COL : (i + 1) * N_COL]
        rank = jnp.sum((rows[:, :LANES] + before) * chosen[i], axis=0, keepdims=True) - 1.0
        before = before + rows[:, LANES:]
        third = (rank >= CAP_ROWS).astype(F32) + (rank >= 2 * CAP_ROWS).astype(F32)
        line = device * CAP_ROWS + rank - third * CAP_ROWS
        parts = [jnp.where(own & (third == float(k)), line + 1.0, 0.0) for k in range(3)]
        filler = jnp.zeros((4, LANES), F32)
        lists.append(
            jnp.concatenate(parts + [jnp.where(own, within + 1.0, 0.0), filler], axis=0)
        )
    return jnp.concatenate(lists, axis=1)


def fluxes(slope, coefficients):
    along_cycle, along_rows = slope[:, :LANES], slope[:, LANES:]
    caa, cab, cbb = coefficients
    return caa * along_cycle + cab * along_rows, cab * along_cycle + cbb * along_rows


def gradient(values, matrices):
    upper, lower = halves(values)
    return dot(jnp.concatenate([upper, lower], axis=1), matrices[0:256, :]) + dot(
        upper, matrices[256:384, :]
    )


def divergence_joined(values, matrices):
    upper, lower = halves(values)
    first = matrices[384:896, :]
    return dot(upper, first) + dot(lower, first) + dot(upper, matrices[896:1408, :])


def rows_joined(below, here, above, low_mask, high_mask):
    parts = []
    for g in range(2):
        part = slice(g * LANES, (g + 1) * LANES)
        parts.append(
            here[:, part]
            + low_mask * turned(below[:, part], -12)
            + high_mask * turned(above[:, part], 12)
        )
    return parts


def row_starts(rows):
    slope, flux, plain = {}, {}, {}
    at = [0, 0, 0]
    for r in rows:
        lean = r in (0, 7)
        for g in range(2):
            slope[r, g] = at[0]
            at[0] += STATE if lean else TILE
        flux[r] = at[1]
        at[1] += STATE if lean else STATE + 16
        plain[r] = at[2]
        at[2] += 8 if lean else 32
    return slope, flux, plain, at


def local_terms(rows, tile, matrices, slopes, flux, plain, coefs, coefs_at):
    slope_at, flux_at, plain_at, _ = row_starts(rows)
    cells = [(r, g) for r in rows for g in range(2)]
    stacked = []
    for r, g in cells:
        stacked.append(tile(r, g, 0, STATE))
        if r not in (0, 7):
            zonal, meridional = tile(r, g, 0, 8), tile(r, g, 8, 8)
            energy = 0.5 * (zonal * zonal + meridional * meridional) + tile(r, g, 16, 8)
            stacked.append(energy)
    slopes[...] = gradient(jnp.concatenate(stacked, axis=0), matrices)
    lane = lane_iota((8, LANES))
    inner_i = (lane % 4 == 1) | (lane % 4 == 2)
    inner_j = (lane // 4 % 4 == 1) | (lane // 4 % 4 == 2)
    weight = jnp.where(inner_i, 5.0 / 6.0, 1.0 / 6.0) * jnp.where(inner_j, 5.0 / 6.0, 1.0 / 6.0)
    for r, g in cells:

        def line(k):
            return jnp.broadcast_to(tile(r, g, STATE + k, 1), (8, LANES))

        jacobian, coriolis = line(0), line(1)
        m11, m12, m21, m22 = 1.0 + line(2), line(3), line(4), 1.0 + line(5)
        caa = jacobian * (m11 * m11 + m12 * m12)
        cab = jacobian * (m11 * m21 + m12 * m22)
        cbb = jacobian * (m21 * m21 + m22 * m22)
        at = coefs_at(r, g)
        if at is not None:
            coefs[at : at + 8, :] = caa
            coefs[at + 8 : at + 16, :] = cab
            coefs[at + 16 : at + 24, :] = cbb
        mass = jacobian * weight
        at = slope_at[r, g]
        first = slice(g * 2 * LANES, (g * 2 + 1) * LANES)
        second = slice((g * 2 + 1) * LANES, (g * 2 + 2) * LANES)
        part = slice(g * LANES, (g + 1) * LANES)
        to, direct = flux_at[r], plain_at[r]
        for f in range(FIELDS):
            one, two = fluxes(slopes[at + 8 * f : at + 8 * f + 8, :], (caa, cab, cbb))
            flux[to + 8 * f : to + 8 * f + 8, first] = one
            flux[to + 8 * f : to + 8 * f + 8, second] = two
        plain[direct : direct + 8, part] = mass
        if r in (0, 7):
            continue
        zonal, meridional = tile(r, g, 0, 8), tile(r, g, 8, 8)
        flow1 = jacobian * (m11 * zonal + m12 * meridional)
        flow2 = jacobian * (m21 * zonal + m22 * meridional)
        for k in range(2):
            carried = tile(r, g, 24 + 8 * k, 8)
            flux[to + 40 + 8 * k : to + 48 + 8 * k, first] = carried * flow1
            flux[to + 40 + 8 * k : to + 48 + 8 * k, second] = carried * flow2
        ea, eb = slopes[at + 40 : at + 48, :LANES], slopes[at + 40 : at + 48, LANES:]
        ta, tb = slopes[at + 16 : at + 24, :LANES], slopes[at + 16 : at + 24, LANES:]
        plain[direct + 8 : direct + 16, part] = mass * (
            coriolis * meridional - (m11 * ea + m21 * eb)
        )
        plain[direct + 16 : direct + 24, part] = -mass * (
            coriolis * zonal + (m12 * ea + m22 * eb)
        )
        plain[direct + 24 : direct + 32, part] = -mass * (
            zonal * (m11 * ta + m21 * tb) + meridional * (m12 * ta + m22 * tb)
        )
    spread = divergence_joined(flux[...], matrices)
    upper, lower = halves(plain[...])
    join = matrices[1408:1664, :]
    return spread, dot(upper, join) + dot(lower, join)


def face_masks():
    lane = lane_iota((1, LANES)) % 16
    return (lane < 4).astype(F32), (lane >= 12).astype(F32)


def repeated(block):
    return jnp.concatenate([block] * FIELDS, axis=0)


def second_laplacian(rows, smoothing, inverse, coefficients, matrices):
    smooth = [smoothing[r][g] * repeated(inverse[r, g]) for r in rows for g in range(2)]
    again = gradient(jnp.concatenate(smooth, axis=0), matrices)
    flat = []
    for n, r in enumerate(rows):
        parts = []
        for g in range(2):
            triple = tuple(repeated(coefficients(r, g, k)) for k in range(3))
            start = (2 * n + g) * STATE
            parts += list(fluxes(again[start : start + STATE, :], triple))
        flat.append(jnp.concatenate(parts, axis=1))
    return divergence_joined(jnp.concatenate(flat, axis=0), matrices)


def mass_inverse(mass_sum):
    return 1.0 / jnp.where(mass_sum > 0.0, mass_sum, 1.0)


def advanced(state, straight, carried, inverse):
    return state + (TIME_STEP * jnp.concatenate([straight, -carried], axis=0)) * repeated(inverse)


OWN_ROWS = (2, 3, 4, 5)
OUTER_ROWS = (0, 1, 6, 7)
MIDDLE_ROWS = (3, 4)
EDGE_ROWS = (1, 2, 5, 6)


def inner_kernel(
    low_ref,
    high_ref,
    matrices,
    lists_ref,
    spread_ref,
    direct_ref,
    coefs,
    picks_ref,
    middle_ref,
    damped_ref,
    inverse_ref,
    slopes,
    flux,
    plain,
):
    def tile(r, g, start=0, size=TILE):
        offset = ((r % 2) * 2 + g) * TILE + start
        return (low_ref if r < 4 else high_ref)[offset : offset + size, :]

    def coefs_at(r, g):
        return (2 * (r - 2) + g) * 24

    lists = send_lists([tile(r, g, STATE + 6, 1) for r in OWN_ROWS for g in range(2)])
    lists_ref[...] = lists
    line = (lists[0:1] + lists[1:2] + lists[2:3]).astype(jnp.int32) - 1
    picks_ref[...] = (row_iota((POINTS_DEV, 1024)) == line).astype(F32).astype(BF16)
    spread, direct = local_terms(
        OWN_ROWS, tile, matrices, slopes, flux, plain, coefs, coefs_at
    )
    spread_ref[...] = spread
    direct_ref[...] = direct
    masks = face_masks()

    def joined(value, size, r, start, count):
        def rows(k):
            at = (k - 2) * size + start
            return value[at : at + count, :]

        return rows_joined(rows(r - 1), rows(r), rows(r + 1), *masks)

    inverse, smoothing = {}, {}
    for r in MIDDLE_ROWS:
        mass_sum = joined(direct, 32, r, 0, 8)
        smoothing[r] = joined(spread, 56, r, 0, STATE)
        straight = joined(direct, 32, r, 8, 24)
        carried = joined(spread, 56, r, STATE, 16)
        for g in range(2):
            inverse[r, g] = mass_inverse(mass_sum[g])
            at = 2 * (r - 3) + g
            inverse_ref[8 * at : 8 * at + 8, :] = inverse[r, g]
            middle_ref[STATE * at : STATE * at + STATE, :] = advanced(
                tile(r, g, 0, STATE), straight[g], carried[g], inverse[r, g]
            )

    def coefficients(r, g, k):
        return coefs[coefs_at(r, g) + 8 * k : coefs_at(r, g) + 8 * k + 8, :]

    damped_ref[...] = second_laplacian(MIDDLE_ROWS, smoothing, inverse, coefficients, matrices)


def section_kernel(
    first_far_ref,
    second_far_ref,
    low_ref,
    high_ref,
    lists_ref,
    picks_ref,
    matrices,
    inner_spread,
    inner_direct,
    inner_coefs,
    middle_ref,
    middle_damped,
    middle_inverse,
    whole_ref,
    send_ref,
    outside,
    slopes,
    flux,
    plain,
    outer_coefs,
):
    even = lax.rem(lax.axis_index("curve"), 2) == 0
    outside[0] = jnp.where(even, second_far_ref[...], first_far_ref[...])
    outside[1] = jnp.where(even, first_far_ref[...], second_far_ref[...])

    def tile(r, g, start=0, size=TILE):
        offset = ((r % 2) * 2 + g) * TILE + start
        if r in OUTER_ROWS:
            return outside[r // 6, offset : offset + size, :]
        return (low_ref if r < 4 else high_ref)[offset : offset + size, :]

    outer_spread, outer_direct = local_terms(
        OUTER_ROWS,
        tile,
        matrices,
        slopes,
        flux,
        plain,
        outer_coefs,
        lambda r, g: {1: 24 * g, 6: 48 + 24 * g}.get(r),
    )
    masks = face_masks()
    _, outer_flux_at, outer_plain_at, _ = row_starts(OUTER_ROWS)
    _, inner_flux_at, inner_plain_at, _ = row_starts(OWN_ROWS)

    def joined(spread, r, start, count):
        def rows(k):
            if k in OUTER_ROWS:
                at = (outer_flux_at if spread else outer_plain_at)[k] + start
                return (outer_spread if spread else outer_direct)[at : at + count, :]
            at = (inner_flux_at if spread else inner_plain_at)[k] + start
            return (inner_spread if spread else inner_direct)[at : at + count, :]

        return rows_joined(rows(r - 1), rows(r), rows(r + 1), *masks)

    def coefficients(r, g, k):
        if r in OUTER_ROWS:
            at = (0 if r == 1 else 48) + 24 * g + 8 * k
            return outer_coefs[at : at + 8, :]
        at = (2 * (r - 2) + g) * 24 + 8 * k
        return inner_coefs[at : at + 8, :]

    inverse, smoothing = {}, {}
    for r in EDGE_ROWS:
        mass_sum = joined(False, r, 0, 8)
        smoothing[r] = joined(True, r, 0, STATE)
        for g in range(2):
            inverse[r, g] = mass_inverse(mass_sum[g])
    for r in MIDDLE_ROWS:
        for g in range(2):
            at = 8 * (2 * (r - 3) + g)
            inverse[r, g] = middle_inverse[at : at + 8, :]
    damped = second_laplacian(EDGE_ROWS, smoothing, inverse, coefficients, matrices)

    def damped_row(r):
        if r in MIDDLE_ROWS:
            return middle_damped[(r - 3) * STATE : (r - 2) * STATE, :]
        at = EDGE_ROWS.index(r) * STATE
        return damped[at : at + STATE, :]

    ordered = []
    for r in OWN_ROWS:
        damping = rows_joined(damped_row(r - 1), damped_row(r), damped_row(r + 1), *masks)
        if r not in MIDDLE_ROWS:
            straight = joined(False, r, 8, 24)
            carried = joined(True, r, STATE, 16)
        for g in range(2):
            if r in MIDDLE_ROWS:
                at = STATE * (2 * (r - 3) + g)
                base = middle_ref[at : at + STATE, :]
            else:
                base = advanced(tile(r, g, 0, STATE), straight[g], carried[g], inverse[r, g])
            ordered.append(
                base - ((TIME_STEP * HYPER_NU) * damping[g]) * repeated(inverse[r, g])
            )
    whole = jnp.concatenate(ordered, axis=1)
    whole_ref[...] = whole
    shares = [(lists_ref[k : k + 1, :] > 0.0).astype(F32) for k in range(3)]
    slots = [jnp.broadcast_to(lists_ref[3:4, :] * shares[k], (8, 1024)) for k in range(3)]
    row = row_iota((8, 1024))
    slot_rows = sum(jnp.where(row == k, slots[k], 0.0) for k in range(3))
    columns = jnp.concatenate([whole * share for share in shares] + [slot_rows], axis=0)
    upper, lower = halves(columns)
    sent = dot_last(picks_ref[...], jnp.concatenate([upper, lower], axis=0))
    send_ref[...] = sent[:, :LANES] + sent[:, LANES:]


def restore_kernel(whole_ref, place_ref, updated_ref):
    first, second, third = three_parts(whole_ref[...])
    hits = (row_iota((1024, POINTS_DEV)) == place_ref[0:1, :]).astype(F32).astype(BF16)
    updated_ref[...] = dot(first, hits) + dot(second, hits) + dot(third, hits)


def receive_kernel(received_ref, physics_ref):
    turned_over = received_ref[...].T
    upper, lower = halves(turned_over)
    places = slice(3 * STATE, 3 * STATE + 3)
    slot = turned_over[places, :].astype(jnp.int32) - 1
    both = jnp.concatenate([upper, lower], axis=0)
    count = 2 * LANES
    for start in range(0, POINTS_DEV, count):
        row = row_iota((count, POINTS_DEV)) + start
        hits = (row == slot[0:1]) | (row == slot[1:2]) | (row == slot[2:3])
        rows = dot_last(both, hits.astype(F32).astype(BF16))
        rows = rows[:LANES] + rows[LANES:]
        own = rows[places, :] == (lane_iota((3, count)) + (start + 1)).astype(F32)
        physics_ref[:, start : start + count] = jnp.where(
            own[0:1],
            rows[:STATE],
            jnp.where(own[1:2], rows[STATE : 2 * STATE], rows[2 * STATE : 3 * STATE]),
        )


def call(kernel, shapes, scratch=(), flops=0, moved=0, vmem=VMEM_LIMIT, **specs):
    return pl.pallas_call(
        kernel,
        out_shape=[jax.ShapeDtypeStruct(s, d) for s, d in shapes],
        scratch_shapes=list(scratch),
        **specs,
        compiler_params=pltpu.CompilerParams(vmem_limit_bytes=vmem),
        cost_estimate=pl.CostEstimate(flops=flops, bytes_accessed=moved, transcendentals=0),
    )


def swaps(count, pairs_from):
    route = []
    for i in range(pairs_from, count - 1, 2):
        route += [(i, i + 1), (i + 1, i)]
    return route


def body(
    evolving_state_array, point_id, neighbours, jacobian, inverse_metric, coriolis, column_slot
):
    anywhere = pl.BlockSpec(memory_space=pltpu.HBM)
    half = ((4 * TILE, LANES), F32)
    strip = ((TILE, LANES), F32)
    values_shape = ((TILE + 8, POINTS_DEV), F32)
    far, close, values = call(
        strip_kernel,
        [strip, strip, values_shape],
        scratch=[
            pltpu.VMEM((8, ELEMS_DEV), jnp.int32),
            pltpu.VMEM((POINTS_DEV,), F32),
            pltpu.VMEM((POINTS_DEV,), F32),
            pltpu.VMEM((4, POINTS_DEV), F32),
            pltpu.VMEM((POINTS_DEV,), jnp.int32),
            pltpu.VMEM((FIELDS, LEV, POINTS_DEV), F32),
            pltpu.SemaphoreType.DMA((6,)),
        ],
        in_specs=[anywhere] * 6,
        vmem=64 * 1024 * 1024 - 524288,
    )(evolving_state_array, jacobian, coriolis, inverse_metric, neighbours, column_slot)
    cols, rows = lax.axis_size("col"), lax.axis_size("curve")
    from_far = lax.ppermute(far, "col", swaps(cols, 1) + [(cols - 1, 0), (0, cols - 1)])
    from_close = lax.ppermute(close, "col", swaps(cols, 0))
    low, high, place = call(
        arrange_kernel,
        [half, half, ((8, POINTS_DEV), jnp.int32)],
        flops=400_000_000,
        moved=1_000_000,
    )(values)
    first, second, low, high = call(margin_kernel, [half] * 4)(low, high, from_far, from_close)
    second_far = lax.ppermute(second, "curve", swaps(rows, 1))
    first_far = lax.ppermute(first, "curve", swaps(rows, 0))
    matrices = jnp.asarray(operators())
    def scratch(rows):
        slope_rows, flux_rows, plain_rows = row_starts(rows)[3]
        return [
            pltpu.VMEM((slope_rows, 2 * LANES), F32),
            pltpu.VMEM((flux_rows, 4 * LANES), F32),
            pltpu.VMEM((plain_rows, 2 * LANES), F32),
        ]

    inner = call(
        inner_kernel,
        [
            ((8, 1024), F32),
            ((4 * 56, 2 * LANES), F32),
            ((4 * 32, 2 * LANES), F32),
            ((8 * 24, LANES), F32),
            ((POINTS_DEV, 1024), BF16),
            ((4 * STATE, LANES), F32),
            ((2 * STATE, 2 * LANES), F32),
            ((4 * 8, LANES), F32),
        ],
        scratch=scratch(OWN_ROWS),
        flops=400_000_000,
        moved=1_000_000,
    )(low, high, matrices)
    lists, spread, direct, coefs, picks, middle, middle_damped, middle_inverse = inner
    whole, sent = call(
        section_kernel,
        [((STATE, 1024), F32), ((POINTS_DEV, LANES), F32)],
        scratch=[pltpu.VMEM((2, 4 * TILE, LANES), F32)]
        + scratch(OUTER_ROWS)
        + [pltpu.VMEM((4 * 24, LANES), F32)],
    )(
        first_far,
        second_far,
        low,
        high,
        lists,
        picks,
        matrices,
        spread,
        direct,
        coefs,
        middle,
        middle_damped,
        middle_inverse,
    )
    received = lax.all_to_all(sent, "col", split_axis=0, concat_axis=0, tiled=True)
    (updated,) = call(
        restore_kernel, [((STATE, POINTS_DEV), F32)], flops=400_000_000, moved=1_000_000
    )(whole, place)
    (physics,) = call(receive_kernel, [((STATE, POINTS_DEV), F32)])(received)
    shape = evolving_state_array.shape
    return updated.reshape(shape), physics.reshape(shape)


def solution(mesh):
    split = ("curve", "col")
    return jax.shard_map(
        body,
        mesh=mesh,
        in_specs=(
            P(None, None, split),
            P(split),
            P(None, split),
            P(split),
            P(None, split),
            P(split),
            P(split),
        ),
        out_specs=(P(None, None, split), P(None, None, split)),
        check_vma=False,
    )
```

```python
import functools
import math

import jax
import jax.numpy as jnp
import numpy as np
from jax import lax
from jax.experimental import pallas as pl
from jax.experimental.pallas import tpu as pltpu
from jax.sharding import PartitionSpec as P

FIELDS = 5
LEV = 8
STATE = FIELDS * LEV
TILE = 48
LANES = 128
ELEMS_DEV = 48
POINTS_DEV = 768
N_COL = 32
CAP = 72
CAP_ROWS = CAP // 3
TIME_STEP = 0.1
HYPER_NU = 0.002
F32 = jnp.float32
BF16 = jnp.bfloat16
VMEM_LIMIT = 32 * 1024 * 1024


def gll_tables():
    root_fifth = 1.0 / math.sqrt(5.0)
    nodes = np.array([-1.0, -root_fifth, root_fifth, 1.0])
    weights = np.array([1.0, 5.0, 5.0, 1.0]) / 6.0
    table = np.zeros((4, 4))
    for i in range(4):
        for m in range(4):
            if i == m:
                table[i, m] = sum(1.0 / (nodes[i] - nodes[o]) for o in range(4) if o != i)
            else:
                upper = np.prod([nodes[i] - nodes[o] for o in range(4) if o != i])
                lower = np.prod([nodes[m] - nodes[o] for o in range(4) if o != m])
                table[i, m] = upper / (lower * (nodes[i] - nodes[m]))
    return table, weights


def two_parts(matrix):
    upper = matrix.astype(np.float32).astype(jnp.bfloat16)
    lower = (matrix - upper.astype(np.float64)).astype(np.float32).astype(jnp.bfloat16)
    return upper, lower


@functools.lru_cache(maxsize=None)
def operators():
    table, weights = gll_tables()
    eye4, eye8 = np.eye(4), np.eye(8)
    along_cycle = np.kron(eye4, table.T)
    along_rows = np.kron(table.T, eye4)
    grad = np.concatenate([np.kron(eye8, along_cycle), np.kron(eye8, along_rows)], axis=1)
    weight = np.diag(np.outer(weights, weights).reshape(16))
    div = np.concatenate(
        [np.kron(eye8, along_cycle @ weight), np.kron(eye8, along_rows @ weight)], axis=0
    )
    join = np.eye(256)
    for place in range(15):
        for j in range(4):
            low, high = place * 16 + 4 * j + 3, place * 16 + 16 + 4 * j
            join[low, high] = 1.0
            join[high, low] = 1.0
    both = np.zeros((512, 256))
    both[:256, :128] = div
    both[256:, 128:] = div
    div_join = both @ join
    grad_hi, grad_lo = two_parts(grad)
    div_hi, div_lo = two_parts(div_join)
    return np.concatenate(
        [grad_hi, grad_hi, grad_lo, div_hi, div_lo, join.astype(jnp.bfloat16)], axis=0
    )


def dot(left, right):
    return jnp.dot(left, right, preferred_element_type=F32)


def dot_last(left, right):
    return lax.dot_general(left, right, (((1,), (1,)), ((), ())), preferred_element_type=F32)


def halves(value):
    upper = value.astype(BF16)
    lower = (value - upper.astype(F32)).astype(BF16)
    return upper, lower


def lane_iota(shape):
    return lax.broadcasted_iota(jnp.int32, shape, 1)


def row_iota(shape):
    return lax.broadcasted_iota(jnp.int32, shape, 0)


def one_step(local, index):
    hit = (row_iota((ELEMS_DEV, ELEMS_DEV)) == index) & local
    return hit.astype(F32).astype(BF16)


def wide(local):
    return jnp.broadcast_to(local.astype(F32), (8, ELEMS_DEV))


def chain_length(local, index, doublings):
    length = wide(local)
    step = one_step(local, index)
    for k in range(doublings):
        length = length + dot(length.astype(BF16), step)
        if k + 1 < doublings:
            step = dot(step, step).astype(BF16)
    return length


def local_lists(near):
    base = (lax.axis_index("curve") * N_COL + lax.axis_index("col")) * ELEMS_DEV
    index = near - base
    return index, (index >= 0) & (index < ELEMS_DEV)


def over_points(element_values):
    shape = (ELEMS_DEV, POINTS_DEV)
    spread = (lane_iota(shape) // 16 == row_iota(shape)).astype(F32).astype(BF16)
    return dot(element_values.astype(BF16), spread)[0:1].astype(jnp.int32)


def three_parts(value):
    first = value.astype(BF16)
    rest = value - first.astype(F32)
    second = rest.astype(BF16)
    return first, second, (rest - second.astype(F32)).astype(BF16)


def strip_kernel(
    state_ref, jacobian_ref, coriolis_ref, metric_ref, near_ref, slot_ref, far_ref, close_ref,
    values_ref, near, jac, cor, metric, slot, state, sems
):
    copies = [
        pltpu.make_async_copy(source, target, sems.at[i])
        for i, (source, target) in enumerate(
            [
                (near_ref, near),
                (state_ref, state),
                (jacobian_ref, jac),
                (coriolis_ref, cor),
                (metric_ref, metric),
                (slot_ref, slot),
            ]
        )
    ]
    for copy in copies:
        copy.start()
    copies[0].wait()
    index, local = local_lists(near[...])
    row = chain_length(local[2:3], index[2:3], 2)
    sides = []
    for side in range(2):
        here, there = local[side : side + 1], index[side : side + 1]
        second = dot(wide(here).astype(BF16), one_step(here, there))
        edge = wide(~here)
        sides.append((edge, wide(here) * (1.0 - second)))
    (first, second), (last, second_last) = sides
    unit = (first + second) * (2.0 * row + 1.0 + second)
    unit = unit + (last + second_last) * (2.0 * row + 9.0 + last)
    lane = (over_points(unit) - 1) * 16 + lane_iota((1, POINTS_DEV)) % 16
    hits = (row_iota((2 * LANES, POINTS_DEV)) == lane).astype(F32).astype(BF16)
    for copy in copies[1:]:
        copy.wait()
    values = jnp.concatenate(
        [
            state[...].reshape(STATE, POINTS_DEV),
            jac[...].reshape(1, POINTS_DEV),
            cor[...].reshape(1, POINTS_DEV),
            metric[...],
            slot[...].astype(F32).reshape(1, POINTS_DEV),
            jnp.zeros((1, POINTS_DEV), F32),
        ],
        axis=0,
    )
    values_ref[0:TILE, :] = values
    values_ref[TILE:, 0:ELEMS_DEV] = jnp.where(local, index, -1).astype(F32)
    parts = dot_last(jnp.concatenate(three_parts(values), axis=0), hits)
    strips = parts[0:TILE] + parts[TILE : 2 * TILE] + parts[2 * TILE :]
    even = lax.rem(lax.axis_index("col"), 2) == 0
    to_left, to_right = strips[:, :LANES], strips[:, LANES:]
    far_ref[...] = jnp.where(even, to_left, to_right)
    close_ref[...] = jnp.where(even, to_right, to_left)


def arrange_kernel(values_ref, low_ref, high_ref, place_ref):
    index = values_ref[TILE:, 0:ELEMS_DEV].astype(jnp.int32)
    local = index >= 0
    place = chain_length(local[0:1], index[0:1], 4)
    row = chain_length(local[2:3], index[2:3], 2)
    target = over_points(row * 16.0 + place + 2.0) * 16 + lane_iota((1, POINTS_DEV)) % 16
    place_ref[...] = jnp.broadcast_to(target, (8, POINTS_DEV))
    hits = (row_iota((1024, POINTS_DEV)) == target).astype(F32).astype(BF16)
    parts = dot_last(jnp.concatenate(three_parts(values_ref[0:TILE, :]), axis=0), hits)
    ordered = parts[0:TILE] + parts[TILE : 2 * TILE] + parts[2 * TILE :]
    for r in range(4):
        for g in range(2):
            block = ordered[:, (2 * r + g) * LANES : (2 * r + g + 1) * LANES]
            ref = low_ref if r < 2 else high_ref
            start = ((r % 2) * 2 + g) * TILE
            ref[start : start + TILE, :] = block


def turned(block, by):
    by = by % LANES
    return block if by == 0 else pltpu.roll(block, by, 1)


def margin_kernel(
    low_in, high_in, from_far, from_close, first_ref, second_ref, low_ref, high_ref
):
    lane = lane_iota((TILE, LANES))
    even = lax.rem(lax.axis_index("col"), 2) == 0
    from_left = jnp.where(even, from_far[...], from_close[...])
    from_right = jnp.where(even, from_close[...], from_far[...])
    halves_of_rows = []
    for source, start_row in ((low_in, 0), (high_in, 2)):
        blocks = []
        for r in range(2):
            turn = start_row + r
            start = r * 2 * TILE
            blocks.append(
                jnp.where(lane < 32, turned(from_left, -32 * turn), source[start : start + TILE, :])
            )
            start += TILE
            blocks.append(
                jnp.where(
                    lane >= 96, turned(from_right, 96 - 32 * turn), source[start : start + TILE, :]
                )
            )
        halves_of_rows.append(jnp.concatenate(blocks, axis=0))
    low, high = halves_of_rows
    low_ref[...] = low
    high_ref[...] = high
    even = lax.rem(lax.axis_index("curve"), 2) == 0
    first_ref[...] = jnp.where(even, high, low)
    second_ref[...] = jnp.where(even, low, high)


def send_lists(slots):
    square = (LANES, LANES)
    upto = (row_iota(square) <= lane_iota(square)).astype(F32)
    count = jnp.concatenate([upto, jnp.ones(square, F32)], axis=1).astype(BF16)
    lane = lane_iota((1, LANES))
    chosen, devices, withins, owns = [], [], [], []
    for i, slot in enumerate(slots):
        own = lane >= 32 if i % 2 == 0 else lane < 96
        device = jnp.where(own, jnp.floor((slot + 0.5) * (1.0 / POINTS_DEV)), -1.0)
        wanted = jnp.broadcast_to(device.astype(jnp.int32), (N_COL, LANES))
        chosen.append((wanted == row_iota((N_COL, LANES))).astype(F32))
        devices.append(device)
        withins.append(slot - device * POINTS_DEV)
        owns.append(own)
    counted = dot(jnp.concatenate(chosen, axis=0).astype(BF16), count)
    before = jnp.zeros((N_COL, LANES), F32)
    lists = []
    for i, (device, within, own) in enumerate(zip(devices, withins, owns)):
        rows = counted[i * N_COL : (i + 1) * N_COL]
        rank = jnp.sum((rows[:, :LANES] + before) * chosen[i], axis=0, keepdims=True) - 1.0
        before = before + rows[:, LANES:]
        third = (rank >= CAP_ROWS).astype(F32) + (rank >= 2 * CAP_ROWS).astype(F32)
        line = device * CAP_ROWS + rank - third * CAP_ROWS
        parts = [jnp.where(own & (third == float(k)), line + 1.0, 0.0) for k in range(3)]
        filler = jnp.zeros((4, LANES), F32)
        lists.append(
            jnp.concatenate(parts + [jnp.where(own, within + 1.0, 0.0), filler], axis=0)
        )
    return jnp.concatenate(lists, axis=1)


def fluxes(slope, coefficients):
    along_cycle, along_rows = slope[:, :LANES], slope[:, LANES:]
    caa, cab, cbb = coefficients
    return caa * along_cycle + cab * along_rows, cab * along_cycle + cbb * along_rows


def gradient(values, matrices):
    upper, lower = halves(values)
    return dot(jnp.concatenate([upper, lower], axis=1), matrices[0:256, :]) + dot(
        upper, matrices[256:384, :]
    )


def divergence_joined(values, matrices):
    upper, lower = halves(values)
    first = matrices[384:896, :]
    return dot(upper, first) + dot(lower, first) + dot(upper, matrices[896:1408, :])


def rows_joined(below, here, above, low_mask, high_mask):
    parts = []
    for g in range(2):
        part = slice(g * LANES, (g + 1) * LANES)
        parts.append(
            here[:, part]
            + low_mask * turned(below[:, part], -12)
            + high_mask * turned(above[:, part], 12)
        )
    return parts


def row_starts(rows):
    slope, flux, plain = {}, {}, {}
    at = [0, 0, 0]
    for r in rows:
        lean = r in (0, 7)
        for g in range(2):
            slope[r, g] = at[0]
            at[0] += STATE if lean else TILE
        flux[r] = at[1]
        at[1] += STATE if lean else STATE + 16
        plain[r] = at[2]
        at[2] += 8 if lean else 32
    return slope, flux, plain, at


def local_terms(rows, tile, matrices, slopes, flux, plain, coefs, coefs_at):
    slope_at, flux_at, plain_at, _ = row_starts(rows)
    cells = [(r, g) for r in rows for g in range(2)]
    stacked = []
    for r, g in cells:
        stacked.append(tile(r, g, 0, STATE))
        if r not in (0, 7):
            zonal, meridional = tile(r, g, 0, 8), tile(r, g, 8, 8)
            energy = 0.5 * (zonal * zonal + meridional * meridional) + tile(r, g, 16, 8)
            stacked.append(energy)
    slopes[...] = gradient(jnp.concatenate(stacked, axis=0), matrices)
    lane = lane_iota((8, LANES))
    inner_i = (lane % 4 == 1) | (lane % 4 == 2)
    inner_j = (lane // 4 % 4 == 1) | (lane // 4 % 4 == 2)
    weight = jnp.where(inner_i, 5.0 / 6.0, 1.0 / 6.0) * jnp.where(inner_j, 5.0 / 6.0, 1.0 / 6.0)
    for r, g in cells:

        def line(k):
            return jnp.broadcast_to(tile(r, g, STATE + k, 1), (8, LANES))

        jacobian, coriolis = line(0), line(1)
        m11, m12, m21, m22 = 1.0 + line(2), line(3), line(4), 1.0 + line(5)
        caa = jacobian * (m11 * m11 + m12 * m12)
        cab = jacobian * (m11 * m21 + m12 * m22)
        cbb = jacobian * (m21 * m21 + m22 * m22)
        at = coefs_at(r, g)
        if at is not None:
            coefs[at : at + 8, :] = caa
            coefs[at + 8 : at + 16, :] = cab
            coefs[at + 16 : at + 24, :] = cbb
        mass = jacobian * weight
        at = slope_at[r, g]
        first = slice(g * 2 * LANES, (g * 2 + 1) * LANES)
        second = slice((g * 2 + 1) * LANES, (g * 2 + 2) * LANES)
        part = slice(g * LANES, (g + 1) * LANES)
        to, direct = flux_at[r], plain_at[r]
        for f in range(FIELDS):
            one, two = fluxes(slopes[at + 8 * f : at + 8 * f + 8, :], (caa, cab, cbb))
            flux[to + 8 * f : to + 8 * f + 8, first] = one
            flux[to + 8 * f : to + 8 * f + 8, second] = two
        plain[direct : direct + 8, part] = mass
        if r in (0, 7):
            continue
        zonal, meridional = tile(r, g, 0, 8), tile(r, g, 8, 8)
        flow1 = jacobian * (m11 * zonal + m12 * meridional)
        flow2 = jacobian * (m21 * zonal + m22 * meridional)
        for k in range(2):
            carried = tile(r, g, 24 + 8 * k, 8)
            flux[to + 40 + 8 * k : to + 48 + 8 * k, first] = carried * flow1
            flux[to + 40 + 8 * k : to + 48 + 8 * k, second] = carried * flow2
        ea, eb = slopes[at + 40 : at + 48, :LANES], slopes[at + 40 : at + 48, LANES:]
        ta, tb = slopes[at + 16 : at + 24, :LANES], slopes[at + 16 : at + 24, LANES:]
        plain[direct + 8 : direct + 16, part] = mass * (
            coriolis * meridional - (m11 * ea + m21 * eb)
        )
        plain[direct + 16 : direct + 24, part] = -mass * (
            coriolis * zonal + (m12 * ea + m22 * eb)
        )
        plain[direct + 24 : direct + 32, part] = -mass * (
            zonal * (m11 * ta + m21 * tb) + meridional * (m12 * ta + m22 * tb)
        )
    spread = divergence_joined(flux[...], matrices)
    upper, lower = halves(plain[...])
    join = matrices[1408:1664, :]
    return spread, dot(upper, join) + dot(lower, join)


def face_masks():
    lane = lane_iota((1, LANES)) % 16
    return (lane < 4).astype(F32), (lane >= 12).astype(F32)


def repeated(block):
    return jnp.concatenate([block] * FIELDS, axis=0)


def second_laplacian(rows, smoothing, inverse, coefficients, matrices):
    smooth = [smoothing[r][g] * repeated(inverse[r, g]) for r in rows for g in range(2)]
    again = gradient(jnp.concatenate(smooth, axis=0), matrices)
    flat = []
    for n, r in enumerate(rows):
        parts = []
        for g in range(2):
            triple = tuple(repeated(coefficients(r, g, k)) for k in range(3))
            start = (2 * n + g) * STATE
            parts += list(fluxes(again[start : start + STATE, :], triple))
        flat.append(jnp.concatenate(parts, axis=1))
    return divergence_joined(jnp.concatenate(flat, axis=0), matrices)


def mass_inverse(mass_sum):
    return 1.0 / jnp.where(mass_sum > 0.0, mass_sum, 1.0)


def advanced(state, straight, carried, inverse):
    return state + (TIME_STEP * jnp.concatenate([straight, -carried], axis=0)) * repeated(inverse)


OWN_ROWS = (2, 3, 4, 5)
OUTER_ROWS = (0, 1, 6, 7)
MIDDLE_ROWS = (3, 4)
EDGE_ROWS = (1, 2, 5, 6)


def inner_kernel(
    low_ref,
    high_ref,
    matrices,
    lists_ref,
    spread_ref,
    direct_ref,
    coefs,
    picks_ref,
    middle_ref,
    damped_ref,
    inverse_ref,
    slopes,
    flux,
    plain,
):
    def tile(r, g, start=0, size=TILE):
        offset = ((r % 2) * 2 + g) * TILE + start
        return (low_ref if r < 4 else high_ref)[offset : offset + size, :]

    def coefs_at(r, g):
        return (2 * (r - 2) + g) * 24

    lists = send_lists([tile(r, g, STATE + 6, 1) for r in OWN_ROWS for g in range(2)])
    lists_ref[...] = lists
    line = (lists[0:1] + lists[1:2] + lists[2:3]).astype(jnp.int32) - 1
    picks_ref[...] = (row_iota((POINTS_DEV, 1024)) == line).astype(F32).astype(BF16)
    spread, direct = local_terms(
        OWN_ROWS, tile, matrices, slopes, flux, plain, coefs, coefs_at
    )
    spread_ref[...] = spread
    direct_ref[...] = direct
    masks = face_masks()

    def joined(value, size, r, start, count):
        def rows(k):
            at = (k - 2) * size + start
            return value[at : at + count, :]

        return rows_joined(rows(r - 1), rows(r), rows(r + 1), *masks)

    inverse, smoothing = {}, {}
    for r in MIDDLE_ROWS:
        mass_sum = joined(direct, 32, r, 0, 8)
        smoothing[r] = joined(spread, 56, r, 0, STATE)
        straight = joined(direct, 32, r, 8, 24)
        carried = joined(spread, 56, r, STATE, 16)
        for g in range(2):
            inverse[r, g] = mass_inverse(mass_sum[g])
            at = 2 * (r - 3) + g
            inverse_ref[8 * at : 8 * at + 8, :] = inverse[r, g]
            middle_ref[STATE * at : STATE * at + STATE, :] = advanced(
                tile(r, g, 0, STATE), straight[g], carried[g], inverse[r, g]
            )

    def coefficients(r, g, k):
        return coefs[coefs_at(r, g) + 8 * k : coefs_at(r, g) + 8 * k + 8, :]

    damped_ref[...] = second_laplacian(MIDDLE_ROWS, smoothing, inverse, coefficients, matrices)


def section_kernel(
    first_far_ref,
    second_far_ref,
    low_ref,
    high_ref,
    lists_ref,
    picks_ref,
    matrices,
    inner_spread,
    inner_direct,
    inner_coefs,
    middle_ref,
    middle_damped,
    middle_inverse,
    whole_ref,
    send_ref,
    outside,
    slopes,
    flux,
    plain,
    outer_coefs,
):
    even = lax.rem(lax.axis_index("curve"), 2) == 0
    outside[0] = jnp.where(even, second_far_ref[...], first_far_ref[...])
    outside[1] = jnp.where(even, first_far_ref[...], second_far_ref[...])

    def tile(r, g, start=0, size=TILE):
        offset = ((r % 2) * 2 + g) * TILE + start
        if r in OUTER_ROWS:
            return outside[r // 6, offset : offset + size, :]
        return (low_ref if r < 4 else high_ref)[offset : offset + size, :]

    outer_spread, outer_direct = local_terms(
        OUTER_ROWS,
        tile,
        matrices,
        slopes,
        flux,
        plain,
        outer_coefs,
        lambda r, g: {1: 24 * g, 6: 48 + 24 * g}.get(r),
    )
    masks = face_masks()
    _, outer_flux_at, outer_plain_at, _ = row_starts(OUTER_ROWS)
    _, inner_flux_at, inner_plain_at, _ = row_starts(OWN_ROWS)

    def joined(spread, r, start, count):
        def rows(k):
            if k in OUTER_ROWS:
                at = (outer_flux_at if spread else outer_plain_at)[k] + start
                return (outer_spread if spread else outer_direct)[at : at + count, :]
            at = (inner_flux_at if spread else inner_plain_at)[k] + start
            return (inner_spread if spread else inner_direct)[at : at + count, :]

        return rows_joined(rows(r - 1), rows(r), rows(r + 1), *masks)

    def coefficients(r, g, k):
        if r in OUTER_ROWS:
            at = (0 if r == 1 else 48) + 24 * g + 8 * k
            return outer_coefs[at : at + 8, :]
        at = (2 * (r - 2) + g) * 24 + 8 * k
        return inner_coefs[at : at + 8, :]

    inverse, smoothing = {}, {}
    for r in EDGE_ROWS:
        mass_sum = joined(False, r, 0, 8)
        smoothing[r] = joined(True, r, 0, STATE)
        for g in range(2):
            inverse[r, g] = mass_inverse(mass_sum[g])
    for r in MIDDLE_ROWS:
        for g in range(2):
            at = 8 * (2 * (r - 3) + g)
            inverse[r, g] = middle_inverse[at : at + 8, :]
    damped = second_laplacian(EDGE_ROWS, smoothing, inverse, coefficients, matrices)

    def damped_row(r):
        if r in MIDDLE_ROWS:
            return middle_damped[(r - 3) * STATE : (r - 2) * STATE, :]
        at = EDGE_ROWS.index(r) * STATE
        return damped[at : at + STATE, :]

    ordered = []
    for r in OWN_ROWS:
        damping = rows_joined(damped_row(r - 1), damped_row(r), damped_row(r + 1), *masks)
        if r not in MIDDLE_ROWS:
            straight = joined(False, r, 8, 24)
            carried = joined(True, r, STATE, 16)
        for g in range(2):
            if r in MIDDLE_ROWS:
                at = STATE * (2 * (r - 3) + g)
                base = middle_ref[at : at + STATE, :]
            else:
                base = advanced(tile(r, g, 0, STATE), straight[g], carried[g], inverse[r, g])
            ordered.append(
                base - ((TIME_STEP * HYPER_NU) * damping[g]) * repeated(inverse[r, g])
            )
    whole = jnp.concatenate(ordered, axis=1)
    whole_ref[...] = whole
    shares = [(lists_ref[k : k + 1, :] > 0.0).astype(F32) for k in range(3)]
    slots = [jnp.broadcast_to(lists_ref[3:4, :] * shares[k], (8, 1024)) for k in range(3)]
    row = row_iota((8, 1024))
    slot_rows = sum(jnp.where(row == k, slots[k], 0.0) for k in range(3))
    columns = jnp.concatenate([whole * share for share in shares] + [slot_rows], axis=0)
    upper, lower = halves(columns)
    sent = dot_last(picks_ref[...], jnp.concatenate([upper, lower], axis=0))
    send_ref[...] = sent[:, :LANES] + sent[:, LANES:]


def restore_kernel(whole_ref, place_ref, updated_ref):
    first, second, third = three_parts(whole_ref[...])
    hits = (row_iota((1024, POINTS_DEV)) == place_ref[0:1, :]).astype(F32).astype(BF16)
    updated_ref[...] = dot(first, hits) + dot(second, hits) + dot(third, hits)


def receive_kernel(received_ref, physics_ref):
    turned_over = received_ref[...].T
    upper, lower = halves(turned_over)
    places = slice(3 * STATE, 3 * STATE + 3)
    slot = turned_over[places, :].astype(jnp.int32) - 1
    both = jnp.concatenate([upper, lower], axis=0)
    count = 2 * LANES
    for start in range(0, POINTS_DEV, count):
        row = row_iota((count, POINTS_DEV)) + start
        hits = (row == slot[0:1]) | (row == slot[1:2]) | (row == slot[2:3])
        rows = dot_last(both, hits.astype(F32).astype(BF16))
        rows = rows[:LANES] + rows[LANES:]
        own = rows[places, :] == (lane_iota((3, count)) + (start + 1)).astype(F32)
        physics_ref[:, start : start + count] = jnp.where(
            own[0:1],
            rows[:STATE],
            jnp.where(own[1:2], rows[STATE : 2 * STATE], rows[2 * STATE : 3 * STATE]),
        )


def call(kernel, shapes, scratch=(), flops=0, moved=0, vmem=VMEM_LIMIT, **specs):
    return pl.pallas_call(
        kernel,
        out_shape=[
            jax.ShapeDtypeStruct(*s) if isinstance(s, tuple) else s for s in shapes
        ],
        scratch_shapes=list(scratch),
        **specs,
        compiler_params=pltpu.CompilerParams(vmem_limit_bytes=vmem),
        cost_estimate=pl.CostEstimate(flops=flops, bytes_accessed=moved, transcendentals=0),
    )


def swaps(count, pairs_from):
    route = []
    for i in range(pairs_from, count - 1, 2):
        route += [(i, i + 1), (i + 1, i)]
    return route


def body(
    evolving_state_array, point_id, neighbours, jacobian, inverse_metric, coriolis, column_slot
):
    anywhere = pl.BlockSpec(memory_space=pltpu.HBM)
    half = ((4 * TILE, LANES), F32)
    strip = ((TILE, LANES), F32)
    values_shape = ((TILE + 8, POINTS_DEV), F32)
    far, close, values = call(
        strip_kernel,
        [pltpu.VMEM(*strip), pltpu.VMEM(*strip), pltpu.VMEM(*values_shape)],
        scratch=[
            pltpu.VMEM((8, ELEMS_DEV), jnp.int32),
            pltpu.VMEM((POINTS_DEV,), F32),
            pltpu.VMEM((POINTS_DEV,), F32),
            pltpu.VMEM((4, POINTS_DEV), F32),
            pltpu.VMEM((POINTS_DEV,), jnp.int32),
            pltpu.VMEM((FIELDS, LEV, POINTS_DEV), F32),
            pltpu.SemaphoreType.DMA((6,)),
        ],
        in_specs=[anywhere] * 6,
        vmem=64 * 1024 * 1024 - 524288,
    )(evolving_state_array, jacobian, coriolis, inverse_metric, neighbours, column_slot)
    cols, rows = lax.axis_size("col"), lax.axis_size("curve")
    from_far = lax.ppermute(far, "col", swaps(cols, 1) + [(cols - 1, 0), (0, cols - 1)])
    from_close = lax.ppermute(close, "col", swaps(cols, 0))
    low, high, place = call(
        arrange_kernel,
        [half, half, ((8, POINTS_DEV), jnp.int32)],
        flops=400_000_000,
        moved=1_000_000,
    )(values)
    first, second, low, high = call(margin_kernel, [half] * 4)(low, high, from_far, from_close)
    second_far = lax.ppermute(second, "curve", swaps(rows, 1))
    first_far = lax.ppermute(first, "curve", swaps(rows, 0))
    matrices = jnp.asarray(operators())
    def scratch(rows):
        slope_rows, flux_rows, plain_rows = row_starts(rows)[3]
        return [
            pltpu.VMEM((slope_rows, 2 * LANES), F32),
            pltpu.VMEM((flux_rows, 4 * LANES), F32),
            pltpu.VMEM((plain_rows, 2 * LANES), F32),
        ]

    inner = call(
        inner_kernel,
        [
            ((8, 1024), F32),
            ((4 * 56, 2 * LANES), F32),
            ((4 * 32, 2 * LANES), F32),
            ((8 * 24, LANES), F32),
            ((POINTS_DEV, 1024), BF16),
            ((4 * STATE, LANES), F32),
            ((2 * STATE, 2 * LANES), F32),
            ((4 * 8, LANES), F32),
        ],
        scratch=scratch(OWN_ROWS),
        flops=400_000_000,
        moved=1_000_000,
    )(low, high, matrices)
    lists, spread, direct, coefs, picks, middle, middle_damped, middle_inverse = inner
    whole, sent = call(
        section_kernel,
        [((STATE, 1024), F32), ((POINTS_DEV, LANES), F32)],
        scratch=[pltpu.VMEM((2, 4 * TILE, LANES), F32)]
        + scratch(OUTER_ROWS)
        + [pltpu.VMEM((4 * 24, LANES), F32)],
    )(
        first_far,
        second_far,
        low,
        high,
        lists,
        picks,
        matrices,
        spread,
        direct,
        coefs,
        middle,
        middle_damped,
        middle_inverse,
    )
    received = lax.all_to_all(sent, "col", split_axis=0, concat_axis=0, tiled=True)
    (updated,) = call(
        restore_kernel, [((STATE, POINTS_DEV), F32)], flops=400_000_000, moved=1_000_000
    )(whole, place)
    (physics,) = call(receive_kernel, [((STATE, POINTS_DEV), F32)])(received)
    shape = evolving_state_array.shape
    return updated.reshape(shape), physics.reshape(shape)


def solution(mesh):
    split = ("curve", "col")
    return jax.shard_map(
        body,
        mesh=mesh,
        in_specs=(
            P(None, None, split),
            P(split),
            P(None, split),
            P(split),
            P(None, split),
            P(split),
            P(split),
        ),
        out_specs=(P(None, None, split), P(None, None, split)),
        check_vma=False,
    )
```

```python
import functools
import math

import jax
import jax.numpy as jnp
import numpy as np
from jax import lax
from jax.experimental import pallas as pl
from jax.experimental.pallas import tpu as pltpu
from jax.sharding import PartitionSpec as P

FIELDS = 5
LEV = 8
STATE = FIELDS * LEV
TILE = 48
LANES = 128
ELEMS_DEV = 48
POINTS_DEV = 768
N_COL = 32
CAP = 72
CAP_ROWS = CAP // 3
TIME_STEP = 0.1
HYPER_NU = 0.002
F32 = jnp.float32
BF16 = jnp.bfloat16
VMEM_LIMIT = 32 * 1024 * 1024


def gll_tables():
    root_fifth = 1.0 / math.sqrt(5.0)
    nodes = np.array([-1.0, -root_fifth, root_fifth, 1.0])
    weights = np.array([1.0, 5.0, 5.0, 1.0]) / 6.0
    table = np.zeros((4, 4))
    for i in range(4):
        for m in range(4):
            if i == m:
                table[i, m] = sum(1.0 / (nodes[i] - nodes[o]) for o in range(4) if o != i)
            else:
                upper = np.prod([nodes[i] - nodes[o] for o in range(4) if o != i])
                lower = np.prod([nodes[m] - nodes[o] for o in range(4) if o != m])
                table[i, m] = upper / (lower * (nodes[i] - nodes[m]))
    return table, weights


def two_parts(matrix):
    upper = matrix.astype(np.float32).astype(jnp.bfloat16)
    lower = (matrix - upper.astype(np.float64)).astype(np.float32).astype(jnp.bfloat16)
    return upper, lower


@functools.lru_cache(maxsize=None)
def operators():
    table, weights = gll_tables()
    eye4, eye8 = np.eye(4), np.eye(8)
    along_cycle = np.kron(eye4, table.T)
    along_rows = np.kron(table.T, eye4)
    grad = np.concatenate([np.kron(eye8, along_cycle), np.kron(eye8, along_rows)], axis=1)
    weight = np.diag(np.outer(weights, weights).reshape(16))
    div = np.concatenate(
        [np.kron(eye8, along_cycle @ weight), np.kron(eye8, along_rows @ weight)], axis=0
    )
    join = np.eye(256)
    for place in range(15):
        for j in range(4):
            low, high = place * 16 + 4 * j + 3, place * 16 + 16 + 4 * j
            join[low, high] = 1.0
            join[high, low] = 1.0
    both = np.zeros((512, 256))
    both[:256, :128] = div
    both[256:, 128:] = div
    div_join = both @ join
    grad_hi, grad_lo = two_parts(grad)
    div_hi, div_lo = two_parts(div_join)
    return np.concatenate(
        [grad_hi, grad_hi, grad_lo, div_hi, div_lo, join.astype(jnp.bfloat16)], axis=0
    )


def dot(left, right):
    return jnp.dot(left, right, preferred_element_type=F32)


def dot_last(left, right):
    return lax.dot_general(left, right, (((1,), (1,)), ((), ())), preferred_element_type=F32)


def halves(value):
    upper = value.astype(BF16)
    lower = (value - upper.astype(F32)).astype(BF16)
    return upper, lower


def lane_iota(shape):
    return lax.broadcasted_iota(jnp.int32, shape, 1)


def row_iota(shape):
    return lax.broadcasted_iota(jnp.int32, shape, 0)


def one_step(local, index):
    hit = (row_iota((ELEMS_DEV, ELEMS_DEV)) == index) & local
    return hit.astype(F32).astype(BF16)


def wide(local):
    return jnp.broadcast_to(local.astype(F32), (8, ELEMS_DEV))


def chain_length(local, index, doublings):
    length = wide(local)
    step = one_step(local, index)
    for k in range(doublings):
        length = length + dot(length.astype(BF16), step)
        if k + 1 < doublings:
            step = dot(step, step).astype(BF16)
    return length


def local_lists(near):
    base = (lax.axis_index("curve") * N_COL + lax.axis_index("col")) * ELEMS_DEV
    index = near - base
    return index, (index >= 0) & (index < ELEMS_DEV)


def over_points(element_values):
    shape = (ELEMS_DEV, POINTS_DEV)
    spread = (lane_iota(shape) // 16 == row_iota(shape)).astype(F32).astype(BF16)
    return dot(element_values.astype(BF16), spread)[0:1].astype(jnp.int32)


def three_parts(value):
    first = value.astype(BF16)
    rest = value - first.astype(F32)
    second = rest.astype(BF16)
    return first, second, (rest - second.astype(F32)).astype(BF16)


def strip_kernel(
    state_ref, jacobian_ref, coriolis_ref, metric_ref, near_ref, slot_ref, far_ref, close_ref,
    values_ref, near, jac, cor, metric, slot, state, sems
):
    copies = [
        pltpu.make_async_copy(source, target, sems.at[i])
        for i, (source, target) in enumerate(
            [
                (near_ref, near),
                (state_ref, state),
                (jacobian_ref, jac),
                (coriolis_ref, cor),
                (metric_ref, metric),
                (slot_ref, slot),
            ]
        )
    ]
    for copy in copies:
        copy.start()
    copies[0].wait()
    index, local = local_lists(near[...])
    row = chain_length(local[2:3], index[2:3], 2)
    sides = []
    for side in range(2):
        here, there = local[side : side + 1], index[side : side + 1]
        second = dot(wide(here).astype(BF16), one_step(here, there))
        edge = wide(~here)
        sides.append((edge, wide(here) * (1.0 - second)))
    (first, second), (last, second_last) = sides
    unit = (first + second) * (2.0 * row + 1.0 + second)
    unit = unit + (last + second_last) * (2.0 * row + 9.0 + last)
    lane = (over_points(unit) - 1) * 16 + lane_iota((1, POINTS_DEV)) % 16
    hits = (row_iota((2 * LANES, POINTS_DEV)) == lane).astype(F32).astype(BF16)
    for copy in copies[1:]:
        copy.wait()
    values = jnp.concatenate(
        [
            state[...].reshape(STATE, POINTS_DEV),
            jac[...].reshape(1, POINTS_DEV),
            cor[...].reshape(1, POINTS_DEV),
            metric[...],
            slot[...].astype(F32).reshape(1, POINTS_DEV),
            jnp.zeros((1, POINTS_DEV), F32),
        ],
        axis=0,
    )
    values_ref[0:TILE, :] = values
    values_ref[TILE:, 0:ELEMS_DEV] = jnp.where(local, index, -1).astype(F32)
    parts = dot_last(jnp.concatenate(three_parts(values), axis=0), hits)
    strips = parts[0:TILE] + parts[TILE : 2 * TILE] + parts[2 * TILE :]
    even = lax.rem(lax.axis_index("col"), 2) == 0
    to_left, to_right = strips[:, :LANES], strips[:, LANES:]
    far_ref[...] = jnp.where(even, to_left, to_right)
    close_ref[...] = jnp.where(even, to_right, to_left)


def arrange_kernel(values_ref, low_ref, high_ref, hits_ref):
    index = values_ref[TILE:, 0:ELEMS_DEV].astype(jnp.int32)
    local = index >= 0
    place = chain_length(local[0:1], index[0:1], 4)
    row = chain_length(local[2:3], index[2:3], 2)
    target = over_points(row * 16.0 + place + 2.0) * 16 + lane_iota((1, POINTS_DEV)) % 16
    hits = (row_iota((1024, POINTS_DEV)) == target).astype(F32).astype(BF16)
    hits_ref[...] = hits
    parts = dot_last(jnp.concatenate(three_parts(values_ref[0:TILE, :]), axis=0), hits)
    ordered = parts[0:TILE] + parts[TILE : 2 * TILE] + parts[2 * TILE :]
    for r in range(4):
        for g in range(2):
            block = ordered[:, (2 * r + g) * LANES : (2 * r + g + 1) * LANES]
            ref = low_ref if r < 2 else high_ref
            start = ((r % 2) * 2 + g) * TILE
            ref[start : start + TILE, :] = block


def turned(block, by):
    by = by % LANES
    return block if by == 0 else pltpu.roll(block, by, 1)


def margin_kernel(
    low_in, high_in, from_far, from_close, first_ref, second_ref, low_ref, high_ref
):
    lane = lane_iota((TILE, LANES))
    even = lax.rem(lax.axis_index("col"), 2) == 0
    from_left = jnp.where(even, from_far[...], from_close[...])
    from_right = jnp.where(even, from_close[...], from_far[...])
    halves_of_rows = []
    for source, start_row in ((low_in, 0), (high_in, 2)):
        blocks = []
        for r in range(2):
            turn = start_row + r
            start = r * 2 * TILE
            blocks.append(
                jnp.where(lane < 32, turned(from_left, -32 * turn), source[start : start + TILE, :])
            )
            start += TILE
            blocks.append(
                jnp.where(
                    lane >= 96, turned(from_right, 96 - 32 * turn), source[start : start + TILE, :]
                )
            )
        halves_of_rows.append(jnp.concatenate(blocks, axis=0))
    low, high = halves_of_rows
    low_ref[...] = low
    high_ref[...] = high
    even = lax.rem(lax.axis_index("curve"), 2) == 0
    first_ref[...] = jnp.where(even, high, low)
    second_ref[...] = jnp.where(even, low, high)


def send_lists(slots):
    square = (LANES, LANES)
    upto = (row_iota(square) <= lane_iota(square)).astype(F32)
    count = jnp.concatenate([upto, jnp.ones(square, F32)], axis=1).astype(BF16)
    lane = lane_iota((1, LANES))
    chosen, devices, withins, owns = [], [], [], []
    for i, slot in enumerate(slots):
        own = lane >= 32 if i % 2 == 0 else lane < 96
        device = jnp.where(own, jnp.floor((slot + 0.5) * (1.0 / POINTS_DEV)), -1.0)
        wanted = jnp.broadcast_to(device.astype(jnp.int32), (N_COL, LANES))
        chosen.append((wanted == row_iota((N_COL, LANES))).astype(F32))
        devices.append(device)
        withins.append(slot - device * POINTS_DEV)
        owns.append(own)
    counted = dot(jnp.concatenate(chosen, axis=0).astype(BF16), count)
    before = jnp.zeros((N_COL, LANES), F32)
    lists = []
    for i, (device, within, own) in enumerate(zip(devices, withins, owns)):
        rows = counted[i * N_COL : (i + 1) * N_COL]
        rank = jnp.sum((rows[:, :LANES] + before) * chosen[i], axis=0, keepdims=True) - 1.0
        before = before + rows[:, LANES:]
        third = (rank >= CAP_ROWS).astype(F32) + (rank >= 2 * CAP_ROWS).astype(F32)
        line = device * CAP_ROWS + rank - third * CAP_ROWS
        parts = [jnp.where(own & (third == float(k)), line + 1.0, 0.0) for k in range(3)]
        filler = jnp.zeros((4, LANES), F32)
        lists.append(
            jnp.concatenate(parts + [jnp.where(own, within + 1.0, 0.0), filler], axis=0)
        )
    return jnp.concatenate(lists, axis=1)


def fluxes(slope, coefficients):
    along_cycle, along_rows = slope[:, :LANES], slope[:, LANES:]
    caa, cab, cbb = coefficients
    return caa * along_cycle + cab * along_rows, cab * along_cycle + cbb * along_rows


def gradient(values, matrices):
    upper, lower = halves(values)
    return dot(jnp.concatenate([upper, lower], axis=1), matrices[0:256, :]) + dot(
        upper, matrices[256:384, :]
    )


def divergence_joined(values, matrices):
    upper, lower = halves(values)
    first = matrices[384:896, :]
    return dot(upper, first) + dot(lower, first) + dot(upper, matrices[896:1408, :])


def rows_joined(below, here, above, low_mask, high_mask):
    parts = []
    for g in range(2):
        part = slice(g * LANES, (g + 1) * LANES)
        parts.append(
            here[:, part]
            + low_mask * turned(below[:, part], -12)
            + high_mask * turned(above[:, part], 12)
        )
    return parts


def row_starts(rows):
    slope, flux, plain = {}, {}, {}
    at = [0, 0, 0]
    for r in rows:
        lean = r in (0, 7)
        for g in range(2):
            slope[r, g] = at[0]
            at[0] += STATE if lean else TILE
        flux[r] = at[1]
        at[1] += STATE if lean else STATE + 16
        plain[r] = at[2]
        at[2] += 8 if lean else 32
    return slope, flux, plain, at


def local_terms(rows, tile, matrices, slopes, flux, plain, coefs, coefs_at):
    slope_at, flux_at, plain_at, _ = row_starts(rows)
    cells = [(r, g) for r in rows for g in range(2)]
    stacked = []
    for r, g in cells:
        stacked.append(tile(r, g, 0, STATE))
        if r not in (0, 7):
            zonal, meridional = tile(r, g, 0, 8), tile(r, g, 8, 8)
            energy = 0.5 * (zonal * zonal + meridional * meridional) + tile(r, g, 16, 8)
            stacked.append(energy)
    slopes[...] = gradient(jnp.concatenate(stacked, axis=0), matrices)
    lane = lane_iota((8, LANES))
    inner_i = (lane % 4 == 1) | (lane % 4 == 2)
    inner_j = (lane // 4 % 4 == 1) | (lane // 4 % 4 == 2)
    weight = jnp.where(inner_i, 5.0 / 6.0, 1.0 / 6.0) * jnp.where(inner_j, 5.0 / 6.0, 1.0 / 6.0)
    for r, g in cells:

        def line(k):
            return jnp.broadcast_to(tile(r, g, STATE + k, 1), (8, LANES))

        jacobian, coriolis = line(0), line(1)
        m11, m12, m21, m22 = 1.0 + line(2), line(3), line(4), 1.0 + line(5)
        caa = jacobian * (m11 * m11 + m12 * m12)
        cab = jacobian * (m11 * m21 + m12 * m22)
        cbb = jacobian * (m21 * m21 + m22 * m22)
        at = coefs_at(r, g)
        if at is not None:
            coefs[at : at + 8, :] = caa
            coefs[at + 8 : at + 16, :] = cab
            coefs[at + 16 : at + 24, :] = cbb
        mass = jacobian * weight
        at = slope_at[r, g]
        first = slice(g * 2 * LANES, (g * 2 + 1) * LANES)
        second = slice((g * 2 + 1) * LANES, (g * 2 + 2) * LANES)
        part = slice(g * LANES, (g + 1) * LANES)
        to, direct = flux_at[r], plain_at[r]
        for f in range(FIELDS):
            one, two = fluxes(slopes[at + 8 * f : at + 8 * f + 8, :], (caa, cab, cbb))
            flux[to + 8 * f : to + 8 * f + 8, first] = one
            flux[to + 8 * f : to + 8 * f + 8, second] = two
        plain[direct : direct + 8, part] = mass
        if r in (0, 7):
            continue
        zonal, meridional = tile(r, g, 0, 8), tile(r, g, 8, 8)
        flow1 = jacobian * (m11 * zonal + m12 * meridional)
        flow2 = jacobian * (m21 * zonal + m22 * meridional)
        for k in range(2):
            carried = tile(r, g, 24 + 8 * k, 8)
            flux[to + 40 + 8 * k : to + 48 + 8 * k, first] = carried * flow1
            flux[to + 40 + 8 * k : to + 48 + 8 * k, second] = carried * flow2
        ea, eb = slopes[at + 40 : at + 48, :LANES], slopes[at + 40 : at + 48, LANES:]
        ta, tb = slopes[at + 16 : at + 24, :LANES], slopes[at + 16 : at + 24, LANES:]
        plain[direct + 8 : direct + 16, part] = mass * (
            coriolis * meridional - (m11 * ea + m21 * eb)
        )
        plain[direct + 16 : direct + 24, part] = -mass * (
            coriolis * zonal + (m12 * ea + m22 * eb)
        )
        plain[direct + 24 : direct + 32, part] = -mass * (
            zonal * (m11 * ta + m21 * tb) + meridional * (m12 * ta + m22 * tb)
        )
    spread = divergence_joined(flux[...], matrices)
    upper, lower = halves(plain[...])
    join = matrices[1408:1664, :]
    return spread, dot(upper, join) + dot(lower, join)


def face_masks():
    lane = lane_iota((1, LANES)) % 16
    return (lane < 4).astype(F32), (lane >= 12).astype(F32)


def repeated(block):
    return jnp.concatenate([block] * FIELDS, axis=0)


def second_laplacian(rows, smoothing, inverse, coefficients, matrices):
    smooth = [smoothing[r][g] * repeated(inverse[r, g]) for r in rows for g in range(2)]
    again = gradient(jnp.concatenate(smooth, axis=0), matrices)
    flat = []
    for n, r in enumerate(rows):
        parts = []
        for g in range(2):
            triple = tuple(repeated(coefficients(r, g, k)) for k in range(3))
            start = (2 * n + g) * STATE
            parts += list(fluxes(again[start : start + STATE, :], triple))
        flat.append(jnp.concatenate(parts, axis=1))
    return divergence_joined(jnp.concatenate(flat, axis=0), matrices)


def mass_inverse(mass_sum):
    return 1.0 / jnp.where(mass_sum > 0.0, mass_sum, 1.0)


def advanced(state, straight, carried, inverse):
    return state + (TIME_STEP * jnp.concatenate([straight, -carried], axis=0)) * repeated(inverse)


OWN_ROWS = (2, 3, 4, 5)
OUTER_ROWS = (0, 1, 6, 7)
MIDDLE_ROWS = (3, 4)
EDGE_ROWS = (1, 2, 5, 6)


def inner_kernel(
    low_ref,
    high_ref,
    matrices,
    lists_ref,
    spread_ref,
    direct_ref,
    coefs,
    picks_ref,
    middle_ref,
    damped_ref,
    inverse_ref,
    slopes,
    flux,
    plain,
):
    def tile(r, g, start=0, size=TILE):
        offset = ((r % 2) * 2 + g) * TILE + start
        return (low_ref if r < 4 else high_ref)[offset : offset + size, :]

    def coefs_at(r, g):
        return (2 * (r - 2) + g) * 24

    lists = send_lists([tile(r, g, STATE + 6, 1) for r in OWN_ROWS for g in range(2)])
    lists_ref[...] = lists
    line = (lists[0:1] + lists[1:2] + lists[2:3]).astype(jnp.int32) - 1
    picks_ref[...] = (row_iota((POINTS_DEV, 1024)) == line).astype(F32).astype(BF16)
    spread, direct = local_terms(
        OWN_ROWS, tile, matrices, slopes, flux, plain, coefs, coefs_at
    )
    spread_ref[...] = spread
    direct_ref[...] = direct
    masks = face_masks()

    def joined(value, size, r, start, count):
        def rows(k):
            at = (k - 2) * size + start
            return value[at : at + count, :]

        return rows_joined(rows(r - 1), rows(r), rows(r + 1), *masks)

    inverse, smoothing = {}, {}
    for r in MIDDLE_ROWS:
        mass_sum = joined(direct, 32, r, 0, 8)
        smoothing[r] = joined(spread, 56, r, 0, STATE)
        straight = joined(direct, 32, r, 8, 24)
        carried = joined(spread, 56, r, STATE, 16)
        for g in range(2):
            inverse[r, g] = mass_inverse(mass_sum[g])
            at = 2 * (r - 3) + g
            inverse_ref[8 * at : 8 * at + 8, :] = inverse[r, g]
            middle_ref[STATE * at : STATE * at + STATE, :] = advanced(
                tile(r, g, 0, STATE), straight[g], carried[g], inverse[r, g]
            )

    def coefficients(r, g, k):
        return coefs[coefs_at(r, g) + 8 * k : coefs_at(r, g) + 8 * k + 8, :]

    damped_ref[...] = second_laplacian(MIDDLE_ROWS, smoothing, inverse, coefficients, matrices)


def section_kernel(
    first_far_ref,
    second_far_ref,
    low_ref,
    high_ref,
    lists_ref,
    picks_ref,
    matrices,
    inner_spread,
    inner_direct,
    inner_coefs,
    middle_ref,
    middle_damped,
    middle_inverse,
    whole_ref,
    send_ref,
    outside,
    slopes,
    flux,
    plain,
    outer_coefs,
):
    even = lax.rem(lax.axis_index("curve"), 2) == 0
    outside[0] = jnp.where(even, second_far_ref[...], first_far_ref[...])
    outside[1] = jnp.where(even, first_far_ref[...], second_far_ref[...])

    def tile(r, g, start=0, size=TILE):
        offset = ((r % 2) * 2 + g) * TILE + start
        if r in OUTER_ROWS:
            return outside[r // 6, offset : offset + size, :]
        return (low_ref if r < 4 else high_ref)[offset : offset + size, :]

    outer_spread, outer_direct = local_terms(
        OUTER_ROWS,
        tile,
        matrices,
        slopes,
        flux,
        plain,
        outer_coefs,
        lambda r, g: {1: 24 * g, 6: 48 + 24 * g}.get(r),
    )
    masks = face_masks()
    _, outer_flux_at, outer_plain_at, _ = row_starts(OUTER_ROWS)
    _, inner_flux_at, inner_plain_at, _ = row_starts(OWN_ROWS)

    def joined(spread, r, start, count):
        def rows(k):
            if k in OUTER_ROWS:
                at = (outer_flux_at if spread else outer_plain_at)[k] + start
                return (outer_spread if spread else outer_direct)[at : at + count, :]
            at = (inner_flux_at if spread else inner_plain_at)[k] + start
            return (inner_spread if spread else inner_direct)[at : at + count, :]

        return rows_joined(rows(r - 1), rows(r), rows(r + 1), *masks)

    def coefficients(r, g, k):
        if r in OUTER_ROWS:
            at = (0 if r == 1 else 48) + 24 * g + 8 * k
            return outer_coefs[at : at + 8, :]
        at = (2 * (r - 2) + g) * 24 + 8 * k
        return inner_coefs[at : at + 8, :]

    inverse, smoothing = {}, {}
    for r in EDGE_ROWS:
        mass_sum = joined(False, r, 0, 8)
        smoothing[r] = joined(True, r, 0, STATE)
        for g in range(2):
            inverse[r, g] = mass_inverse(mass_sum[g])
    for r in MIDDLE_ROWS:
        for g in range(2):
            at = 8 * (2 * (r - 3) + g)
            inverse[r, g] = middle_inverse[at : at + 8, :]
    damped = second_laplacian(EDGE_ROWS, smoothing, inverse, coefficients, matrices)

    def damped_row(r):
        if r in MIDDLE_ROWS:
            return middle_damped[(r - 3) * STATE : (r - 2) * STATE, :]
        at = EDGE_ROWS.index(r) * STATE
        return damped[at : at + STATE, :]

    ordered = []
    for r in OWN_ROWS:
        damping = rows_joined(damped_row(r - 1), damped_row(r), damped_row(r + 1), *masks)
        if r not in MIDDLE_ROWS:
            straight = joined(False, r, 8, 24)
            carried = joined(True, r, STATE, 16)
        for g in range(2):
            if r in MIDDLE_ROWS:
                at = STATE * (2 * (r - 3) + g)
                base = middle_ref[at : at + STATE, :]
            else:
                base = advanced(tile(r, g, 0, STATE), straight[g], carried[g], inverse[r, g])
            ordered.append(
                base - ((TIME_STEP * HYPER_NU) * damping[g]) * repeated(inverse[r, g])
            )
    whole = jnp.concatenate(ordered, axis=1)
    whole_ref[...] = whole
    shares = [(lists_ref[k : k + 1, :] > 0.0).astype(F32) for k in range(3)]
    slots = [jnp.broadcast_to(lists_ref[3:4, :] * shares[k], (8, 1024)) for k in range(3)]
    row = row_iota((8, 1024))
    slot_rows = sum(jnp.where(row == k, slots[k], 0.0) for k in range(3))
    columns = jnp.concatenate([whole * share for share in shares] + [slot_rows], axis=0)
    upper, lower = halves(columns)
    sent = dot_last(picks_ref[...], jnp.concatenate([upper, lower], axis=0))
    send_ref[...] = sent[:, :LANES] + sent[:, LANES:]


def receive_kernel(
    received_ref, whole_ref, hits_ref, updated_ref, physics_ref, updated, pieces, sems
):
    whole = whole_ref[...]
    upper = whole.astype(BF16).astype(F32)
    restored = dot(jnp.concatenate([upper, whole - upper], axis=0).astype(BF16), hits_ref[...])
    updated[...] = restored[:STATE] + restored[STATE:]
    copies = [pltpu.make_async_copy(updated, updated_ref, sems.at[3])]
    copies[0].start()
    turned_over = received_ref[...].T
    upper, lower = halves(turned_over)
    places = slice(3 * STATE, 3 * STATE + 3)
    slot = turned_over[places, :].astype(jnp.int32) - 1
    both = jnp.concatenate([upper, lower], axis=0)
    count = 2 * LANES
    for start in range(0, POINTS_DEV, count):
        row = row_iota((count, POINTS_DEV)) + start
        hits = (row == slot[0:1]) | (row == slot[1:2]) | (row == slot[2:3])
        rows = dot_last(both, hits.astype(F32).astype(BF16))
        rows = rows[:LANES] + rows[LANES:]
        own = rows[places, :] == (lane_iota((3, count)) + (start + 1)).astype(F32)
        piece = start // count
        pieces[piece] = jnp.where(
            own[0:1],
            rows[:STATE],
            jnp.where(own[1:2], rows[STATE : 2 * STATE], rows[2 * STATE : 3 * STATE]),
        )
        copies.append(
            pltpu.make_async_copy(
                pieces.at[piece], physics_ref.at[:, pl.ds(start, count)], sems.at[piece]
            )
        )
        copies[-1].start()
    for copy in copies:
        copy.wait()


def call(kernel, shapes, scratch=(), flops=0, moved=0, vmem=VMEM_LIMIT, **specs):
    return pl.pallas_call(
        kernel,
        out_shape=[
            jax.ShapeDtypeStruct(*s) if isinstance(s, tuple) else s for s in shapes
        ],
        scratch_shapes=list(scratch),
        **specs,
        compiler_params=pltpu.CompilerParams(vmem_limit_bytes=vmem),
        cost_estimate=pl.CostEstimate(flops=flops, bytes_accessed=moved, transcendentals=0),
    )


def swaps(count, pairs_from):
    route = []
    for i in range(pairs_from, count - 1, 2):
        route += [(i, i + 1), (i + 1, i)]
    return route


def body(
    evolving_state_array, point_id, neighbours, jacobian, inverse_metric, coriolis, column_slot
):
    anywhere = pl.BlockSpec(memory_space=pltpu.HBM)
    half = ((4 * TILE, LANES), F32)
    strip = ((TILE, LANES), F32)
    values_shape = ((TILE + 8, POINTS_DEV), F32)
    far, close, values = call(
        strip_kernel,
        [pltpu.VMEM(*strip), pltpu.VMEM(*strip), pltpu.VMEM(*values_shape)],
        scratch=[
            pltpu.VMEM((8, ELEMS_DEV), jnp.int32),
            pltpu.VMEM((POINTS_DEV,), F32),
            pltpu.VMEM((POINTS_DEV,), F32),
            pltpu.VMEM((4, POINTS_DEV), F32),
            pltpu.VMEM((POINTS_DEV,), jnp.int32),
            pltpu.VMEM((FIELDS, LEV, POINTS_DEV), F32),
            pltpu.SemaphoreType.DMA((6,)),
        ],
        in_specs=[anywhere] * 6,
        vmem=64 * 1024 * 1024 - 524288,
    )(evolving_state_array, jacobian, coriolis, inverse_metric, neighbours, column_slot)
    cols, rows = lax.axis_size("col"), lax.axis_size("curve")
    from_far = lax.ppermute(far, "col", swaps(cols, 1) + [(cols - 1, 0), (0, cols - 1)])
    from_close = lax.ppermute(close, "col", swaps(cols, 0))
    low, high, hits = call(
        arrange_kernel,
        [half, half, pltpu.VMEM((1024, POINTS_DEV), BF16)],
        flops=400_000_000,
        moved=1_000_000,
    )(values)
    first, second, low, high = call(margin_kernel, [half] * 4)(low, high, from_far, from_close)
    second_far = lax.ppermute(second, "curve", swaps(rows, 1))
    first_far = lax.ppermute(first, "curve", swaps(rows, 0))
    matrices = jnp.asarray(operators())
    def scratch(rows):
        slope_rows, flux_rows, plain_rows = row_starts(rows)[3]
        return [
            pltpu.VMEM((slope_rows, 2 * LANES), F32),
            pltpu.VMEM((flux_rows, 4 * LANES), F32),
            pltpu.VMEM((plain_rows, 2 * LANES), F32),
        ]

    inner = call(
        inner_kernel,
        [
            ((8, 1024), F32),
            ((4 * 56, 2 * LANES), F32),
            ((4 * 32, 2 * LANES), F32),
            ((8 * 24, LANES), F32),
            ((POINTS_DEV, 1024), BF16),
            ((4 * STATE, LANES), F32),
            ((2 * STATE, 2 * LANES), F32),
            ((4 * 8, LANES), F32),
        ],
        scratch=scratch(OWN_ROWS),
        flops=400_000_000,
        moved=1_000_000,
    )(low, high, matrices)
    lists, spread, direct, coefs, picks, middle, middle_damped, middle_inverse = inner
    whole, sent = call(
        section_kernel,
        [((STATE, 1024), F32), ((POINTS_DEV, LANES), F32)],
        scratch=[pltpu.VMEM((2, 4 * TILE, LANES), F32)]
        + scratch(OUTER_ROWS)
        + [pltpu.VMEM((4 * 24, LANES), F32)],
    )(
        first_far,
        second_far,
        low,
        high,
        lists,
        picks,
        matrices,
        spread,
        direct,
        coefs,
        middle,
        middle_damped,
        middle_inverse,
    )
    received = lax.all_to_all(sent, "col", split_axis=0, concat_axis=0, tiled=True)
    updated, physics = call(
        receive_kernel,
        [((STATE, POINTS_DEV), F32)] * 2,
        scratch=[
            pltpu.VMEM((STATE, POINTS_DEV), F32),
            pltpu.VMEM((3, STATE, 2 * LANES), F32),
            pltpu.SemaphoreType.DMA((4,)),
        ],
        in_specs=[pl.BlockSpec(memory_space=pltpu.VMEM)] * 3,
        out_specs=[anywhere] * 2,
    )(received, whole, hits)
    shape = evolving_state_array.shape
    return updated.reshape(shape), physics.reshape(shape)


def solution(mesh):
    split = ("curve", "col")
    return jax.shard_map(
        body,
        mesh=mesh,
        in_specs=(
            P(None, None, split),
            P(split),
            P(None, split),
            P(split),
            P(None, split),
            P(split),
            P(split),
        ),
        out_specs=(P(None, None, split), P(None, None, split)),
        check_vma=False,
    )
```

```python
import functools
import math

import jax
import jax.numpy as jnp
import numpy as np
from jax import lax
from jax.experimental import pallas as pl
from jax.experimental.pallas import tpu as pltpu
from jax.sharding import PartitionSpec as P

FIELDS = 5
LEV = 8
STATE = FIELDS * LEV
TILE = 48
LANES = 128
ELEMS_DEV = 48
POINTS_DEV = 768
N_COL = 32
CAP = 72
CAP_ROWS = CAP // 3
TIME_STEP = 0.1
HYPER_NU = 0.002
F32 = jnp.float32
BF16 = jnp.bfloat16
VMEM_LIMIT = 32 * 1024 * 1024


def gll_tables():
    root_fifth = 1.0 / math.sqrt(5.0)
    nodes = np.array([-1.0, -root_fifth, root_fifth, 1.0])
    weights = np.array([1.0, 5.0, 5.0, 1.0]) / 6.0
    table = np.zeros((4, 4))
    for i in range(4):
        for m in range(4):
            if i == m:
                table[i, m] = sum(1.0 / (nodes[i] - nodes[o]) for o in range(4) if o != i)
            else:
                upper = np.prod([nodes[i] - nodes[o] for o in range(4) if o != i])
                lower = np.prod([nodes[m] - nodes[o] for o in range(4) if o != m])
                table[i, m] = upper / (lower * (nodes[i] - nodes[m]))
    return table, weights


def two_parts(matrix):
    upper = matrix.astype(np.float32).astype(jnp.bfloat16)
    lower = (matrix - upper.astype(np.float64)).astype(np.float32).astype(jnp.bfloat16)
    return upper, lower


@functools.lru_cache(maxsize=None)
def operators():
    table, weights = gll_tables()
    eye4, eye8 = np.eye(4), np.eye(8)
    along_cycle = np.kron(eye4, table.T)
    along_rows = np.kron(table.T, eye4)
    grad = np.concatenate([np.kron(eye8, along_cycle), np.kron(eye8, along_rows)], axis=1)
    weight = np.diag(np.outer(weights, weights).reshape(16))
    div = np.concatenate(
        [np.kron(eye8, along_cycle @ weight), np.kron(eye8, along_rows @ weight)], axis=0
    )
    join = np.eye(256)
    for place in range(15):
        for j in range(4):
            low, high = place * 16 + 4 * j + 3, place * 16 + 16 + 4 * j
            join[low, high] = 1.0
            join[high, low] = 1.0
    both = np.zeros((512, 256))
    both[:256, :128] = div
    both[256:, 128:] = div
    div_join = both @ join
    grad_hi, grad_lo = two_parts(grad)
    div_hi, div_lo = two_parts(div_join)
    return np.concatenate(
        [grad_hi, grad_hi, grad_lo, div_hi, div_lo, join.astype(jnp.bfloat16)], axis=0
    )


def dot(left, right):
    return jnp.dot(left, right, preferred_element_type=F32)


def dot_last(left, right):
    return lax.dot_general(left, right, (((1,), (1,)), ((), ())), preferred_element_type=F32)


def halves(value):
    upper = value.astype(BF16)
    lower = (value - upper.astype(F32)).astype(BF16)
    return upper, lower


def lane_iota(shape):
    return lax.broadcasted_iota(jnp.int32, shape, 1)


def row_iota(shape):
    return lax.broadcasted_iota(jnp.int32, shape, 0)


def one_step(local, index):
    hit = (row_iota((ELEMS_DEV, ELEMS_DEV)) == index) & local
    return hit.astype(F32).astype(BF16)


def wide(local):
    return jnp.broadcast_to(local.astype(F32), (8, ELEMS_DEV))


def chain_length(local, index, doublings):
    length = wide(local)
    step = one_step(local, index)
    for k in range(doublings):
        length = length + dot(length.astype(BF16), step)
        if k + 1 < doublings:
            step = dot(step, step).astype(BF16)
    return length


def local_lists(near):
    base = (lax.axis_index("curve") * N_COL + lax.axis_index("col")) * ELEMS_DEV
    index = near - base
    return index, (index >= 0) & (index < ELEMS_DEV)


def over_points(element_values):
    shape = (ELEMS_DEV, POINTS_DEV)
    spread = (lane_iota(shape) // 16 == row_iota(shape)).astype(F32).astype(BF16)
    return dot(element_values.astype(BF16), spread)[0:1].astype(jnp.int32)


def three_parts(value):
    first = value.astype(BF16)
    rest = value - first.astype(F32)
    second = rest.astype(BF16)
    return first, second, (rest - second.astype(F32)).astype(BF16)


def strip_kernel(
    state_ref, jacobian_ref, coriolis_ref, metric_ref, near_ref, slot_ref, far_ref, close_ref,
    values_ref, near, jac, cor, metric, slot, state, sems
):
    copies = [
        pltpu.make_async_copy(source, target, sems.at[i])
        for i, (source, target) in enumerate(
            [
                (near_ref, near),
                (state_ref, state),
                (jacobian_ref, jac),
                (coriolis_ref, cor),
                (metric_ref, metric),
                (slot_ref, slot),
            ]
        )
    ]
    for copy in copies:
        copy.start()
    copies[0].wait()
    index, local = local_lists(near[...])
    lower = wide(local[2:3])
    row = lower + dot(lower.astype(BF16), one_step(local[2:3], index[2:3])) + wide(~local[3:4])
    sides = []
    for side in range(2):
        here, there = local[side : side + 1], index[side : side + 1]
        second = dot(wide(here).astype(BF16), one_step(here, there))
        edge = wide(~here)
        sides.append((edge, wide(here) * (1.0 - second)))
    (first, second), (last, second_last) = sides
    unit = (first + second) * (2.0 * row + 1.0 + second)
    unit = unit + (last + second_last) * (2.0 * row + 9.0 + last)
    lane = (over_points(unit) - 1) * 16 + lane_iota((1, POINTS_DEV)) % 16
    hits = (row_iota((2 * LANES, POINTS_DEV)) == lane).astype(F32).astype(BF16)
    for copy in copies[1:]:
        copy.wait()
    values = jnp.concatenate(
        [
            state[...].reshape(STATE, POINTS_DEV),
            jac[...].reshape(1, POINTS_DEV),
            cor[...].reshape(1, POINTS_DEV),
            metric[...],
            slot[...].astype(F32).reshape(1, POINTS_DEV),
            jnp.zeros((1, POINTS_DEV), F32),
        ],
        axis=0,
    )
    values_ref[0:TILE, :] = values
    values_ref[TILE:, 0:ELEMS_DEV] = jnp.where(local, index, -1).astype(F32)
    parts = dot_last(jnp.concatenate(halves(values), axis=0), hits)
    strips = parts[:TILE] + parts[TILE:]
    even = lax.rem(lax.axis_index("col"), 2) == 0
    to_left, to_right = strips[:, :LANES], strips[:, LANES:]
    far_ref[...] = jnp.where(even, to_left, to_right)
    close_ref[...] = jnp.where(even, to_right, to_left)


def arrange_kernel(values_ref, low_ref, high_ref, hits_ref):
    index = values_ref[TILE:, 0:ELEMS_DEV].astype(jnp.int32)
    local = index >= 0
    place = chain_length(local[0:1], index[0:1], 4)
    row = chain_length(local[2:3], index[2:3], 2)
    target = over_points(row * 16.0 + place + 2.0) * 16 + lane_iota((1, POINTS_DEV)) % 16
    hits = (row_iota((1024, POINTS_DEV)) == target).astype(F32).astype(BF16)
    hits_ref[...] = hits
    parts = dot_last(jnp.concatenate(three_parts(values_ref[0:TILE, :]), axis=0), hits)
    ordered = parts[0:TILE] + parts[TILE : 2 * TILE] + parts[2 * TILE :]
    for r in range(4):
        for g in range(2):
            block = ordered[:, (2 * r + g) * LANES : (2 * r + g + 1) * LANES]
            ref = low_ref if r < 2 else high_ref
            start = ((r % 2) * 2 + g) * TILE
            ref[start : start + TILE, :] = block


def turned(block, by):
    by = by % LANES
    return block if by == 0 else pltpu.roll(block, by, 1)


def margin_kernel(
    low_in, high_in, from_far, from_close, first_ref, second_ref, low_ref, high_ref
):
    lane = lane_iota((TILE, LANES))
    even = lax.rem(lax.axis_index("col"), 2) == 0
    from_left = jnp.where(even, from_far[...], from_close[...])
    from_right = jnp.where(even, from_close[...], from_far[...])
    halves_of_rows = []
    for source, start_row in ((low_in, 0), (high_in, 2)):
        blocks = []
        for r in range(2):
            turn = start_row + r
            start = r * 2 * TILE
            blocks.append(
                jnp.where(lane < 32, turned(from_left, -32 * turn), source[start : start + TILE, :])
            )
            start += TILE
            blocks.append(
                jnp.where(
                    lane >= 96, turned(from_right, 96 - 32 * turn), source[start : start + TILE, :]
                )
            )
        halves_of_rows.append(jnp.concatenate(blocks, axis=0))
    low, high = halves_of_rows
    low_ref[...] = low
    high_ref[...] = high
    even = lax.rem(lax.axis_index("curve"), 2) == 0
    first_ref[...] = jnp.where(even, high, low)
    second_ref[...] = jnp.where(even, low, high)


def send_lists(slots):
    square = (LANES, LANES)
    upto = (row_iota(square) <= lane_iota(square)).astype(F32)
    count = jnp.concatenate([upto, jnp.ones(square, F32)], axis=1).astype(BF16)
    lane = lane_iota((1, LANES))
    chosen, devices, withins, owns = [], [], [], []
    for i, slot in enumerate(slots):
        own = lane >= 32 if i % 2 == 0 else lane < 96
        device = jnp.where(own, jnp.floor((slot + 0.5) * (1.0 / POINTS_DEV)), -1.0)
        wanted = jnp.broadcast_to(device.astype(jnp.int32), (N_COL, LANES))
        chosen.append((wanted == row_iota((N_COL, LANES))).astype(F32))
        devices.append(device)
        withins.append(slot - device * POINTS_DEV)
        owns.append(own)
    counted = dot(jnp.concatenate(chosen, axis=0).astype(BF16), count)
    before = jnp.zeros((N_COL, LANES), F32)
    lists = []
    for i, (device, within, own) in enumerate(zip(devices, withins, owns)):
        rows = counted[i * N_COL : (i + 1) * N_COL]
        rank = jnp.sum((rows[:, :LANES] + before) * chosen[i], axis=0, keepdims=True) - 1.0
        before = before + rows[:, LANES:]
        third = (rank >= CAP_ROWS).astype(F32) + (rank >= 2 * CAP_ROWS).astype(F32)
        line = device * CAP_ROWS + rank - third * CAP_ROWS
        parts = [jnp.where(own & (third == float(k)), line + 1.0, 0.0) for k in range(3)]
        filler = jnp.zeros((4, LANES), F32)
        lists.append(
            jnp.concatenate(parts + [jnp.where(own, within + 1.0, 0.0), filler], axis=0)
        )
    return jnp.concatenate(lists, axis=1)


def fluxes(slope, coefficients):
    along_cycle, along_rows = slope[:, :LANES], slope[:, LANES:]
    caa, cab, cbb = coefficients
    return caa * along_cycle + cab * along_rows, cab * along_cycle + cbb * along_rows


def gradient(values, matrices):
    upper, lower = halves(values)
    return dot(jnp.concatenate([upper, lower], axis=1), matrices[0:256, :]) + dot(
        upper, matrices[256:384, :]
    )


def divergence_joined(values, matrices):
    upper, lower = halves(values)
    first = matrices[384:896, :]
    return dot(upper, first) + dot(lower, first) + dot(upper, matrices[896:1408, :])


def rows_joined(below, here, above, low_mask, high_mask):
    parts = []
    for g in range(2):
        part = slice(g * LANES, (g + 1) * LANES)
        parts.append(
            here[:, part]
            + low_mask * turned(below[:, part], -12)
            + high_mask * turned(above[:, part], 12)
        )
    return parts


def row_starts(rows):
    slope, flux, plain = {}, {}, {}
    at = [0, 0, 0]
    for r in rows:
        lean = r in (0, 7)
        for g in range(2):
            slope[r, g] = at[0]
            at[0] += STATE if lean else TILE
        flux[r] = at[1]
        at[1] += STATE if lean else STATE + 16
        plain[r] = at[2]
        at[2] += 8 if lean else 32
    return slope, flux, plain, at


def local_terms(rows, tile, matrices, slopes, flux, plain, coefs, coefs_at):
    slope_at, flux_at, plain_at, _ = row_starts(rows)
    cells = [(r, g) for r in rows for g in range(2)]
    stacked = []
    for r, g in cells:
        stacked.append(tile(r, g, 0, STATE))
        if r not in (0, 7):
            zonal, meridional = tile(r, g, 0, 8), tile(r, g, 8, 8)
            energy = 0.5 * (zonal * zonal + meridional * meridional) + tile(r, g, 16, 8)
            stacked.append(energy)
    slopes[...] = gradient(jnp.concatenate(stacked, axis=0), matrices)
    lane = lane_iota((8, LANES))
    inner_i = (lane % 4 == 1) | (lane % 4 == 2)
    inner_j = (lane // 4 % 4 == 1) | (lane // 4 % 4 == 2)
    weight = jnp.where(inner_i, 5.0 / 6.0, 1.0 / 6.0) * jnp.where(inner_j, 5.0 / 6.0, 1.0 / 6.0)
    for r, g in cells:

        def line(k):
            return jnp.broadcast_to(tile(r, g, STATE + k, 1), (8, LANES))

        jacobian, coriolis = line(0), line(1)
        m11, m12, m21, m22 = 1.0 + line(2), line(3), line(4), 1.0 + line(5)
        caa = jacobian * (m11 * m11 + m12 * m12)
        cab = jacobian * (m11 * m21 + m12 * m22)
        cbb = jacobian * (m21 * m21 + m22 * m22)
        at = coefs_at(r, g)
        if at is not None:
            coefs[at : at + 8, :] = caa
            coefs[at + 8 : at + 16, :] = cab
            coefs[at + 16 : at + 24, :] = cbb
        mass = jacobian * weight
        at = slope_at[r, g]
        first = slice(g * 2 * LANES, (g * 2 + 1) * LANES)
        second = slice((g * 2 + 1) * LANES, (g * 2 + 2) * LANES)
        part = slice(g * LANES, (g + 1) * LANES)
        to, direct = flux_at[r], plain_at[r]
        for f in range(FIELDS):
            one, two = fluxes(slopes[at + 8 * f : at + 8 * f + 8, :], (caa, cab, cbb))
            flux[to + 8 * f : to + 8 * f + 8, first] = one
            flux[to + 8 * f : to + 8 * f + 8, second] = two
        plain[direct : direct + 8, part] = mass
        if r in (0, 7):
            continue
        zonal, meridional = tile(r, g, 0, 8), tile(r, g, 8, 8)
        flow1 = jacobian * (m11 * zonal + m12 * meridional)
        flow2 = jacobian * (m21 * zonal + m22 * meridional)
        for k in range(2):
            carried = tile(r, g, 24 + 8 * k, 8)
            flux[to + 40 + 8 * k : to + 48 + 8 * k, first] = carried * flow1
            flux[to + 40 + 8 * k : to + 48 + 8 * k, second] = carried * flow2
        ea, eb = slopes[at + 40 : at + 48, :LANES], slopes[at + 40 : at + 48, LANES:]
        ta, tb = slopes[at + 16 : at + 24, :LANES], slopes[at + 16 : at + 24, LANES:]
        plain[direct + 8 : direct + 16, part] = mass * (
            coriolis * meridional - (m11 * ea + m21 * eb)
        )
        plain[direct + 16 : direct + 24, part] = -mass * (
            coriolis * zonal + (m12 * ea + m22 * eb)
        )
        plain[direct + 24 : direct + 32, part] = -mass * (
            zonal * (m11 * ta + m21 * tb) + meridional * (m12 * ta + m22 * tb)
        )
    spread = divergence_joined(flux[...], matrices)
    upper, lower = halves(plain[...])
    join = matrices[1408:1664, :]
    return spread, dot(upper, join) + dot(lower, join)


def face_masks():
    lane = lane_iota((1, LANES)) % 16
    return (lane < 4).astype(F32), (lane >= 12).astype(F32)


def repeated(block):
    return jnp.concatenate([block] * FIELDS, axis=0)


def second_laplacian(rows, smoothing, inverse, coefficients, matrices):
    smooth = [smoothing[r][g] * repeated(inverse[r, g]) for r in rows for g in range(2)]
    again = gradient(jnp.concatenate(smooth, axis=0), matrices)
    flat = []
    for n, r in enumerate(rows):
        parts = []
        for g in range(2):
            triple = tuple(repeated(coefficients(r, g, k)) for k in range(3))
            start = (2 * n + g) * STATE
            parts += list(fluxes(again[start : start + STATE, :], triple))
        flat.append(jnp.concatenate(parts, axis=1))
    return divergence_joined(jnp.concatenate(flat, axis=0), matrices)


def mass_inverse(mass_sum):
    return 1.0 / jnp.where(mass_sum > 0.0, mass_sum, 1.0)


def advanced(state, straight, carried, inverse):
    return state + (TIME_STEP * jnp.concatenate([straight, -carried], axis=0)) * repeated(inverse)


OWN_ROWS = (2, 3, 4, 5)
OUTER_ROWS = (0, 1, 6, 7)
MIDDLE_ROWS = (3, 4)
EDGE_ROWS = (1, 2, 5, 6)


def inner_kernel(
    low_ref,
    high_ref,
    matrices,
    lists_ref,
    spread_ref,
    direct_ref,
    coefs,
    picks_ref,
    middle_ref,
    damped_ref,
    inverse_ref,
    slopes,
    flux,
    plain,
):
    def tile(r, g, start=0, size=TILE):
        offset = ((r % 2) * 2 + g) * TILE + start
        return (low_ref if r < 4 else high_ref)[offset : offset + size, :]

    def coefs_at(r, g):
        return (2 * (r - 2) + g) * 24

    lists = send_lists([tile(r, g, STATE + 6, 1) for r in OWN_ROWS for g in range(2)])
    lists_ref[...] = lists
    line = (lists[0:1] + lists[1:2] + lists[2:3]).astype(jnp.int32) - 1
    picks_ref[...] = (row_iota((POINTS_DEV, 1024)) == line).astype(F32).astype(BF16)
    spread, direct = local_terms(
        OWN_ROWS, tile, matrices, slopes, flux, plain, coefs, coefs_at
    )
    spread_ref[...] = spread
    direct_ref[...] = direct
    masks = face_masks()

    def joined(value, size, r, start, count):
        def rows(k):
            at = (k - 2) * size + start
            return value[at : at + count, :]

        return rows_joined(rows(r - 1), rows(r), rows(r + 1), *masks)

    inverse, smoothing = {}, {}
    for r in MIDDLE_ROWS:
        mass_sum = joined(direct, 32, r, 0, 8)
        smoothing[r] = joined(spread, 56, r, 0, STATE)
        straight = joined(direct, 32, r, 8, 24)
        carried = joined(spread, 56, r, STATE, 16)
        for g in range(2):
            inverse[r, g] = mass_inverse(mass_sum[g])
            at = 2 * (r - 3) + g
            inverse_ref[8 * at : 8 * at + 8, :] = inverse[r, g]
            middle_ref[STATE * at : STATE * at + STATE, :] = advanced(
                tile(r, g, 0, STATE), straight[g], carried[g], inverse[r, g]
            )

    def coefficients(r, g, k):
        return coefs[coefs_at(r, g) + 8 * k : coefs_at(r, g) + 8 * k + 8, :]

    damped_ref[...] = second_laplacian(MIDDLE_ROWS, smoothing, inverse, coefficients, matrices)


def section_kernel(
    first_far_ref,
    second_far_ref,
    low_ref,
    high_ref,
    lists_ref,
    picks_ref,
    matrices,
    inner_spread,
    inner_direct,
    inner_coefs,
    middle_ref,
    middle_damped,
    middle_inverse,
    whole_ref,
    send_ref,
    outside,
    slopes,
    flux,
    plain,
    outer_coefs,
):
    even = lax.rem(lax.axis_index("curve"), 2) == 0
    outside[0] = jnp.where(even, second_far_ref[...], first_far_ref[...])
    outside[1] = jnp.where(even, first_far_ref[...], second_far_ref[...])

    def tile(r, g, start=0, size=TILE):
        offset = ((r % 2) * 2 + g) * TILE + start
        if r in OUTER_ROWS:
            return outside[r // 6, offset : offset + size, :]
        return (low_ref if r < 4 else high_ref)[offset : offset + size, :]

    outer_spread, outer_direct = local_terms(
        OUTER_ROWS,
        tile,
        matrices,
        slopes,
        flux,
        plain,
        outer_coefs,
        lambda r, g: {1: 24 * g, 6: 48 + 24 * g}.get(r),
    )
    masks = face_masks()
    _, outer_flux_at, outer_plain_at, _ = row_starts(OUTER_ROWS)
    _, inner_flux_at, inner_plain_at, _ = row_starts(OWN_ROWS)

    def joined(spread, r, start, count):
        def rows(k):
            if k in OUTER_ROWS:
                at = (outer_flux_at if spread else outer_plain_at)[k] + start
                return (outer_spread if spread else outer_direct)[at : at + count, :]
            at = (inner_flux_at if spread else inner_plain_at)[k] + start
            return (inner_spread if spread else inner_direct)[at : at + count, :]

        return rows_joined(rows(r - 1), rows(r), rows(r + 1), *masks)

    def coefficients(r, g, k):
        if r in OUTER_ROWS:
            at = (0 if r == 1 else 48) + 24 * g + 8 * k
            return outer_coefs[at : at + 8, :]
        at = (2 * (r - 2) + g) * 24 + 8 * k
        return inner_coefs[at : at + 8, :]

    inverse, smoothing = {}, {}
    for r in EDGE_ROWS:
        mass_sum = joined(False, r, 0, 8)
        smoothing[r] = joined(True, r, 0, STATE)
        for g in range(2):
            inverse[r, g] = mass_inverse(mass_sum[g])
    for r in MIDDLE_ROWS:
        for g in range(2):
            at = 8 * (2 * (r - 3) + g)
            inverse[r, g] = middle_inverse[at : at + 8, :]
    damped = second_laplacian(EDGE_ROWS, smoothing, inverse, coefficients, matrices)

    def damped_row(r):
        if r in MIDDLE_ROWS:
            return middle_damped[(r - 3) * STATE : (r - 2) * STATE, :]
        at = EDGE_ROWS.index(r) * STATE
        return damped[at : at + STATE, :]

    ordered = []
    for r in OWN_ROWS:
        damping = rows_joined(damped_row(r - 1), damped_row(r), damped_row(r + 1), *masks)
        if r not in MIDDLE_ROWS:
            straight = joined(False, r, 8, 24)
            carried = joined(True, r, STATE, 16)
        for g in range(2):
            if r in MIDDLE_ROWS:
                at = STATE * (2 * (r - 3) + g)
                base = middle_ref[at : at + STATE, :]
            else:
                base = advanced(tile(r, g, 0, STATE), straight[g], carried[g], inverse[r, g])
            ordered.append(
                base - ((TIME_STEP * HYPER_NU) * damping[g]) * repeated(inverse[r, g])
            )
    whole = jnp.concatenate(ordered, axis=1)
    whole_ref[...] = whole
    shares = [(lists_ref[k : k + 1, :] > 0.0).astype(F32) for k in range(3)]
    slots = [jnp.broadcast_to(lists_ref[3:4, :] * shares[k], (8, 1024)) for k in range(3)]
    row = row_iota((8, 1024))
    slot_rows = sum(jnp.where(row == k, slots[k], 0.0) for k in range(3))
    columns = jnp.concatenate([whole * share for share in shares] + [slot_rows], axis=0)
    upper, lower = halves(columns)
    sent = dot_last(picks_ref[...], jnp.concatenate([upper, lower], axis=0))
    send_ref[...] = sent[:, :LANES] + sent[:, LANES:]


def receive_kernel(
    received_ref, whole_ref, hits_ref, updated_ref, physics_ref, updated, pieces, sems
):
    whole = whole_ref[...]
    upper = whole.astype(BF16).astype(F32)
    restored = dot(jnp.concatenate([upper, whole - upper], axis=0).astype(BF16), hits_ref[...])
    updated[...] = restored[:STATE] + restored[STATE:]
    copies = [pltpu.make_async_copy(updated, updated_ref, sems.at[3])]
    copies[0].start()
    turned_over = received_ref[...].T
    upper, lower = halves(turned_over)
    places = slice(3 * STATE, 3 * STATE + 3)
    slot = turned_over[places, :].astype(jnp.int32) - 1
    slots = [slot[k : k + 1].astype(jnp.int16) for k in range(3)]
    both = jnp.concatenate([upper, lower], axis=0)
    count = 2 * LANES
    for start in range(0, POINTS_DEV, count):
        row = (row_iota((count, POINTS_DEV)) + start).astype(jnp.int16)
        hits = (row == slots[0]) | (row == slots[1]) | (row == slots[2])
        rows = dot_last(both, jnp.where(hits, jnp.bfloat16(1), jnp.bfloat16(0)))
        rows = rows[:LANES] + rows[LANES:]
        own = rows[places, :] == (lane_iota((3, count)) + (start + 1)).astype(F32)
        piece = start // count
        pieces[piece] = jnp.where(
            own[0:1],
            rows[:STATE],
            jnp.where(own[1:2], rows[STATE : 2 * STATE], rows[2 * STATE : 3 * STATE]),
        )
        copies.append(
            pltpu.make_async_copy(
                pieces.at[piece], physics_ref.at[:, pl.ds(start, count)], sems.at[piece]
            )
        )
        copies[-1].start()
    for copy in copies:
        copy.wait()


def call(kernel, shapes, scratch=(), flops=0, moved=0, vmem=VMEM_LIMIT, **specs):
    return pl.pallas_call(
        kernel,
        out_shape=[
            jax.ShapeDtypeStruct(*s) if isinstance(s, tuple) else s for s in shapes
        ],
        scratch_shapes=list(scratch),
        **specs,
        compiler_params=pltpu.CompilerParams(vmem_limit_bytes=vmem),
        cost_estimate=pl.CostEstimate(flops=flops, bytes_accessed=moved, transcendentals=0),
    )


def swaps(count, pairs_from):
    route = []
    for i in range(pairs_from, count - 1, 2):
        route += [(i, i + 1), (i + 1, i)]
    return route


def body(
    evolving_state_array, point_id, neighbours, jacobian, inverse_metric, coriolis, column_slot
):
    anywhere = pl.BlockSpec(memory_space=pltpu.HBM)
    half = ((4 * TILE, LANES), F32)
    strip = ((TILE, LANES), F32)
    values_shape = ((TILE + 8, POINTS_DEV), F32)
    far, close, values = call(
        strip_kernel,
        [pltpu.VMEM(*strip), pltpu.VMEM(*strip), pltpu.VMEM(*values_shape)],
        scratch=[
            pltpu.VMEM((8, ELEMS_DEV), jnp.int32),
            pltpu.VMEM((POINTS_DEV,), F32),
            pltpu.VMEM((POINTS_DEV,), F32),
            pltpu.VMEM((4, POINTS_DEV), F32),
            pltpu.VMEM((POINTS_DEV,), jnp.int32),
            pltpu.VMEM((FIELDS, LEV, POINTS_DEV), F32),
            pltpu.SemaphoreType.DMA((6,)),
        ],
        in_specs=[anywhere] * 6,
        vmem=64 * 1024 * 1024 - 524288,
    )(evolving_state_array, jacobian, coriolis, inverse_metric, neighbours, column_slot)
    cols, rows = lax.axis_size("col"), lax.axis_size("curve")
    from_far = lax.ppermute(far, "col", swaps(cols, 1) + [(cols - 1, 0), (0, cols - 1)])
    from_close = lax.ppermute(close, "col", swaps(cols, 0))
    low, high, hits = call(
        arrange_kernel,
        [half, half, pltpu.VMEM((1024, POINTS_DEV), BF16)],
        flops=400_000_000,
        moved=1_000_000,
    )(values)
    first, second, low, high = call(margin_kernel, [half] * 4)(low, high, from_far, from_close)
    second_far = lax.ppermute(second, "curve", swaps(rows, 1))
    first_far = lax.ppermute(first, "curve", swaps(rows, 0))
    matrices = jnp.asarray(operators())
    def scratch(rows):
        slope_rows, flux_rows, plain_rows = row_starts(rows)[3]
        return [
            pltpu.VMEM((slope_rows, 2 * LANES), F32),
            pltpu.VMEM((flux_rows, 4 * LANES), F32),
            pltpu.VMEM((plain_rows, 2 * LANES), F32),
        ]

    inner = call(
        inner_kernel,
        [
            ((8, 1024), F32),
            ((4 * 56, 2 * LANES), F32),
            ((4 * 32, 2 * LANES), F32),
            ((8 * 24, LANES), F32),
            ((POINTS_DEV, 1024), BF16),
            ((4 * STATE, LANES), F32),
            ((2 * STATE, 2 * LANES), F32),
            ((4 * 8, LANES), F32),
        ],
        scratch=scratch(OWN_ROWS),
        flops=400_000_000,
        moved=1_000_000,
    )(low, high, matrices)
    lists, spread, direct, coefs, picks, middle, middle_damped, middle_inverse = inner
    whole, sent = call(
        section_kernel,
        [((STATE, 1024), F32), ((POINTS_DEV, LANES), F32)],
        scratch=[pltpu.VMEM((2, 4 * TILE, LANES), F32)]
        + scratch(OUTER_ROWS)
        + [pltpu.VMEM((4 * 24, LANES), F32)],
    )(
        first_far,
        second_far,
        low,
        high,
        lists,
        picks,
        matrices,
        spread,
        direct,
        coefs,
        middle,
        middle_damped,
        middle_inverse,
    )
    received = lax.all_to_all(sent, "col", split_axis=0, concat_axis=0, tiled=True)
    updated, physics = call(
        receive_kernel,
        [((STATE, POINTS_DEV), F32)] * 2,
        scratch=[
            pltpu.VMEM((STATE, POINTS_DEV), F32),
            pltpu.VMEM((3, STATE, 2 * LANES), F32),
            pltpu.SemaphoreType.DMA((4,)),
        ],
        in_specs=[pl.BlockSpec(memory_space=pltpu.VMEM)] * 3,
        out_specs=[anywhere] * 2,
    )(received, whole, hits)
    shape = evolving_state_array.shape
    return updated.reshape(shape), physics.reshape(shape)


def solution(mesh):
    split = ("curve", "col")
    return jax.shard_map(
        body,
        mesh=mesh,
        in_specs=(
            P(None, None, split),
            P(split),
            P(None, split),
            P(split),
            P(None, split),
            P(split),
            P(split),
        ),
        out_specs=(P(None, None, split), P(None, None, split)),
        check_vma=False,
    )
```

```python
import functools
import math

import jax
import jax.numpy as jnp
import numpy as np
from jax import lax
from jax.experimental import pallas as pl
from jax.experimental.pallas import tpu as pltpu
from jax.sharding import PartitionSpec as P

FIELDS = 5
LEV = 8
STATE = FIELDS * LEV
TILE = 48
LANES = 128
ELEMS_DEV = 48
POINTS_DEV = 768
N_COL = 32
CAP = 72
CAP_ROWS = CAP // 3
TIME_STEP = 0.1
HYPER_NU = 0.002
F32 = jnp.float32
BF16 = jnp.bfloat16
VMEM_LIMIT = 32 * 1024 * 1024


def gll_tables():
    root_fifth = 1.0 / math.sqrt(5.0)
    nodes = np.array([-1.0, -root_fifth, root_fifth, 1.0])
    weights = np.array([1.0, 5.0, 5.0, 1.0]) / 6.0
    table = np.zeros((4, 4))
    for i in range(4):
        for m in range(4):
            if i == m:
                table[i, m] = sum(1.0 / (nodes[i] - nodes[o]) for o in range(4) if o != i)
            else:
                upper = np.prod([nodes[i] - nodes[o] for o in range(4) if o != i])
                lower = np.prod([nodes[m] - nodes[o] for o in range(4) if o != m])
                table[i, m] = upper / (lower * (nodes[i] - nodes[m]))
    return table, weights


def two_parts(matrix):
    upper = matrix.astype(np.float32).astype(jnp.bfloat16)
    lower = (matrix - upper.astype(np.float64)).astype(np.float32).astype(jnp.bfloat16)
    return upper, lower


@functools.lru_cache(maxsize=None)
def operators():
    table, weights = gll_tables()
    eye4, eye8 = np.eye(4), np.eye(8)
    along_cycle = np.kron(eye4, table.T)
    along_rows = np.kron(table.T, eye4)
    grad = np.concatenate([np.kron(eye8, along_cycle), np.kron(eye8, along_rows)], axis=1)
    weight = np.diag(np.outer(weights, weights).reshape(16))
    div = np.concatenate(
        [np.kron(eye8, along_cycle @ weight), np.kron(eye8, along_rows @ weight)], axis=0
    )
    join = np.eye(256)
    for place in range(15):
        for j in range(4):
            low, high = place * 16 + 4 * j + 3, place * 16 + 16 + 4 * j
            join[low, high] = 1.0
            join[high, low] = 1.0
    both = np.zeros((512, 256))
    both[:256, :128] = div
    both[256:, 128:] = div
    div_join = both @ join
    grad_hi, grad_lo = two_parts(grad)
    div_hi, div_lo = two_parts(div_join)
    return np.concatenate(
        [grad_hi, grad_hi, grad_lo, div_hi, div_lo, join.astype(jnp.bfloat16)], axis=0
    )


def dot(left, right):
    return jnp.dot(left, right, preferred_element_type=F32)


def dot_last(left, right):
    return lax.dot_general(left, right, (((1,), (1,)), ((), ())), preferred_element_type=F32)


def halves(value):
    upper = value.astype(BF16)
    lower = (value - upper.astype(F32)).astype(BF16)
    return upper, lower


def lane_iota(shape):
    return lax.broadcasted_iota(jnp.int32, shape, 1)


def row_iota(shape):
    return lax.broadcasted_iota(jnp.int32, shape, 0)


def one_step(local, index):
    hit = (row_iota((ELEMS_DEV, ELEMS_DEV)) == index) & local
    return hit.astype(F32).astype(BF16)


def wide(local):
    return jnp.broadcast_to(local.astype(F32), (8, ELEMS_DEV))


def chain_length(local, index, doublings):
    length = wide(local)
    step = one_step(local, index)
    for k in range(doublings):
        length = length + dot(length.astype(BF16), step)
        if k + 1 < doublings:
            step = dot(step, step).astype(BF16)
    return length


def local_lists(near):
    base = (lax.axis_index("curve") * N_COL + lax.axis_index("col")) * ELEMS_DEV
    index = near - base
    return index, (index >= 0) & (index < ELEMS_DEV)


def over_points(element_values):
    shape = (ELEMS_DEV, POINTS_DEV)
    spread = (lane_iota(shape) // 16 == row_iota(shape)).astype(F32).astype(BF16)
    return dot(element_values.astype(BF16), spread)[0:1].astype(jnp.int32)


def three_parts(value):
    first = value.astype(BF16)
    rest = value - first.astype(F32)
    second = rest.astype(BF16)
    return first, second, (rest - second.astype(F32)).astype(BF16)


def strip_kernel(
    state_ref, jacobian_ref, coriolis_ref, metric_ref, near_ref, slot_ref, far_ref, close_ref,
    values_ref, near, jac, cor, metric, slot, state, sems
):
    copies = [
        pltpu.make_async_copy(source, target, sems.at[i])
        for i, (source, target) in enumerate(
            [
                (near_ref, near),
                (state_ref, state),
                (jacobian_ref, jac),
                (coriolis_ref, cor),
                (metric_ref, metric),
                (slot_ref, slot),
            ]
        )
    ]
    for copy in copies:
        copy.start()
    copies[0].wait()
    index, local = local_lists(near[...])
    lower = wide(local[2:3])
    row = lower + dot(lower.astype(BF16), one_step(local[2:3], index[2:3])) + wide(~local[3:4])
    sides = []
    for side in range(2):
        here, there = local[side : side + 1], index[side : side + 1]
        second = dot(wide(here).astype(BF16), one_step(here, there))
        edge = wide(~here)
        sides.append((edge, wide(here) * (1.0 - second)))
    (first, second), (last, second_last) = sides
    unit = (first + second) * (2.0 * row + 1.0 + second)
    unit = unit + (last + second_last) * (2.0 * row + 9.0 + last)
    lane = (over_points(unit) - 1) * 16 + lane_iota((1, POINTS_DEV)) % 16
    row16 = row_iota((2 * LANES, POINTS_DEV)).astype(jnp.int16)
    hits = jnp.where(row16 == lane.astype(jnp.int16), jnp.bfloat16(1), jnp.bfloat16(0))
    for copy in copies[1:]:
        copy.wait()
    values = jnp.concatenate(
        [
            state[...].reshape(STATE, POINTS_DEV),
            jac[...].reshape(1, POINTS_DEV),
            cor[...].reshape(1, POINTS_DEV),
            metric[...],
            slot[...].astype(F32).reshape(1, POINTS_DEV),
            jnp.zeros((1, POINTS_DEV), F32),
        ],
        axis=0,
    )
    values_ref[0:TILE, :] = values
    values_ref[TILE:, 0:ELEMS_DEV] = jnp.where(local, index, -1).astype(F32)
    parts = dot_last(jnp.concatenate(halves(values), axis=0), hits)
    strips = parts[:TILE] + parts[TILE:]
    even = lax.rem(lax.axis_index("col"), 2) == 0
    to_left, to_right = strips[:, :LANES], strips[:, LANES:]
    far_ref[...] = jnp.where(even, to_left, to_right)
    close_ref[...] = jnp.where(even, to_right, to_left)


def arrange_kernel(values_ref, low_ref, high_ref, hits_ref):
    index = values_ref[TILE:, 0:ELEMS_DEV].astype(jnp.int32)
    local = index >= 0
    place = chain_length(local[0:1], index[0:1], 4)
    row = chain_length(local[2:3], index[2:3], 2)
    target = over_points(row * 16.0 + place + 2.0) * 16 + lane_iota((1, POINTS_DEV)) % 16
    hits = (row_iota((1024, POINTS_DEV)) == target).astype(F32).astype(BF16)
    hits_ref[...] = hits
    parts = dot_last(jnp.concatenate(three_parts(values_ref[0:TILE, :]), axis=0), hits)
    ordered = parts[0:TILE] + parts[TILE : 2 * TILE] + parts[2 * TILE :]
    for r in range(4):
        for g in range(2):
            block = ordered[:, (2 * r + g) * LANES : (2 * r + g + 1) * LANES]
            ref = low_ref if r < 2 else high_ref
            start = ((r % 2) * 2 + g) * TILE
            ref[start : start + TILE, :] = block


def turned(block, by):
    by = by % LANES
    return block if by == 0 else pltpu.roll(block, by, 1)


def margin_kernel(
    low_in, high_in, from_far, from_close, first_ref, second_ref, low_ref, high_ref
):
    lane = lane_iota((TILE, LANES))
    even = lax.rem(lax.axis_index("col"), 2) == 0
    from_left = jnp.where(even, from_far[...], from_close[...])
    from_right = jnp.where(even, from_close[...], from_far[...])
    halves_of_rows = []
    for source, start_row in ((low_in, 0), (high_in, 2)):
        blocks = []
        for r in range(2):
            turn = start_row + r
            start = r * 2 * TILE
            blocks.append(
                jnp.where(lane < 32, turned(from_left, -32 * turn), source[start : start + TILE, :])
            )
            start += TILE
            blocks.append(
                jnp.where(
                    lane >= 96, turned(from_right, 96 - 32 * turn), source[start : start + TILE, :]
                )
            )
        halves_of_rows.append(jnp.concatenate(blocks, axis=0))
    low, high = halves_of_rows
    low_ref[...] = low
    high_ref[...] = high
    even = lax.rem(lax.axis_index("curve"), 2) == 0
    first_ref[...] = jnp.where(even, high, low)
    second_ref[...] = jnp.where(even, low, high)


def send_lists(slots):
    square = (LANES, LANES)
    upto = (row_iota(square) <= lane_iota(square)).astype(F32)
    count = jnp.concatenate([upto, jnp.ones(square, F32)], axis=1).astype(BF16)
    lane = lane_iota((1, LANES))
    chosen, devices, withins, owns = [], [], [], []
    for i, slot in enumerate(slots):
        own = lane >= 32 if i % 2 == 0 else lane < 96
        device = jnp.where(own, jnp.floor((slot + 0.5) * (1.0 / POINTS_DEV)), -1.0)
        wanted = jnp.broadcast_to(device.astype(jnp.int32), (N_COL, LANES))
        chosen.append((wanted == row_iota((N_COL, LANES))).astype(F32))
        devices.append(device)
        withins.append(slot - device * POINTS_DEV)
        owns.append(own)
    counted = dot(jnp.concatenate(chosen, axis=0).astype(BF16), count)
    before = jnp.zeros((N_COL, LANES), F32)
    lists = []
    for i, (device, within, own) in enumerate(zip(devices, withins, owns)):
        rows = counted[i * N_COL : (i + 1) * N_COL]
        rank = jnp.sum((rows[:, :LANES] + before) * chosen[i], axis=0, keepdims=True) - 1.0
        before = before + rows[:, LANES:]
        third = (rank >= CAP_ROWS).astype(F32) + (rank >= 2 * CAP_ROWS).astype(F32)
        line = device * CAP_ROWS + rank - third * CAP_ROWS
        parts = [jnp.where(own & (third == float(k)), line + 1.0, 0.0) for k in range(3)]
        filler = jnp.zeros((4, LANES), F32)
        lists.append(
            jnp.concatenate(parts + [jnp.where(own, within + 1.0, 0.0), filler], axis=0)
        )
    return jnp.concatenate(lists, axis=1)


def fluxes(slope, coefficients):
    along_cycle, along_rows = slope[:, :LANES], slope[:, LANES:]
    caa, cab, cbb = coefficients
    return caa * along_cycle + cab * along_rows, cab * along_cycle + cbb * along_rows


def gradient(values, matrices):
    upper, lower = halves(values)
    return dot(jnp.concatenate([upper, lower], axis=1), matrices[0:256, :]) + dot(
        upper, matrices[256:384, :]
    )


def both_parts(upper, lower, matrix):
    count = upper.shape[0]
    result = dot(jnp.concatenate([upper, lower], axis=0), matrix)
    return result[:count] + result[count:]


def divergence_joined(values, matrices):
    upper, lower = halves(values)
    return both_parts(upper, lower, matrices[384:896, :]) + dot(upper, matrices[896:1408, :])


def rows_joined(below, here, above, low_mask, high_mask):
    parts = []
    for g in range(2):
        part = slice(g * LANES, (g + 1) * LANES)
        parts.append(
            here[:, part]
            + low_mask * turned(below[:, part], -12)
            + high_mask * turned(above[:, part], 12)
        )
    return parts


def row_starts(rows):
    slope, flux, plain = {}, {}, {}
    at = [0, 0, 0]
    for r in rows:
        lean = r in (0, 7)
        for g in range(2):
            slope[r, g] = at[0]
            at[0] += STATE if lean else TILE
        flux[r] = at[1]
        at[1] += STATE if lean else STATE + 16
        plain[r] = at[2]
        at[2] += 8 if lean else 32
    return slope, flux, plain, at


def local_terms(rows, tile, matrices, slopes, flux, plain, coefs, coefs_at):
    slope_at, flux_at, plain_at, _ = row_starts(rows)
    cells = [(r, g) for r in rows for g in range(2)]
    stacked = []
    for r, g in cells:
        stacked.append(tile(r, g, 0, STATE))
        if r not in (0, 7):
            zonal, meridional = tile(r, g, 0, 8), tile(r, g, 8, 8)
            energy = 0.5 * (zonal * zonal + meridional * meridional) + tile(r, g, 16, 8)
            stacked.append(energy)
    slopes[...] = gradient(jnp.concatenate(stacked, axis=0), matrices)
    lane = lane_iota((8, LANES))
    inner_i = (lane % 4 == 1) | (lane % 4 == 2)
    inner_j = (lane // 4 % 4 == 1) | (lane // 4 % 4 == 2)
    weight = jnp.where(inner_i, 5.0 / 6.0, 1.0 / 6.0) * jnp.where(inner_j, 5.0 / 6.0, 1.0 / 6.0)
    for r, g in cells:

        def line(k):
            return jnp.broadcast_to(tile(r, g, STATE + k, 1), (8, LANES))

        jacobian, coriolis = line(0), line(1)
        m11, m12, m21, m22 = 1.0 + line(2), line(3), line(4), 1.0 + line(5)
        caa = jacobian * (m11 * m11 + m12 * m12)
        cab = jacobian * (m11 * m21 + m12 * m22)
        cbb = jacobian * (m21 * m21 + m22 * m22)
        at = coefs_at(r, g)
        if at is not None:
            coefs[at : at + 8, :] = caa
            coefs[at + 8 : at + 16, :] = cab
            coefs[at + 16 : at + 24, :] = cbb
        mass = jacobian * weight
        at = slope_at[r, g]
        first = slice(g * 2 * LANES, (g * 2 + 1) * LANES)
        second = slice((g * 2 + 1) * LANES, (g * 2 + 2) * LANES)
        part = slice(g * LANES, (g + 1) * LANES)
        to, direct = flux_at[r], plain_at[r]
        for f in range(FIELDS):
            one, two = fluxes(slopes[at + 8 * f : at + 8 * f + 8, :], (caa, cab, cbb))
            flux[to + 8 * f : to + 8 * f + 8, first] = one
            flux[to + 8 * f : to + 8 * f + 8, second] = two
        plain[direct : direct + 8, part] = mass
        if r in (0, 7):
            continue
        zonal, meridional = tile(r, g, 0, 8), tile(r, g, 8, 8)
        flow1 = jacobian * (m11 * zonal + m12 * meridional)
        flow2 = jacobian * (m21 * zonal + m22 * meridional)
        for k in range(2):
            carried = tile(r, g, 24 + 8 * k, 8)
            flux[to + 40 + 8 * k : to + 48 + 8 * k, first] = carried * flow1
            flux[to + 40 + 8 * k : to + 48 + 8 * k, second] = carried * flow2
        ea, eb = slopes[at + 40 : at + 48, :LANES], slopes[at + 40 : at + 48, LANES:]
        ta, tb = slopes[at + 16 : at + 24, :LANES], slopes[at + 16 : at + 24, LANES:]
        plain[direct + 8 : direct + 16, part] = mass * (
            coriolis * meridional - (m11 * ea + m21 * eb)
        )
        plain[direct + 16 : direct + 24, part] = -mass * (
            coriolis * zonal + (m12 * ea + m22 * eb)
        )
        plain[direct + 24 : direct + 32, part] = -mass * (
            zonal * (m11 * ta + m21 * tb) + meridional * (m12 * ta + m22 * tb)
        )
    spread = divergence_joined(flux[...], matrices)
    upper, lower = halves(plain[...])
    return spread, both_parts(upper, lower, matrices[1408:1664, :])


def face_masks():
    lane = lane_iota((1, LANES)) % 16
    return (lane < 4).astype(F32), (lane >= 12).astype(F32)


def repeated(block):
    return jnp.concatenate([block] * FIELDS, axis=0)


def second_laplacian(rows, smoothing, inverse, coefficients, matrices):
    smooth = [smoothing[r][g] * repeated(inverse[r, g]) for r in rows for g in range(2)]
    again = gradient(jnp.concatenate(smooth, axis=0), matrices)
    flat = []
    for n, r in enumerate(rows):
        parts = []
        for g in range(2):
            triple = tuple(repeated(coefficients(r, g, k)) for k in range(3))
            start = (2 * n + g) * STATE
            parts += list(fluxes(again[start : start + STATE, :], triple))
        flat.append(jnp.concatenate(parts, axis=1))
    return divergence_joined(jnp.concatenate(flat, axis=0), matrices)


def mass_inverse(mass_sum):
    return 1.0 / jnp.where(mass_sum > 0.0, mass_sum, 1.0)


def advanced(state, straight, carried, inverse):
    return state + (TIME_STEP * jnp.concatenate([straight, -carried], axis=0)) * repeated(inverse)


OWN_ROWS = (2, 3, 4, 5)
OUTER_ROWS = (0, 1, 6, 7)
MIDDLE_ROWS = (3, 4)
EDGE_ROWS = (1, 2, 5, 6)


def inner_kernel(
    low_ref,
    high_ref,
    matrices,
    lists_ref,
    spread_ref,
    direct_ref,
    coefs,
    picks_ref,
    middle_ref,
    damped_ref,
    inverse_ref,
    slopes,
    flux,
    plain,
):
    def tile(r, g, start=0, size=TILE):
        offset = ((r % 2) * 2 + g) * TILE + start
        return (low_ref if r < 4 else high_ref)[offset : offset + size, :]

    def coefs_at(r, g):
        return (2 * (r - 2) + g) * 24

    lists = send_lists([tile(r, g, STATE + 6, 1) for r in OWN_ROWS for g in range(2)])
    lists_ref[...] = lists
    line = (lists[0:1] + lists[1:2] + lists[2:3]).astype(jnp.int32) - 1
    picks_ref[...] = (row_iota((POINTS_DEV, 1024)) == line).astype(F32).astype(BF16)
    spread, direct = local_terms(
        OWN_ROWS, tile, matrices, slopes, flux, plain, coefs, coefs_at
    )
    spread_ref[...] = spread
    direct_ref[...] = direct
    masks = face_masks()

    def joined(value, size, r, start, count):
        def rows(k):
            at = (k - 2) * size + start
            return value[at : at + count, :]

        return rows_joined(rows(r - 1), rows(r), rows(r + 1), *masks)

    inverse, smoothing = {}, {}
    for r in MIDDLE_ROWS:
        mass_sum = joined(direct, 32, r, 0, 8)
        smoothing[r] = joined(spread, 56, r, 0, STATE)
        straight = joined(direct, 32, r, 8, 24)
        carried = joined(spread, 56, r, STATE, 16)
        for g in range(2):
            inverse[r, g] = mass_inverse(mass_sum[g])
            at = 2 * (r - 3) + g
            inverse_ref[8 * at : 8 * at + 8, :] = inverse[r, g]
            middle_ref[STATE * at : STATE * at + STATE, :] = advanced(
                tile(r, g, 0, STATE), straight[g], carried[g], inverse[r, g]
            )

    def coefficients(r, g, k):
        return coefs[coefs_at(r, g) + 8 * k : coefs_at(r, g) + 8 * k + 8, :]

    damped_ref[...] = second_laplacian(MIDDLE_ROWS, smoothing, inverse, coefficients, matrices)


def section_kernel(
    first_far_ref,
    second_far_ref,
    low_ref,
    high_ref,
    lists_ref,
    picks_ref,
    matrices,
    inner_spread,
    inner_direct,
    inner_coefs,
    middle_ref,
    middle_damped,
    middle_inverse,
    whole_ref,
    send_ref,
    outside,
    slopes,
    flux,
    plain,
    outer_coefs,
):
    even = lax.rem(lax.axis_index("curve"), 2) == 0
    outside[0] = jnp.where(even, second_far_ref[...], first_far_ref[...])
    outside[1] = jnp.where(even, first_far_ref[...], second_far_ref[...])

    def tile(r, g, start=0, size=TILE):
        offset = ((r % 2) * 2 + g) * TILE + start
        if r in OUTER_ROWS:
            return outside[r // 6, offset : offset + size, :]
        return (low_ref if r < 4 else high_ref)[offset : offset + size, :]

    outer_spread, outer_direct = local_terms(
        OUTER_ROWS,
        tile,
        matrices,
        slopes,
        flux,
        plain,
        outer_coefs,
        lambda r, g: {1: 24 * g, 6: 48 + 24 * g}.get(r),
    )
    masks = face_masks()
    _, outer_flux_at, outer_plain_at, _ = row_starts(OUTER_ROWS)
    _, inner_flux_at, inner_plain_at, _ = row_starts(OWN_ROWS)

    def joined(spread, r, start, count):
        def rows(k):
            if k in OUTER_ROWS:
                at = (outer_flux_at if spread else outer_plain_at)[k] + start
                return (outer_spread if spread else outer_direct)[at : at + count, :]
            at = (inner_flux_at if spread else inner_plain_at)[k] + start
            return (inner_spread if spread else inner_direct)[at : at + count, :]

        return rows_joined(rows(r - 1), rows(r), rows(r + 1), *masks)

    def coefficients(r, g, k):
        if r in OUTER_ROWS:
            at = (0 if r == 1 else 48) + 24 * g + 8 * k
            return outer_coefs[at : at + 8, :]
        at = (2 * (r - 2) + g) * 24 + 8 * k
        return inner_coefs[at : at + 8, :]

    inverse, smoothing = {}, {}
    for r in EDGE_ROWS:
        mass_sum = joined(False, r, 0, 8)
        smoothing[r] = joined(True, r, 0, STATE)
        for g in range(2):
            inverse[r, g] = mass_inverse(mass_sum[g])
    for r in MIDDLE_ROWS:
        for g in range(2):
            at = 8 * (2 * (r - 3) + g)
            inverse[r, g] = middle_inverse[at : at + 8, :]
    damped = second_laplacian(EDGE_ROWS, smoothing, inverse, coefficients, matrices)

    def damped_row(r):
        if r in MIDDLE_ROWS:
            return middle_damped[(r - 3) * STATE : (r - 2) * STATE, :]
        at = EDGE_ROWS.index(r) * STATE
        return damped[at : at + STATE, :]

    ordered = []
    for r in OWN_ROWS:
        damping = rows_joined(damped_row(r - 1), damped_row(r), damped_row(r + 1), *masks)
        if r not in MIDDLE_ROWS:
            straight = joined(False, r, 8, 24)
            carried = joined(True, r, STATE, 16)
        for g in range(2):
            if r in MIDDLE_ROWS:
                at = STATE * (2 * (r - 3) + g)
                base = middle_ref[at : at + STATE, :]
            else:
                base = advanced(tile(r, g, 0, STATE), straight[g], carried[g], inverse[r, g])
            ordered.append(
                base - ((TIME_STEP * HYPER_NU) * damping[g]) * repeated(inverse[r, g])
            )
    whole = jnp.concatenate(ordered, axis=1)
    whole_ref[...] = whole
    shares = [(lists_ref[k : k + 1, :] > 0.0).astype(F32) for k in range(3)]
    slots = [jnp.broadcast_to(lists_ref[3:4, :] * shares[k], (8, 1024)) for k in range(3)]
    row = row_iota((8, 1024))
    slot_rows = sum(jnp.where(row == k, slots[k], 0.0) for k in range(3))
    columns = jnp.concatenate([whole * share for share in shares] + [slot_rows], axis=0)
    upper, lower = halves(columns)
    sent = dot_last(picks_ref[...], jnp.concatenate([upper, lower], axis=0))
    send_ref[...] = sent[:, :LANES] + sent[:, LANES:]


def receive_kernel(
    received_ref, whole_ref, hits_ref, updated_ref, physics_ref, updated, pieces, sems
):
    whole = whole_ref[...]
    upper = whole.astype(BF16).astype(F32)
    restored = dot(jnp.concatenate([upper, whole - upper], axis=0).astype(BF16), hits_ref[...])
    updated[...] = restored[:STATE] + restored[STATE:]
    copies = [pltpu.make_async_copy(updated, updated_ref, sems.at[3])]
    copies[0].start()
    turned_over = received_ref[...].T
    upper, lower = halves(turned_over)
    places = slice(3 * STATE, 3 * STATE + 3)
    slot = turned_over[places, :].astype(jnp.int32) - 1
    slots = [slot[k : k + 1].astype(jnp.int16) for k in range(3)]
    both = jnp.concatenate([upper, lower], axis=0)
    count = 2 * LANES
    for start in range(0, POINTS_DEV, count):
        row = (row_iota((count, POINTS_DEV)) + start).astype(jnp.int16)
        hits = (row == slots[0]) | (row == slots[1]) | (row == slots[2])
        rows = dot_last(both, jnp.where(hits, jnp.bfloat16(1), jnp.bfloat16(0)))
        rows = rows[:LANES] + rows[LANES:]
        own = rows[places, :] == (lane_iota((3, count)) + (start + 1)).astype(F32)
        piece = start // count
        pieces[piece] = jnp.where(
            own[0:1],
            rows[:STATE],
            jnp.where(own[1:2], rows[STATE : 2 * STATE], rows[2 * STATE : 3 * STATE]),
        )
        copies.append(
            pltpu.make_async_copy(
                pieces.at[piece], physics_ref.at[:, pl.ds(start, count)], sems.at[piece]
            )
        )
        copies[-1].start()
    for copy in copies:
        copy.wait()


def call(kernel, shapes, scratch=(), flops=0, moved=0, vmem=VMEM_LIMIT, **specs):
    return pl.pallas_call(
        kernel,
        out_shape=[
            jax.ShapeDtypeStruct(*s) if isinstance(s, tuple) else s for s in shapes
        ],
        scratch_shapes=list(scratch),
        **specs,
        compiler_params=pltpu.CompilerParams(vmem_limit_bytes=vmem),
        cost_estimate=pl.CostEstimate(flops=flops, bytes_accessed=moved, transcendentals=0),
    )


def swaps(count, pairs_from):
    route = []
    for i in range(pairs_from, count - 1, 2):
        route += [(i, i + 1), (i + 1, i)]
    return route


def body(
    evolving_state_array, point_id, neighbours, jacobian, inverse_metric, coriolis, column_slot
):
    anywhere = pl.BlockSpec(memory_space=pltpu.HBM)
    half = ((4 * TILE, LANES), F32)
    strip = ((TILE, LANES), F32)
    values_shape = ((TILE + 8, POINTS_DEV), F32)
    far, close, values = call(
        strip_kernel,
        [pltpu.VMEM(*strip), pltpu.VMEM(*strip), pltpu.VMEM(*values_shape)],
        scratch=[
            pltpu.VMEM((8, ELEMS_DEV), jnp.int32),
            pltpu.VMEM((POINTS_DEV,), F32),
            pltpu.VMEM((POINTS_DEV,), F32),
            pltpu.VMEM((4, POINTS_DEV), F32),
            pltpu.VMEM((POINTS_DEV,), jnp.int32),
            pltpu.VMEM((FIELDS, LEV, POINTS_DEV), F32),
            pltpu.SemaphoreType.DMA((6,)),
        ],
        in_specs=[anywhere] * 6,
        vmem=64 * 1024 * 1024 - 524288,
    )(evolving_state_array, jacobian, coriolis, inverse_metric, neighbours, column_slot)
    cols, rows = lax.axis_size("col"), lax.axis_size("curve")
    from_far = lax.ppermute(far, "col", swaps(cols, 1) + [(cols - 1, 0), (0, cols - 1)])
    from_close = lax.ppermute(close, "col", swaps(cols, 0))
    low, high, hits = call(
        arrange_kernel,
        [half, half, pltpu.VMEM((1024, POINTS_DEV), BF16)],
        flops=400_000_000,
        moved=1_000_000,
    )(values)
    first, second, low, high = call(margin_kernel, [half] * 4)(low, high, from_far, from_close)
    second_far = lax.ppermute(second, "curve", swaps(rows, 1))
    first_far = lax.ppermute(first, "curve", swaps(rows, 0))
    matrices = jnp.asarray(operators())
    def scratch(rows):
        slope_rows, flux_rows, plain_rows = row_starts(rows)[3]
        return [
            pltpu.VMEM((slope_rows, 2 * LANES), F32),
            pltpu.VMEM((flux_rows, 4 * LANES), F32),
            pltpu.VMEM((plain_rows, 2 * LANES), F32),
        ]

    inner = call(
        inner_kernel,
        [
            ((8, 1024), F32),
            ((4 * 56, 2 * LANES), F32),
            ((4 * 32, 2 * LANES), F32),
            ((8 * 24, LANES), F32),
            ((POINTS_DEV, 1024), BF16),
            ((4 * STATE, LANES), F32),
            ((2 * STATE, 2 * LANES), F32),
            ((4 * 8, LANES), F32),
        ],
        scratch=scratch(OWN_ROWS),
        flops=400_000_000,
        moved=1_000_000,
    )(low, high, matrices)
    lists, spread, direct, coefs, picks, middle, middle_damped, middle_inverse = inner
    whole, sent = call(
        section_kernel,
        [((STATE, 1024), F32), ((POINTS_DEV, LANES), F32)],
        scratch=[pltpu.VMEM((2, 4 * TILE, LANES), F32)]
        + scratch(OUTER_ROWS)
        + [pltpu.VMEM((4 * 24, LANES), F32)],
    )(
        first_far,
        second_far,
        low,
        high,
        lists,
        picks,
        matrices,
        spread,
        direct,
        coefs,
        middle,
        middle_damped,
        middle_inverse,
    )
    received = lax.all_to_all(sent, "col", split_axis=0, concat_axis=0, tiled=True)
    updated, physics = call(
        receive_kernel,
        [((STATE, POINTS_DEV), F32)] * 2,
        scratch=[
            pltpu.VMEM((STATE, POINTS_DEV), F32),
            pltpu.VMEM((3, STATE, 2 * LANES), F32),
            pltpu.SemaphoreType.DMA((4,)),
        ],
        in_specs=[pl.BlockSpec(memory_space=pltpu.VMEM)] * 3,
        out_specs=[anywhere] * 2,
    )(received, whole, hits)
    shape = evolving_state_array.shape
    return updated.reshape(shape), physics.reshape(shape)


def solution(mesh):
    split = ("curve", "col")
    return jax.shard_map(
        body,
        mesh=mesh,
        in_specs=(
            P(None, None, split),
            P(split),
            P(None, split),
            P(split),
            P(None, split),
            P(split),
            P(split),
        ),
        out_specs=(P(None, None, split), P(None, None, split)),
        check_vma=False,
    )
```

```python
import functools
import math

import jax
import jax.numpy as jnp
import numpy as np
from jax import lax
from jax.experimental import pallas as pl
from jax.experimental.pallas import tpu as pltpu
from jax.sharding import PartitionSpec as P

FIELDS = 5
LEV = 8
STATE = FIELDS * LEV
TILE = 48
LANES = 128
ELEMS_DEV = 48
POINTS_DEV = 768
N_COL = 32
CAP = 72
CAP_ROWS = CAP // 3
TIME_STEP = 0.1
HYPER_NU = 0.002
F32 = jnp.float32
BF16 = jnp.bfloat16
VMEM_LIMIT = 32 * 1024 * 1024


def gll_tables():
    root_fifth = 1.0 / math.sqrt(5.0)
    nodes = np.array([-1.0, -root_fifth, root_fifth, 1.0])
    weights = np.array([1.0, 5.0, 5.0, 1.0]) / 6.0
    table = np.zeros((4, 4))
    for i in range(4):
        for m in range(4):
            if i == m:
                table[i, m] = sum(1.0 / (nodes[i] - nodes[o]) for o in range(4) if o != i)
            else:
                upper = np.prod([nodes[i] - nodes[o] for o in range(4) if o != i])
                lower = np.prod([nodes[m] - nodes[o] for o in range(4) if o != m])
                table[i, m] = upper / (lower * (nodes[i] - nodes[m]))
    return table, weights


def two_parts(matrix):
    upper = matrix.astype(np.float32).astype(jnp.bfloat16)
    lower = (matrix - upper.astype(np.float64)).astype(np.float32).astype(jnp.bfloat16)
    return upper, lower


@functools.lru_cache(maxsize=None)
def operators():
    table, weights = gll_tables()
    eye4, eye8 = np.eye(4), np.eye(8)
    along_cycle = np.kron(eye4, table.T)
    along_rows = np.kron(table.T, eye4)
    grad = np.concatenate([np.kron(eye8, along_cycle), np.kron(eye8, along_rows)], axis=1)
    weight = np.diag(np.outer(weights, weights).reshape(16))
    div = np.concatenate(
        [np.kron(eye8, along_cycle @ weight), np.kron(eye8, along_rows @ weight)], axis=0
    )
    join = np.eye(256)
    for place in range(15):
        for j in range(4):
            low, high = place * 16 + 4 * j + 3, place * 16 + 16 + 4 * j
            join[low, high] = 1.0
            join[high, low] = 1.0
    both = np.zeros((512, 256))
    both[:256, :128] = div
    both[256:, 128:] = div
    div_join = both @ join
    grad_hi, grad_lo = two_parts(grad)
    div_hi, div_lo = two_parts(div_join)
    return np.concatenate(
        [grad_hi, grad_hi, grad_lo, div_hi, div_lo, join.astype(jnp.bfloat16)], axis=0
    )


def dot(left, right):
    return jnp.dot(left, right, preferred_element_type=F32)


def dot_last(left, right):
    return lax.dot_general(left, right, (((1,), (1,)), ((), ())), preferred_element_type=F32)


def halves(value):
    upper = value.astype(BF16)
    lower = (value - upper.astype(F32)).astype(BF16)
    return upper, lower


def lane_iota(shape):
    return lax.broadcasted_iota(jnp.int32, shape, 1)


def row_iota(shape):
    return lax.broadcasted_iota(jnp.int32, shape, 0)


def one_step(local, index):
    hit = (row_iota((ELEMS_DEV, ELEMS_DEV)) == index) & local
    return hit.astype(F32).astype(BF16)


def wide(local):
    return jnp.broadcast_to(local.astype(F32), (8, ELEMS_DEV))


def chain_length(local, index, doublings):
    length = wide(local)
    step = one_step(local, index)
    for k in range(doublings):
        length = length + dot(length.astype(BF16), step)
        if k + 1 < doublings:
            step = dot(step, step).astype(BF16)
    return length


def local_lists(near):
    base = (lax.axis_index("curve") * N_COL + lax.axis_index("col")) * ELEMS_DEV
    index = near - base
    return index, (index >= 0) & (index < ELEMS_DEV)


def over_points(element_values):
    shape = (ELEMS_DEV, POINTS_DEV)
    spread = (lane_iota(shape) // 16 == row_iota(shape)).astype(F32).astype(BF16)
    return dot(element_values.astype(BF16), spread)[0:1].astype(jnp.int32)


def three_parts(value):
    first = value.astype(BF16)
    rest = value - first.astype(F32)
    second = rest.astype(BF16)
    return first, second, (rest - second.astype(F32)).astype(BF16)


def strip_kernel(
    state_ref, jacobian_ref, coriolis_ref, metric_ref, near_ref, slot_ref, far_ref, close_ref,
    values_ref, near, jac, cor, metric, slot, state, sems
):
    copies = [
        pltpu.make_async_copy(source, target, sems.at[i])
        for i, (source, target) in enumerate(
            [
                (near_ref, near),
                (state_ref, state),
                (jacobian_ref, jac),
                (coriolis_ref, cor),
                (metric_ref, metric),
                (slot_ref, slot),
            ]
        )
    ]
    for copy in copies:
        copy.start()
    copies[0].wait()
    index, local = local_lists(near[...])
    lower = wide(local[2:3])
    row = lower + dot(lower.astype(BF16), one_step(local[2:3], index[2:3])) + wide(~local[3:4])
    sides = []
    for side in range(2):
        here, there = local[side : side + 1], index[side : side + 1]
        second = dot(wide(here).astype(BF16), one_step(here, there))
        edge = wide(~here)
        sides.append((edge, wide(here) * (1.0 - second)))
    (first, second), (last, second_last) = sides
    unit = (first + second) * (2.0 * row + 1.0 + second)
    unit = unit + (last + second_last) * (2.0 * row + 9.0 + last)
    lane = (over_points(unit) - 1) * 16 + lane_iota((1, POINTS_DEV)) % 16
    row16 = row_iota((2 * LANES, POINTS_DEV)).astype(jnp.int16)
    hits = jnp.where(row16 == lane.astype(jnp.int16), jnp.bfloat16(1), jnp.bfloat16(0))
    for copy in copies[1:]:
        copy.wait()
    values = jnp.concatenate(
        [
            state[...].reshape(STATE, POINTS_DEV),
            jac[...].reshape(1, POINTS_DEV),
            cor[...].reshape(1, POINTS_DEV),
            metric[...],
            slot[...].astype(F32).reshape(1, POINTS_DEV),
            jnp.zeros((1, POINTS_DEV), F32),
        ],
        axis=0,
    )
    values_ref[0:TILE, :] = values
    values_ref[TILE:, 0:ELEMS_DEV] = jnp.where(local, index, -1).astype(F32)
    parts = dot_last(jnp.concatenate(halves(values), axis=0), hits)
    strips = parts[:TILE] + parts[TILE:]
    even = lax.rem(lax.axis_index("col"), 2) == 0
    to_left, to_right = strips[:, :LANES], strips[:, LANES:]
    far_ref[...] = jnp.where(even, to_left, to_right)
    close_ref[...] = jnp.where(even, to_right, to_left)


def arrange_kernel(values_ref, low_ref, high_ref, hits_ref):
    index = values_ref[TILE:, 0:ELEMS_DEV].astype(jnp.int32)
    local = index >= 0
    place = chain_length(local[0:1], index[0:1], 4)
    row = chain_length(local[2:3], index[2:3], 2)
    target = over_points(row * 16.0 + place + 2.0) * 16 + lane_iota((1, POINTS_DEV)) % 16
    row16 = row_iota((1024, POINTS_DEV)).astype(jnp.int16)
    hits = jnp.where(row16 == target.astype(jnp.int16), jnp.bfloat16(1), jnp.bfloat16(0))
    hits_ref[...] = hits
    parts = dot_last(jnp.concatenate(halves(values_ref[0:TILE, :]), axis=0), hits)
    ordered = parts[:TILE] + parts[TILE:]
    for r in range(4):
        for g in range(2):
            block = ordered[:, (2 * r + g) * LANES : (2 * r + g + 1) * LANES]
            ref = low_ref if r < 2 else high_ref
            start = ((r % 2) * 2 + g) * TILE
            ref[start : start + TILE, :] = block


def turned(block, by):
    by = by % LANES
    return block if by == 0 else pltpu.roll(block, by, 1)


def margin_kernel(
    low_in, high_in, from_far, from_close, first_ref, second_ref, low_ref, high_ref
):
    lane = lane_iota((TILE, LANES))
    even = lax.rem(lax.axis_index("col"), 2) == 0
    from_left = jnp.where(even, from_far[...], from_close[...])
    from_right = jnp.where(even, from_close[...], from_far[...])
    halves_of_rows = []
    for source, start_row in ((low_in, 0), (high_in, 2)):
        blocks = []
        for r in range(2):
            turn = start_row + r
            start = r * 2 * TILE
            blocks.append(
                jnp.where(lane < 32, turned(from_left, -32 * turn), source[start : start + TILE, :])
            )
            start += TILE
            blocks.append(
                jnp.where(
                    lane >= 96, turned(from_right, 96 - 32 * turn), source[start : start + TILE, :]
                )
            )
        halves_of_rows.append(jnp.concatenate(blocks, axis=0))
    low, high = halves_of_rows
    low_ref[...] = low
    high_ref[...] = high
    even = lax.rem(lax.axis_index("curve"), 2) == 0
    first_ref[...] = jnp.where(even, high, low)
    second_ref[...] = jnp.where(even, low, high)


def send_lists(slots):
    square = (LANES, LANES)
    upto = (row_iota(square) <= lane_iota(square)).astype(F32)
    count = jnp.concatenate([upto, jnp.ones(square, F32)], axis=1).astype(BF16)
    lane = lane_iota((1, LANES))
    chosen, devices, withins, owns = [], [], [], []
    for i, slot in enumerate(slots):
        own = lane >= 32 if i % 2 == 0 else lane < 96
        device = jnp.where(own, jnp.floor((slot + 0.5) * (1.0 / POINTS_DEV)), -1.0)
        wanted = jnp.broadcast_to(device.astype(jnp.int32), (N_COL, LANES))
        chosen.append((wanted == row_iota((N_COL, LANES))).astype(F32))
        devices.append(device)
        withins.append(slot - device * POINTS_DEV)
        owns.append(own)
    counted = dot(jnp.concatenate(chosen, axis=0).astype(BF16), count)
    before = jnp.zeros((N_COL, LANES), F32)
    lists = []
    for i, (device, within, own) in enumerate(zip(devices, withins, owns)):
        rows = counted[i * N_COL : (i + 1) * N_COL]
        rank = jnp.sum((rows[:, :LANES] + before) * chosen[i], axis=0, keepdims=True) - 1.0
        before = before + rows[:, LANES:]
        third = (rank >= CAP_ROWS).astype(F32) + (rank >= 2 * CAP_ROWS).astype(F32)
        line = device * CAP_ROWS + rank - third * CAP_ROWS
        parts = [jnp.where(own & (third == float(k)), line + 1.0, 0.0) for k in range(3)]
        filler = jnp.zeros((4, LANES), F32)
        lists.append(
            jnp.concatenate(parts + [jnp.where(own, within + 1.0, 0.0), filler], axis=0)
        )
    return jnp.concatenate(lists, axis=1)


def fluxes(slope, coefficients):
    along_cycle, along_rows = slope[:, :LANES], slope[:, LANES:]
    caa, cab, cbb = coefficients
    return caa * along_cycle + cab * along_rows, cab * along_cycle + cbb * along_rows


def gradient(values, matrices):
    upper, lower = halves(values)
    return dot(jnp.concatenate([upper, lower], axis=1), matrices[0:256, :]) + dot(
        upper, matrices[256:384, :]
    )


def both_parts(upper, lower, matrix):
    count = upper.shape[0]
    result = dot(jnp.concatenate([upper, lower], axis=0), matrix)
    return result[:count] + result[count:]


def divergence_joined(values, matrices):
    upper, lower = halves(values)
    return both_parts(upper, lower, matrices[384:896, :]) + dot(upper, matrices[896:1408, :])


def rows_joined(below, here, above, low_mask, high_mask):
    parts = []
    for g in range(2):
        part = slice(g * LANES, (g + 1) * LANES)
        parts.append(
            here[:, part]
            + low_mask * turned(below[:, part], -12)
            + high_mask * turned(above[:, part], 12)
        )
    return parts


def row_starts(rows):
    slope, flux, plain = {}, {}, {}
    at = [0, 0, 0]
    for r in rows:
        lean = r in (0, 7)
        for g in range(2):
            slope[r, g] = at[0]
            at[0] += STATE if lean else TILE
        flux[r] = at[1]
        at[1] += STATE if lean else STATE + 16
        plain[r] = at[2]
        at[2] += 8 if lean else 32
    return slope, flux, plain, at


def local_terms(rows, tile, matrices, slopes, flux, plain, coefs, coefs_at):
    slope_at, flux_at, plain_at, _ = row_starts(rows)
    cells = [(r, g) for r in rows for g in range(2)]
    stacked = []
    for r, g in cells:
        stacked.append(tile(r, g, 0, STATE))
        if r not in (0, 7):
            zonal, meridional = tile(r, g, 0, 8), tile(r, g, 8, 8)
            energy = 0.5 * (zonal * zonal + meridional * meridional) + tile(r, g, 16, 8)
            stacked.append(energy)
    slopes[...] = gradient(jnp.concatenate(stacked, axis=0), matrices)
    lane = lane_iota((8, LANES))
    inner_i = (lane % 4 == 1) | (lane % 4 == 2)
    inner_j = (lane // 4 % 4 == 1) | (lane // 4 % 4 == 2)
    weight = jnp.where(inner_i, 5.0 / 6.0, 1.0 / 6.0) * jnp.where(inner_j, 5.0 / 6.0, 1.0 / 6.0)
    for r, g in cells:

        def line(k):
            return jnp.broadcast_to(tile(r, g, STATE + k, 1), (8, LANES))

        jacobian, coriolis = line(0), line(1)
        m11, m12, m21, m22 = 1.0 + line(2), line(3), line(4), 1.0 + line(5)
        caa = jacobian * (m11 * m11 + m12 * m12)
        cab = jacobian * (m11 * m21 + m12 * m22)
        cbb = jacobian * (m21 * m21 + m22 * m22)
        at = coefs_at(r, g)
        if at is not None:
            coefs[at : at + 8, :] = caa
            coefs[at + 8 : at + 16, :] = cab
            coefs[at + 16 : at + 24, :] = cbb
        mass = jacobian * weight
        at = slope_at[r, g]
        first = slice(g * 2 * LANES, (g * 2 + 1) * LANES)
        second = slice((g * 2 + 1) * LANES, (g * 2 + 2) * LANES)
        part = slice(g * LANES, (g + 1) * LANES)
        to, direct = flux_at[r], plain_at[r]
        for f in range(FIELDS):
            one, two = fluxes(slopes[at + 8 * f : at + 8 * f + 8, :], (caa, cab, cbb))
            flux[to + 8 * f : to + 8 * f + 8, first] = one
            flux[to + 8 * f : to + 8 * f + 8, second] = two
        plain[direct : direct + 8, part] = mass
        if r in (0, 7):
            continue
        zonal, meridional = tile(r, g, 0, 8), tile(r, g, 8, 8)
        flow1 = jacobian * (m11 * zonal + m12 * meridional)
        flow2 = jacobian * (m21 * zonal + m22 * meridional)
        for k in range(2):
            carried = tile(r, g, 24 + 8 * k, 8)
            flux[to + 40 + 8 * k : to + 48 + 8 * k, first] = carried * flow1
            flux[to + 40 + 8 * k : to + 48 + 8 * k, second] = carried * flow2
        ea, eb = slopes[at + 40 : at + 48, :LANES], slopes[at + 40 : at + 48, LANES:]
        ta, tb = slopes[at + 16 : at + 24, :LANES], slopes[at + 16 : at + 24, LANES:]
        plain[direct + 8 : direct + 16, part] = mass * (
            coriolis * meridional - (m11 * ea + m21 * eb)
        )
        plain[direct + 16 : direct + 24, part] = -mass * (
            coriolis * zonal + (m12 * ea + m22 * eb)
        )
        plain[direct + 24 : direct + 32, part] = -mass * (
            zonal * (m11 * ta + m21 * tb) + meridional * (m12 * ta + m22 * tb)
        )
    spread = divergence_joined(flux[...], matrices)
    upper, lower = halves(plain[...])
    return spread, both_parts(upper, lower, matrices[1408:1664, :])


def face_masks():
    lane = lane_iota((1, LANES)) % 16
    return (lane < 4).astype(F32), (lane >= 12).astype(F32)


def repeated(block):
    return jnp.concatenate([block] * FIELDS, axis=0)


def second_laplacian(rows, smoothing, inverse, coefficients, matrices):
    smooth = [smoothing[r][g] * repeated(inverse[r, g]) for r in rows for g in range(2)]
    again = gradient(jnp.concatenate(smooth, axis=0), matrices)
    flat = []
    for n, r in enumerate(rows):
        parts = []
        for g in range(2):
            triple = tuple(repeated(coefficients(r, g, k)) for k in range(3))
            start = (2 * n + g) * STATE
            parts += list(fluxes(again[start : start + STATE, :], triple))
        flat.append(jnp.concatenate(parts, axis=1))
    return divergence_joined(jnp.concatenate(flat, axis=0), matrices)


def mass_inverse(mass_sum):
    return 1.0 / jnp.where(mass_sum > 0.0, mass_sum, 1.0)


def advanced(state, straight, carried, inverse):
    return state + (TIME_STEP * jnp.concatenate([straight, -carried], axis=0)) * repeated(inverse)


OWN_ROWS = (2, 3, 4, 5)
OUTER_ROWS = (0, 1, 6, 7)
MIDDLE_ROWS = (3, 4)
EDGE_ROWS = (1, 2, 5, 6)


def inner_kernel(
    low_ref,
    high_ref,
    matrices,
    lists_ref,
    spread_ref,
    direct_ref,
    coefs,
    picks_ref,
    middle_ref,
    damped_ref,
    inverse_ref,
    slopes,
    flux,
    plain,
):
    def tile(r, g, start=0, size=TILE):
        offset = ((r % 2) * 2 + g) * TILE + start
        return (low_ref if r < 4 else high_ref)[offset : offset + size, :]

    def coefs_at(r, g):
        return (2 * (r - 2) + g) * 24

    lists = send_lists([tile(r, g, STATE + 6, 1) for r in OWN_ROWS for g in range(2)])
    lists_ref[...] = lists
    line = (lists[0:1] + lists[1:2] + lists[2:3]).astype(jnp.int32) - 1
    picks_ref[...] = (row_iota((POINTS_DEV, 1024)) == line).astype(F32).astype(BF16)
    spread, direct = local_terms(
        OWN_ROWS, tile, matrices, slopes, flux, plain, coefs, coefs_at
    )
    spread_ref[...] = spread
    direct_ref[...] = direct
    masks = face_masks()

    def joined(value, size, r, start, count):
        def rows(k):
            at = (k - 2) * size + start
            return value[at : at + count, :]

        return rows_joined(rows(r - 1), rows(r), rows(r + 1), *masks)

    inverse, smoothing = {}, {}
    for r in MIDDLE_ROWS:
        mass_sum = joined(direct, 32, r, 0, 8)
        smoothing[r] = joined(spread, 56, r, 0, STATE)
        straight = joined(direct, 32, r, 8, 24)
        carried = joined(spread, 56, r, STATE, 16)
        for g in range(2):
            inverse[r, g] = mass_inverse(mass_sum[g])
            at = 2 * (r - 3) + g
            inverse_ref[8 * at : 8 * at + 8, :] = inverse[r, g]
            middle_ref[STATE * at : STATE * at + STATE, :] = advanced(
                tile(r, g, 0, STATE), straight[g], carried[g], inverse[r, g]
            )

    def coefficients(r, g, k):
        return coefs[coefs_at(r, g) + 8 * k : coefs_at(r, g) + 8 * k + 8, :]

    damped_ref[...] = second_laplacian(MIDDLE_ROWS, smoothing, inverse, coefficients, matrices)


def section_kernel(
    first_far_ref,
    second_far_ref,
    low_ref,
    high_ref,
    lists_ref,
    picks_ref,
    matrices,
    inner_spread,
    inner_direct,
    inner_coefs,
    middle_ref,
    middle_damped,
    middle_inverse,
    whole_ref,
    send_ref,
    outside,
    slopes,
    flux,
    plain,
    outer_coefs,
):
    even = lax.rem(lax.axis_index("curve"), 2) == 0
    outside[0] = jnp.where(even, second_far_ref[...], first_far_ref[...])
    outside[1] = jnp.where(even, first_far_ref[...], second_far_ref[...])

    def tile(r, g, start=0, size=TILE):
        offset = ((r % 2) * 2 + g) * TILE + start
        if r in OUTER_ROWS:
            return outside[r // 6, offset : offset + size, :]
        return (low_ref if r < 4 else high_ref)[offset : offset + size, :]

    outer_spread, outer_direct = local_terms(
        OUTER_ROWS,
        tile,
        matrices,
        slopes,
        flux,
        plain,
        outer_coefs,
        lambda r, g: {1: 24 * g, 6: 48 + 24 * g}.get(r),
    )
    masks = face_masks()
    _, outer_flux_at, outer_plain_at, _ = row_starts(OUTER_ROWS)
    _, inner_flux_at, inner_plain_at, _ = row_starts(OWN_ROWS)

    def joined(spread, r, start, count):
        def rows(k):
            if k in OUTER_ROWS:
                at = (outer_flux_at if spread else outer_plain_at)[k] + start
                return (outer_spread if spread else outer_direct)[at : at + count, :]
            at = (inner_flux_at if spread else inner_plain_at)[k] + start
            return (inner_spread if spread else inner_direct)[at : at + count, :]

        return rows_joined(rows(r - 1), rows(r), rows(r + 1), *masks)

    def coefficients(r, g, k):
        if r in OUTER_ROWS:
            at = (0 if r == 1 else 48) + 24 * g + 8 * k
            return outer_coefs[at : at + 8, :]
        at = (2 * (r - 2) + g) * 24 + 8 * k
        return inner_coefs[at : at + 8, :]

    inverse, smoothing = {}, {}
    for r in EDGE_ROWS:
        mass_sum = joined(False, r, 0, 8)
        smoothing[r] = joined(True, r, 0, STATE)
        for g in range(2):
            inverse[r, g] = mass_inverse(mass_sum[g])
    for r in MIDDLE_ROWS:
        for g in range(2):
            at = 8 * (2 * (r - 3) + g)
            inverse[r, g] = middle_inverse[at : at + 8, :]
    damped = second_laplacian(EDGE_ROWS, smoothing, inverse, coefficients, matrices)

    def damped_row(r):
        if r in MIDDLE_ROWS:
            return middle_damped[(r - 3) * STATE : (r - 2) * STATE, :]
        at = EDGE_ROWS.index(r) * STATE
        return damped[at : at + STATE, :]

    ordered = []
    for r in OWN_ROWS:
        damping = rows_joined(damped_row(r - 1), damped_row(r), damped_row(r + 1), *masks)
        if r not in MIDDLE_ROWS:
            straight = joined(False, r, 8, 24)
            carried = joined(True, r, STATE, 16)
        for g in range(2):
            if r in MIDDLE_ROWS:
                at = STATE * (2 * (r - 3) + g)
                base = middle_ref[at : at + STATE, :]
            else:
                base = advanced(tile(r, g, 0, STATE), straight[g], carried[g], inverse[r, g])
            ordered.append(
                base - ((TIME_STEP * HYPER_NU) * damping[g]) * repeated(inverse[r, g])
            )
    whole = jnp.concatenate(ordered, axis=1)
    whole_ref[...] = whole
    shares = [(lists_ref[k : k + 1, :] > 0.0).astype(F32) for k in range(3)]
    slots = [jnp.broadcast_to(lists_ref[3:4, :] * shares[k], (8, 1024)) for k in range(3)]
    row = row_iota((8, 1024))
    slot_rows = sum(jnp.where(row == k, slots[k], 0.0) for k in range(3))
    columns = jnp.concatenate([whole * share for share in shares] + [slot_rows], axis=0)
    upper, lower = halves(columns)
    sent = dot_last(picks_ref[...], jnp.concatenate([upper, lower], axis=0))
    send_ref[...] = sent[:, :LANES] + sent[:, LANES:]


def receive_kernel(
    received_ref, whole_ref, hits_ref, updated_ref, physics_ref, updated, pieces, sems
):
    whole = whole_ref[...]
    upper = whole.astype(BF16).astype(F32)
    restored = dot(jnp.concatenate([upper, whole - upper], axis=0).astype(BF16), hits_ref[...])
    updated[...] = restored[:STATE] + restored[STATE:]
    copies = [pltpu.make_async_copy(updated, updated_ref, sems.at[3])]
    copies[0].start()
    turned_over = received_ref[...].T
    upper, lower = halves(turned_over)
    places = slice(3 * STATE, 3 * STATE + 3)
    slot = turned_over[places, :].astype(jnp.int32) - 1
    slots = [slot[k : k + 1].astype(jnp.int16) for k in range(3)]
    both = jnp.concatenate([upper, lower], axis=0)
    count = 2 * LANES
    for start in range(0, POINTS_DEV, count):
        row = (row_iota((count, POINTS_DEV)) + start).astype(jnp.int16)
        hits = (row == slots[0]) | (row == slots[1]) | (row == slots[2])
        rows = dot_last(both, jnp.where(hits, jnp.bfloat16(1), jnp.bfloat16(0)))
        rows = rows[:LANES] + rows[LANES:]
        own = rows[places, :] == (lane_iota((3, count)) + (start + 1)).astype(F32)
        piece = start // count
        pieces[piece] = jnp.where(
            own[0:1],
            rows[:STATE],
            jnp.where(own[1:2], rows[STATE : 2 * STATE], rows[2 * STATE : 3 * STATE]),
        )
        copies.append(
            pltpu.make_async_copy(
                pieces.at[piece], physics_ref.at[:, pl.ds(start, count)], sems.at[piece]
            )
        )
        copies[-1].start()
    for copy in copies:
        copy.wait()


def call(kernel, shapes, scratch=(), flops=0, moved=0, vmem=VMEM_LIMIT, **specs):
    return pl.pallas_call(
        kernel,
        out_shape=[
            jax.ShapeDtypeStruct(*s) if isinstance(s, tuple) else s for s in shapes
        ],
        scratch_shapes=list(scratch),
        **specs,
        compiler_params=pltpu.CompilerParams(vmem_limit_bytes=vmem),
        cost_estimate=pl.CostEstimate(flops=flops, bytes_accessed=moved, transcendentals=0),
    )


def swaps(count, pairs_from):
    route = []
    for i in range(pairs_from, count - 1, 2):
        route += [(i, i + 1), (i + 1, i)]
    return route


def body(
    evolving_state_array, point_id, neighbours, jacobian, inverse_metric, coriolis, column_slot
):
    anywhere = pl.BlockSpec(memory_space=pltpu.HBM)
    half = ((4 * TILE, LANES), F32)
    strip = ((TILE, LANES), F32)
    values_shape = ((TILE + 8, POINTS_DEV), F32)
    far, close, values = call(
        strip_kernel,
        [pltpu.VMEM(*strip), pltpu.VMEM(*strip), pltpu.VMEM(*values_shape)],
        scratch=[
            pltpu.VMEM((8, ELEMS_DEV), jnp.int32),
            pltpu.VMEM((POINTS_DEV,), F32),
            pltpu.VMEM((POINTS_DEV,), F32),
            pltpu.VMEM((4, POINTS_DEV), F32),
            pltpu.VMEM((POINTS_DEV,), jnp.int32),
            pltpu.VMEM((FIELDS, LEV, POINTS_DEV), F32),
            pltpu.SemaphoreType.DMA((6,)),
        ],
        in_specs=[anywhere] * 6,
        vmem=64 * 1024 * 1024 - 524288,
    )(evolving_state_array, jacobian, coriolis, inverse_metric, neighbours, column_slot)
    cols, rows = lax.axis_size("col"), lax.axis_size("curve")
    from_far = lax.ppermute(far, "col", swaps(cols, 1) + [(cols - 1, 0), (0, cols - 1)])
    from_close = lax.ppermute(close, "col", swaps(cols, 0))
    low, high, hits = call(
        arrange_kernel,
        [half, half, pltpu.VMEM((1024, POINTS_DEV), BF16)],
        flops=400_000_000,
        moved=1_000_000,
    )(values)
    first, second, low, high = call(margin_kernel, [half] * 4)(low, high, from_far, from_close)
    second_far = lax.ppermute(second, "curve", swaps(rows, 1))
    first_far = lax.ppermute(first, "curve", swaps(rows, 0))
    matrices = jnp.asarray(operators())
    def scratch(rows):
        slope_rows, flux_rows, plain_rows = row_starts(rows)[3]
        return [
            pltpu.VMEM((slope_rows, 2 * LANES), F32),
            pltpu.VMEM((flux_rows, 4 * LANES), F32),
            pltpu.VMEM((plain_rows, 2 * LANES), F32),
        ]

    inner = call(
        inner_kernel,
        [
            ((8, 1024), F32),
            ((4 * 56, 2 * LANES), F32),
            ((4 * 32, 2 * LANES), F32),
            ((8 * 24, LANES), F32),
            ((POINTS_DEV, 1024), BF16),
            ((4 * STATE, LANES), F32),
            ((2 * STATE, 2 * LANES), F32),
            ((4 * 8, LANES), F32),
        ],
        scratch=scratch(OWN_ROWS),
        flops=400_000_000,
        moved=1_000_000,
    )(low, high, matrices)
    lists, spread, direct, coefs, picks, middle, middle_damped, middle_inverse = inner
    whole, sent = call(
        section_kernel,
        [((STATE, 1024), F32), ((POINTS_DEV, LANES), F32)],
        scratch=[pltpu.VMEM((2, 4 * TILE, LANES), F32)]
        + scratch(OUTER_ROWS)
        + [pltpu.VMEM((4 * 24, LANES), F32)],
    )(
        first_far,
        second_far,
        low,
        high,
        lists,
        picks,
        matrices,
        spread,
        direct,
        coefs,
        middle,
        middle_damped,
        middle_inverse,
    )
    received = lax.all_to_all(sent, "col", split_axis=0, concat_axis=0, tiled=True)
    updated, physics = call(
        receive_kernel,
        [((STATE, POINTS_DEV), F32)] * 2,
        scratch=[
            pltpu.VMEM((STATE, POINTS_DEV), F32),
            pltpu.VMEM((3, STATE, 2 * LANES), F32),
            pltpu.SemaphoreType.DMA((4,)),
        ],
        in_specs=[pl.BlockSpec(memory_space=pltpu.VMEM)] * 3,
        out_specs=[anywhere] * 2,
    )(received, whole, hits)
    shape = evolving_state_array.shape
    return updated.reshape(shape), physics.reshape(shape)


def solution(mesh):
    split = ("curve", "col")
    return jax.shard_map(
        body,
        mesh=mesh,
        in_specs=(
            P(None, None, split),
            P(split),
            P(None, split),
            P(split),
            P(None, split),
            P(split),
            P(split),
        ),
        out_specs=(P(None, None, split), P(None, None, split)),
        check_vma=False,
    )
```

```python
import functools
import math

import jax
import jax.numpy as jnp
import numpy as np
from jax import lax
from jax.experimental import pallas as pl
from jax.experimental.pallas import tpu as pltpu
from jax.sharding import PartitionSpec as P

FIELDS = 5
LEV = 8
STATE = FIELDS * LEV
TILE = 48
LANES = 128
ELEMS_DEV = 48
POINTS_DEV = 768
N_COL = 32
CAP = 72
CAP_ROWS = CAP // 3
TIME_STEP = 0.1
HYPER_NU = 0.002
F32 = jnp.float32
BF16 = jnp.bfloat16
VMEM_LIMIT = 32 * 1024 * 1024


def gll_tables():
    root_fifth = 1.0 / math.sqrt(5.0)
    nodes = np.array([-1.0, -root_fifth, root_fifth, 1.0])
    weights = np.array([1.0, 5.0, 5.0, 1.0]) / 6.0
    table = np.zeros((4, 4))
    for i in range(4):
        for m in range(4):
            if i == m:
                table[i, m] = sum(1.0 / (nodes[i] - nodes[o]) for o in range(4) if o != i)
            else:
                upper = np.prod([nodes[i] - nodes[o] for o in range(4) if o != i])
                lower = np.prod([nodes[m] - nodes[o] for o in range(4) if o != m])
                table[i, m] = upper / (lower * (nodes[i] - nodes[m]))
    return table, weights


def two_parts(matrix):
    upper = matrix.astype(np.float32).astype(jnp.bfloat16)
    lower = (matrix - upper.astype(np.float64)).astype(np.float32).astype(jnp.bfloat16)
    return upper, lower


@functools.lru_cache(maxsize=None)
def operators():
    table, weights = gll_tables()
    eye4, eye8 = np.eye(4), np.eye(8)
    along_cycle = np.kron(eye4, table.T)
    along_rows = np.kron(table.T, eye4)
    grad = np.concatenate([np.kron(eye8, along_cycle), np.kron(eye8, along_rows)], axis=1)
    weight = np.diag(np.outer(weights, weights).reshape(16))
    div = np.concatenate(
        [np.kron(eye8, along_cycle @ weight), np.kron(eye8, along_rows @ weight)], axis=0
    )
    join = np.eye(256)
    for place in range(15):
        for j in range(4):
            low, high = place * 16 + 4 * j + 3, place * 16 + 16 + 4 * j
            join[low, high] = 1.0
            join[high, low] = 1.0
    both = np.zeros((512, 256))
    both[:256, :128] = div
    both[256:, 128:] = div
    div_join = both @ join
    grad_hi, grad_lo = two_parts(grad)
    div_hi, div_lo = two_parts(div_join)
    return np.concatenate(
        [grad_hi, grad_hi, grad_lo, div_hi, div_lo, join.astype(jnp.bfloat16)], axis=0
    )


def dot(left, right):
    return jnp.dot(left, right, preferred_element_type=F32)


def dot_last(left, right):
    return lax.dot_general(left, right, (((1,), (1,)), ((), ())), preferred_element_type=F32)


def halves(value):
    upper = value.astype(BF16)
    lower = (value - upper.astype(F32)).astype(BF16)
    return upper, lower


def lane_iota(shape):
    return lax.broadcasted_iota(jnp.int32, shape, 1)


def row_iota(shape):
    return lax.broadcasted_iota(jnp.int32, shape, 0)


def one_step(local, index):
    hit = (row_iota((ELEMS_DEV, ELEMS_DEV)) == index) & local
    return hit.astype(F32).astype(BF16)


def wide(local):
    return jnp.broadcast_to(local.astype(F32), (8, ELEMS_DEV))


def chain_length(local, index, doublings):
    length = wide(local)
    step = one_step(local, index)
    for k in range(doublings):
        length = length + dot(length.astype(BF16), step)
        if k + 1 < doublings:
            step = dot(step, step).astype(BF16)
    return length


def local_lists(near):
    base = (lax.axis_index("curve") * N_COL + lax.axis_index("col")) * ELEMS_DEV
    index = near - base
    return index, (index >= 0) & (index < ELEMS_DEV)


def over_points(element_values):
    shape = (ELEMS_DEV, POINTS_DEV)
    spread = (lane_iota(shape) // 16 == row_iota(shape)).astype(F32).astype(BF16)
    return dot(element_values.astype(BF16), spread)[0:1].astype(jnp.int32)


def three_parts(value):
    first = value.astype(BF16)
    rest = value - first.astype(F32)
    second = rest.astype(BF16)
    return first, second, (rest - second.astype(F32)).astype(BF16)


def strip_kernel(
    state_ref, jacobian_ref, coriolis_ref, metric_ref, near_ref, slot_ref, far_ref, close_ref,
    values_ref, near, jac, cor, metric, slot, state, sems
):
    copies = [
        pltpu.make_async_copy(source, target, sems.at[i])
        for i, (source, target) in enumerate(
            [
                (near_ref, near),
                (state_ref, state),
                (jacobian_ref, jac),
                (coriolis_ref, cor),
                (metric_ref, metric),
                (slot_ref, slot),
            ]
        )
    ]
    for copy in copies:
        copy.start()
    copies[0].wait()
    index, local = local_lists(near[...])
    lower = wide(local[2:3])
    row = lower + dot(lower.astype(BF16), one_step(local[2:3], index[2:3])) + wide(~local[3:4])
    sides = []
    for side in range(2):
        here, there = local[side : side + 1], index[side : side + 1]
        second = dot(wide(here).astype(BF16), one_step(here, there))
        edge = wide(~here)
        sides.append((edge, wide(here) * (1.0 - second)))
    (first, second), (last, second_last) = sides
    unit = (first + second) * (2.0 * row + 1.0 + second)
    unit = unit + (last + second_last) * (2.0 * row + 9.0 + last)
    lane = (over_points(unit) - 1) * 16 + lane_iota((1, POINTS_DEV)) % 16
    row16 = row_iota((2 * LANES, POINTS_DEV)).astype(jnp.int16)
    hits = jnp.where(row16 == lane.astype(jnp.int16), jnp.bfloat16(1), jnp.bfloat16(0))
    for copy in copies[1:]:
        copy.wait()
    values = jnp.concatenate(
        [
            state[...].reshape(STATE, POINTS_DEV),
            jac[...].reshape(1, POINTS_DEV),
            cor[...].reshape(1, POINTS_DEV),
            metric[...],
            slot[...].astype(F32).reshape(1, POINTS_DEV),
            jnp.zeros((1, POINTS_DEV), F32),
        ],
        axis=0,
    )
    values_ref[0:TILE, :] = values
    values_ref[TILE:, 0:ELEMS_DEV] = jnp.where(local, index, -1).astype(F32)
    parts = dot_last(jnp.concatenate(halves(values), axis=0), hits)
    strips = parts[:TILE] + parts[TILE:]
    even = lax.rem(lax.axis_index("col"), 2) == 0
    to_left, to_right = strips[:, :LANES], strips[:, LANES:]
    far_ref[...] = jnp.where(even, to_left, to_right)
    close_ref[...] = jnp.where(even, to_right, to_left)


def arrange_kernel(values_ref, low_ref, high_ref, hits_ref):
    index = values_ref[TILE:, 0:ELEMS_DEV].astype(jnp.int32)
    local = index >= 0
    place = chain_length(local[0:1], index[0:1], 4)
    row = chain_length(local[2:3], index[2:3], 2)
    target = over_points(row * 16.0 + place + 2.0) * 16 + lane_iota((1, POINTS_DEV)) % 16
    row16 = row_iota((1024, POINTS_DEV)).astype(jnp.int16)
    hits = jnp.where(row16 == target.astype(jnp.int16), jnp.bfloat16(1), jnp.bfloat16(0))
    hits_ref[...] = hits
    parts = dot_last(jnp.concatenate(halves(values_ref[0:TILE, :]), axis=0), hits)
    ordered = parts[:TILE] + parts[TILE:]
    for r in range(4):
        for g in range(2):
            block = ordered[:, (2 * r + g) * LANES : (2 * r + g + 1) * LANES]
            ref = low_ref if r < 2 else high_ref
            start = ((r % 2) * 2 + g) * TILE
            ref[start : start + TILE, :] = block


def turned(block, by):
    by = by % LANES
    return block if by == 0 else pltpu.roll(block, by, 1)


def margin_kernel(
    low_in, high_in, from_far, from_close, first_ref, second_ref, low_ref, high_ref
):
    lane = lane_iota((TILE, LANES))
    even = lax.rem(lax.axis_index("col"), 2) == 0
    from_left = jnp.where(even, from_far[...], from_close[...])
    from_right = jnp.where(even, from_close[...], from_far[...])
    halves_of_rows = []
    for source, start_row in ((low_in, 0), (high_in, 2)):
        blocks = []
        for r in range(2):
            turn = start_row + r
            start = r * 2 * TILE
            blocks.append(
                jnp.where(lane < 32, turned(from_left, -32 * turn), source[start : start + TILE, :])
            )
            start += TILE
            blocks.append(
                jnp.where(
                    lane >= 96, turned(from_right, 96 - 32 * turn), source[start : start + TILE, :]
                )
            )
        halves_of_rows.append(jnp.concatenate(blocks, axis=0))
    low, high = halves_of_rows
    low_ref[...] = low
    high_ref[...] = high
    even = lax.rem(lax.axis_index("curve"), 2) == 0
    first_ref[...] = jnp.where(even, high, low)
    second_ref[...] = jnp.where(even, low, high)


def send_lists(slots):
    square = (LANES, LANES)
    upto = (row_iota(square) <= lane_iota(square)).astype(F32)
    count = jnp.concatenate([upto, jnp.ones(square, F32)], axis=1).astype(BF16)
    lane = lane_iota((1, LANES))
    chosen, devices, withins, owns = [], [], [], []
    for i, slot in enumerate(slots):
        own = lane >= 32 if i % 2 == 0 else lane < 96
        device = jnp.where(own, jnp.floor((slot + 0.5) * (1.0 / POINTS_DEV)), -1.0)
        wanted = jnp.broadcast_to(device.astype(jnp.int32), (N_COL, LANES))
        chosen.append((wanted == row_iota((N_COL, LANES))).astype(F32))
        devices.append(device)
        withins.append(slot - device * POINTS_DEV)
        owns.append(own)
    counted = dot(jnp.concatenate(chosen, axis=0).astype(BF16), count)
    before = jnp.zeros((N_COL, LANES), F32)
    lists = []
    for i, (device, within, own) in enumerate(zip(devices, withins, owns)):
        rows = counted[i * N_COL : (i + 1) * N_COL]
        rank = jnp.sum((rows[:, :LANES] + before) * chosen[i], axis=0, keepdims=True) - 1.0
        before = before + rows[:, LANES:]
        third = (rank >= CAP_ROWS).astype(F32) + (rank >= 2 * CAP_ROWS).astype(F32)
        line = device * CAP_ROWS + rank - third * CAP_ROWS
        parts = [jnp.where(own & (third == float(k)), line + 1.0, 0.0) for k in range(3)]
        filler = jnp.zeros((4, LANES), F32)
        lists.append(
            jnp.concatenate(parts + [jnp.where(own, within + 1.0, 0.0), filler], axis=0)
        )
    return jnp.concatenate(lists, axis=1)


def fluxes(slope, coefficients):
    along_cycle, along_rows = slope[:, :LANES], slope[:, LANES:]
    caa, cab, cbb = coefficients
    return caa * along_cycle + cab * along_rows, cab * along_cycle + cbb * along_rows


def gradient(values, matrices):
    upper, lower = halves(values)
    return dot(jnp.concatenate([upper, lower], axis=1), matrices[0:256, :]) + dot(
        upper, matrices[256:384, :]
    )


def both_parts(upper, lower, matrix):
    count = upper.shape[0]
    result = dot(jnp.concatenate([upper, lower], axis=0), matrix)
    return result[:count] + result[count:]


def divergence_joined(values, matrices):
    upper, lower = halves(values)
    return both_parts(upper, lower, matrices[384:896, :]) + dot(upper, matrices[896:1408, :])


def rows_joined(below, here, above, low_mask, high_mask):
    parts = []
    for g in range(2):
        part = slice(g * LANES, (g + 1) * LANES)
        parts.append(
            here[:, part]
            + low_mask * turned(below[:, part], -12)
            + high_mask * turned(above[:, part], 12)
        )
    return parts


def row_starts(rows):
    slope, flux, plain = {}, {}, {}
    at = [0, 0, 0]
    for r in rows:
        lean = r in (0, 7)
        for g in range(2):
            slope[r, g] = at[0]
            at[0] += STATE if lean else TILE
        flux[r] = at[1]
        at[1] += STATE if lean else STATE + 16
        plain[r] = at[2]
        at[2] += 8 if lean else 32
    return slope, flux, plain, at


def local_terms(rows, tile, matrices, slopes, flux, plain, coefs, coefs_at):
    slope_at, flux_at, plain_at, _ = row_starts(rows)
    cells = [(r, g) for r in rows for g in range(2)]
    stacked = []
    for r, g in cells:
        stacked.append(tile(r, g, 0, STATE))
        if r not in (0, 7):
            zonal, meridional = tile(r, g, 0, 8), tile(r, g, 8, 8)
            energy = 0.5 * (zonal * zonal + meridional * meridional) + tile(r, g, 16, 8)
            stacked.append(energy)
    slopes[...] = gradient(jnp.concatenate(stacked, axis=0), matrices)
    lane = lane_iota((8, LANES))
    inner_i = (lane % 4 == 1) | (lane % 4 == 2)
    inner_j = (lane // 4 % 4 == 1) | (lane // 4 % 4 == 2)
    weight = jnp.where(inner_i, 5.0 / 6.0, 1.0 / 6.0) * jnp.where(inner_j, 5.0 / 6.0, 1.0 / 6.0)
    for r, g in cells:

        def line(k):
            return jnp.broadcast_to(tile(r, g, STATE + k, 1), (8, LANES))

        jacobian, coriolis = line(0), line(1)
        m11, m12, m21, m22 = 1.0 + line(2), line(3), line(4), 1.0 + line(5)
        caa = jacobian * (m11 * m11 + m12 * m12)
        cab = jacobian * (m11 * m21 + m12 * m22)
        cbb = jacobian * (m21 * m21 + m22 * m22)
        at = coefs_at(r, g)
        if at is not None:
            coefs[at : at + 8, :] = caa
            coefs[at + 8 : at + 16, :] = cab
            coefs[at + 16 : at + 24, :] = cbb
        mass = jacobian * weight
        at = slope_at[r, g]
        first = slice(g * 2 * LANES, (g * 2 + 1) * LANES)
        second = slice((g * 2 + 1) * LANES, (g * 2 + 2) * LANES)
        part = slice(g * LANES, (g + 1) * LANES)
        to, direct = flux_at[r], plain_at[r]
        for f in range(FIELDS):
            one, two = fluxes(slopes[at + 8 * f : at + 8 * f + 8, :], (caa, cab, cbb))
            flux[to + 8 * f : to + 8 * f + 8, first] = one
            flux[to + 8 * f : to + 8 * f + 8, second] = two
        plain[direct : direct + 8, part] = mass
        if r in (0, 7):
            continue
        zonal, meridional = tile(r, g, 0, 8), tile(r, g, 8, 8)
        flow1 = jacobian * (m11 * zonal + m12 * meridional)
        flow2 = jacobian * (m21 * zonal + m22 * meridional)
        for k in range(2):
            carried = tile(r, g, 24 + 8 * k, 8)
            flux[to + 40 + 8 * k : to + 48 + 8 * k, first] = carried * flow1
            flux[to + 40 + 8 * k : to + 48 + 8 * k, second] = carried * flow2
        ea, eb = slopes[at + 40 : at + 48, :LANES], slopes[at + 40 : at + 48, LANES:]
        ta, tb = slopes[at + 16 : at + 24, :LANES], slopes[at + 16 : at + 24, LANES:]
        plain[direct + 8 : direct + 16, part] = mass * (
            coriolis * meridional - (m11 * ea + m21 * eb)
        )
        plain[direct + 16 : direct + 24, part] = -mass * (
            coriolis * zonal + (m12 * ea + m22 * eb)
        )
        plain[direct + 24 : direct + 32, part] = -mass * (
            zonal * (m11 * ta + m21 * tb) + meridional * (m12 * ta + m22 * tb)
        )
    spread = divergence_joined(flux[...], matrices)
    upper, lower = halves(plain[...])
    return spread, both_parts(upper, lower, matrices[1408:1664, :])


def face_masks():
    lane = lane_iota((1, LANES)) % 16
    return (lane < 4).astype(F32), (lane >= 12).astype(F32)


def repeated(block):
    return jnp.concatenate([block] * FIELDS, axis=0)


def second_laplacian(rows, smoothing, inverse, coefficients, matrices):
    smooth = [smoothing[r][g] * repeated(inverse[r, g]) for r in rows for g in range(2)]
    again = gradient(jnp.concatenate(smooth, axis=0), matrices)
    flat = []
    for n, r in enumerate(rows):
        parts = []
        for g in range(2):
            triple = tuple(repeated(coefficients(r, g, k)) for k in range(3))
            start = (2 * n + g) * STATE
            parts += list(fluxes(again[start : start + STATE, :], triple))
        flat.append(jnp.concatenate(parts, axis=1))
    return divergence_joined(jnp.concatenate(flat, axis=0), matrices)


def mass_inverse(mass_sum):
    return 1.0 / jnp.where(mass_sum > 0.0, mass_sum, 1.0)


def advanced(state, straight, carried, inverse):
    return state + (TIME_STEP * jnp.concatenate([straight, -carried], axis=0)) * repeated(inverse)


OWN_ROWS = (2, 3, 4, 5)
OUTER_ROWS = (0, 1, 6, 7)
MIDDLE_ROWS = (3, 4)
EDGE_ROWS = (1, 2, 5, 6)


def inner_kernel(
    low_ref,
    high_ref,
    matrices,
    lists_ref,
    spread_ref,
    direct_ref,
    coefs,
    picks_ref,
    middle_ref,
    damped_ref,
    inverse_ref,
    slopes,
    flux,
    plain,
):
    def tile(r, g, start=0, size=TILE):
        offset = ((r % 2) * 2 + g) * TILE + start
        return (low_ref if r < 4 else high_ref)[offset : offset + size, :]

    def coefs_at(r, g):
        return (2 * (r - 2) + g) * 24

    lists = send_lists([tile(r, g, STATE + 6, 1) for r in OWN_ROWS for g in range(2)])
    lists_ref[...] = lists
    line = (lists[0:1] + lists[1:2] + lists[2:3]).astype(jnp.int32) - 1
    row16 = row_iota((POINTS_DEV, 1024)).astype(jnp.int16)
    picks_ref[...] = jnp.where(
        row16 == line.astype(jnp.int16), jnp.bfloat16(1), jnp.bfloat16(0)
    )
    spread, direct = local_terms(
        OWN_ROWS, tile, matrices, slopes, flux, plain, coefs, coefs_at
    )
    spread_ref[...] = spread
    direct_ref[...] = direct
    masks = face_masks()

    def joined(value, size, r, start, count):
        def rows(k):
            at = (k - 2) * size + start
            return value[at : at + count, :]

        return rows_joined(rows(r - 1), rows(r), rows(r + 1), *masks)

    inverse, smoothing = {}, {}
    for r in MIDDLE_ROWS:
        mass_sum = joined(direct, 32, r, 0, 8)
        smoothing[r] = joined(spread, 56, r, 0, STATE)
        straight = joined(direct, 32, r, 8, 24)
        carried = joined(spread, 56, r, STATE, 16)
        for g in range(2):
            inverse[r, g] = mass_inverse(mass_sum[g])
            at = 2 * (r - 3) + g
            inverse_ref[8 * at : 8 * at + 8, :] = inverse[r, g]
            middle_ref[STATE * at : STATE * at + STATE, :] = advanced(
                tile(r, g, 0, STATE), straight[g], carried[g], inverse[r, g]
            )

    def coefficients(r, g, k):
        return coefs[coefs_at(r, g) + 8 * k : coefs_at(r, g) + 8 * k + 8, :]

    damped_ref[...] = second_laplacian(MIDDLE_ROWS, smoothing, inverse, coefficients, matrices)


def section_kernel(
    first_far_ref,
    second_far_ref,
    low_ref,
    high_ref,
    lists_ref,
    picks_ref,
    matrices,
    inner_spread,
    inner_direct,
    inner_coefs,
    middle_ref,
    middle_damped,
    middle_inverse,
    whole_ref,
    send_ref,
    outside,
    slopes,
    flux,
    plain,
    outer_coefs,
):
    even = lax.rem(lax.axis_index("curve"), 2) == 0
    outside[0] = jnp.where(even, second_far_ref[...], first_far_ref[...])
    outside[1] = jnp.where(even, first_far_ref[...], second_far_ref[...])

    def tile(r, g, start=0, size=TILE):
        offset = ((r % 2) * 2 + g) * TILE + start
        if r in OUTER_ROWS:
            return outside[r // 6, offset : offset + size, :]
        return (low_ref if r < 4 else high_ref)[offset : offset + size, :]

    outer_spread, outer_direct = local_terms(
        OUTER_ROWS,
        tile,
        matrices,
        slopes,
        flux,
        plain,
        outer_coefs,
        lambda r, g: {1: 24 * g, 6: 48 + 24 * g}.get(r),
    )
    masks = face_masks()
    _, outer_flux_at, outer_plain_at, _ = row_starts(OUTER_ROWS)
    _, inner_flux_at, inner_plain_at, _ = row_starts(OWN_ROWS)

    def joined(spread, r, start, count):
        def rows(k):
            if k in OUTER_ROWS:
                at = (outer_flux_at if spread else outer_plain_at)[k] + start
                return (outer_spread if spread else outer_direct)[at : at + count, :]
            at = (inner_flux_at if spread else inner_plain_at)[k] + start
            return (inner_spread if spread else inner_direct)[at : at + count, :]

        return rows_joined(rows(r - 1), rows(r), rows(r + 1), *masks)

    def coefficients(r, g, k):
        if r in OUTER_ROWS:
            at = (0 if r == 1 else 48) + 24 * g + 8 * k
            return outer_coefs[at : at + 8, :]
        at = (2 * (r - 2) + g) * 24 + 8 * k
        return inner_coefs[at : at + 8, :]

    inverse, smoothing = {}, {}
    for r in EDGE_ROWS:
        mass_sum = joined(False, r, 0, 8)
        smoothing[r] = joined(True, r, 0, STATE)
        for g in range(2):
            inverse[r, g] = mass_inverse(mass_sum[g])
    for r in MIDDLE_ROWS:
        for g in range(2):
            at = 8 * (2 * (r - 3) + g)
            inverse[r, g] = middle_inverse[at : at + 8, :]
    damped = second_laplacian(EDGE_ROWS, smoothing, inverse, coefficients, matrices)

    def damped_row(r):
        if r in MIDDLE_ROWS:
            return middle_damped[(r - 3) * STATE : (r - 2) * STATE, :]
        at = EDGE_ROWS.index(r) * STATE
        return damped[at : at + STATE, :]

    ordered = []
    for r in OWN_ROWS:
        damping = rows_joined(damped_row(r - 1), damped_row(r), damped_row(r + 1), *masks)
        if r not in MIDDLE_ROWS:
            straight = joined(False, r, 8, 24)
            carried = joined(True, r, STATE, 16)
        for g in range(2):
            if r in MIDDLE_ROWS:
                at = STATE * (2 * (r - 3) + g)
                base = middle_ref[at : at + STATE, :]
            else:
                base = advanced(tile(r, g, 0, STATE), straight[g], carried[g], inverse[r, g])
            ordered.append(
                base - ((TIME_STEP * HYPER_NU) * damping[g]) * repeated(inverse[r, g])
            )
    whole = jnp.concatenate(ordered, axis=1)
    whole_ref[...] = whole
    shares = [(lists_ref[k : k + 1, :] > 0.0).astype(F32) for k in range(3)]
    slots = [jnp.broadcast_to(lists_ref[3:4, :] * shares[k], (8, 1024)) for k in range(3)]
    row = row_iota((8, 1024))
    slot_rows = sum(jnp.where(row == k, slots[k], 0.0) for k in range(3))
    columns = jnp.concatenate([whole * share for share in shares] + [slot_rows], axis=0)
    upper, lower = halves(columns)
    sent = dot_last(picks_ref[...], jnp.concatenate([upper, lower], axis=0))
    send_ref[...] = sent[:, :LANES] + sent[:, LANES:]


def receive_kernel(
    received_ref, whole_ref, hits_ref, updated_ref, physics_ref, updated, pieces, sems
):
    whole = whole_ref[...]
    upper = whole.astype(BF16).astype(F32)
    restored = dot(jnp.concatenate([upper, whole - upper], axis=0).astype(BF16), hits_ref[...])
    updated[...] = restored[:STATE] + restored[STATE:]
    copies = [pltpu.make_async_copy(updated, updated_ref, sems.at[3])]
    copies[0].start()
    turned_over = received_ref[...].T
    upper, lower = halves(turned_over)
    places = slice(3 * STATE, 3 * STATE + 3)
    slot = turned_over[places, :].astype(jnp.int32) - 1
    slots = [slot[k : k + 1].astype(jnp.int16) for k in range(3)]
    both = jnp.concatenate([upper, lower], axis=0)
    count = 2 * LANES
    for start in range(0, POINTS_DEV, count):
        row = (row_iota((count, POINTS_DEV)) + start).astype(jnp.int16)
        hits = (row == slots[0]) | (row == slots[1]) | (row == slots[2])
        rows = dot_last(both, jnp.where(hits, jnp.bfloat16(1), jnp.bfloat16(0)))
        rows = rows[:LANES] + rows[LANES:]
        own = rows[places, :] == (lane_iota((3, count)) + (start + 1)).astype(F32)
        piece = start // count
        pieces[piece] = jnp.where(
            own[0:1],
            rows[:STATE],
            jnp.where(own[1:2], rows[STATE : 2 * STATE], rows[2 * STATE : 3 * STATE]),
        )
        copies.append(
            pltpu.make_async_copy(
                pieces.at[piece], physics_ref.at[:, pl.ds(start, count)], sems.at[piece]
            )
        )
        copies[-1].start()
    for copy in copies:
        copy.wait()


def call(kernel, shapes, scratch=(), flops=0, moved=0, vmem=VMEM_LIMIT, **specs):
    return pl.pallas_call(
        kernel,
        out_shape=[
            jax.ShapeDtypeStruct(*s) if isinstance(s, tuple) else s for s in shapes
        ],
        scratch_shapes=list(scratch),
        **specs,
        compiler_params=pltpu.CompilerParams(vmem_limit_bytes=vmem),
        cost_estimate=pl.CostEstimate(flops=flops, bytes_accessed=moved, transcendentals=0),
    )


def swaps(count, pairs_from):
    route = []
    for i in range(pairs_from, count - 1, 2):
        route += [(i, i + 1), (i + 1, i)]
    return route


def body(
    evolving_state_array, point_id, neighbours, jacobian, inverse_metric, coriolis, column_slot
):
    anywhere = pl.BlockSpec(memory_space=pltpu.HBM)
    half = ((4 * TILE, LANES), F32)
    strip = ((TILE, LANES), F32)
    values_shape = ((TILE + 8, POINTS_DEV), F32)
    far, close, values = call(
        strip_kernel,
        [pltpu.VMEM(*strip), pltpu.VMEM(*strip), pltpu.VMEM(*values_shape)],
        scratch=[
            pltpu.VMEM((8, ELEMS_DEV), jnp.int32),
            pltpu.VMEM((POINTS_DEV,), F32),
            pltpu.VMEM((POINTS_DEV,), F32),
            pltpu.VMEM((4, POINTS_DEV), F32),
            pltpu.VMEM((POINTS_DEV,), jnp.int32),
            pltpu.VMEM((FIELDS, LEV, POINTS_DEV), F32),
            pltpu.SemaphoreType.DMA((6,)),
        ],
        in_specs=[anywhere] * 6,
        vmem=64 * 1024 * 1024 - 524288,
    )(evolving_state_array, jacobian, coriolis, inverse_metric, neighbours, column_slot)
    cols, rows = lax.axis_size("col"), lax.axis_size("curve")
    from_far = lax.ppermute(far, "col", swaps(cols, 1) + [(cols - 1, 0), (0, cols - 1)])
    from_close = lax.ppermute(close, "col", swaps(cols, 0))
    low, high, hits = call(
        arrange_kernel,
        [half, half, pltpu.VMEM((1024, POINTS_DEV), BF16)],
        flops=400_000_000,
        moved=1_000_000,
    )(values)
    first, second, low, high = call(margin_kernel, [half] * 4)(low, high, from_far, from_close)
    second_far = lax.ppermute(second, "curve", swaps(rows, 1))
    first_far = lax.ppermute(first, "curve", swaps(rows, 0))
    matrices = jnp.asarray(operators())
    def scratch(rows):
        slope_rows, flux_rows, plain_rows = row_starts(rows)[3]
        return [
            pltpu.VMEM((slope_rows, 2 * LANES), F32),
            pltpu.VMEM((flux_rows, 4 * LANES), F32),
            pltpu.VMEM((plain_rows, 2 * LANES), F32),
        ]

    inner = call(
        inner_kernel,
        [
            ((8, 1024), F32),
            ((4 * 56, 2 * LANES), F32),
            ((4 * 32, 2 * LANES), F32),
            ((8 * 24, LANES), F32),
            ((POINTS_DEV, 1024), BF16),
            ((4 * STATE, LANES), F32),
            ((2 * STATE, 2 * LANES), F32),
            ((4 * 8, LANES), F32),
        ],
        scratch=scratch(OWN_ROWS),
        flops=400_000_000,
        moved=1_000_000,
    )(low, high, matrices)
    lists, spread, direct, coefs, picks, middle, middle_damped, middle_inverse = inner
    whole, sent = call(
        section_kernel,
        [((STATE, 1024), F32), ((POINTS_DEV, LANES), F32)],
        scratch=[pltpu.VMEM((2, 4 * TILE, LANES), F32)]
        + scratch(OUTER_ROWS)
        + [pltpu.VMEM((4 * 24, LANES), F32)],
    )(
        first_far,
        second_far,
        low,
        high,
        lists,
        picks,
        matrices,
        spread,
        direct,
        coefs,
        middle,
        middle_damped,
        middle_inverse,
    )
    received = lax.all_to_all(sent, "col", split_axis=0, concat_axis=0, tiled=True)
    updated, physics = call(
        receive_kernel,
        [((STATE, POINTS_DEV), F32)] * 2,
        scratch=[
            pltpu.VMEM((STATE, POINTS_DEV), F32),
            pltpu.VMEM((3, STATE, 2 * LANES), F32),
            pltpu.SemaphoreType.DMA((4,)),
        ],
        in_specs=[pl.BlockSpec(memory_space=pltpu.VMEM)] * 3,
        out_specs=[anywhere] * 2,
    )(received, whole, hits)
    shape = evolving_state_array.shape
    return updated.reshape(shape), physics.reshape(shape)


def solution(mesh):
    split = ("curve", "col")
    return jax.shard_map(
        body,
        mesh=mesh,
        in_specs=(
            P(None, None, split),
            P(split),
            P(None, split),
            P(split),
            P(None, split),
            P(split),
            P(split),
        ),
        out_specs=(P(None, None, split), P(None, None, split)),
        check_vma=False,
    )
```

```python
import functools
import math

import jax
import jax.numpy as jnp
import numpy as np
from jax import lax
from jax.experimental import pallas as pl
from jax.experimental.pallas import tpu as pltpu
from jax.sharding import PartitionSpec as P

FIELDS = 5
LEV = 8
STATE = FIELDS * LEV
TILE = 48
LANES = 128
ELEMS_DEV = 48
POINTS_DEV = 768
N_COL = 32
CAP = 72
CAP_ROWS = CAP // 3
TIME_STEP = 0.1
HYPER_NU = 0.002
F32 = jnp.float32
BF16 = jnp.bfloat16
VMEM_LIMIT = 32 * 1024 * 1024


def gll_tables():
    root_fifth = 1.0 / math.sqrt(5.0)
    nodes = np.array([-1.0, -root_fifth, root_fifth, 1.0])
    weights = np.array([1.0, 5.0, 5.0, 1.0]) / 6.0
    table = np.zeros((4, 4))
    for i in range(4):
        for m in range(4):
            if i == m:
                table[i, m] = sum(1.0 / (nodes[i] - nodes[o]) for o in range(4) if o != i)
            else:
                upper = np.prod([nodes[i] - nodes[o] for o in range(4) if o != i])
                lower = np.prod([nodes[m] - nodes[o] for o in range(4) if o != m])
                table[i, m] = upper / (lower * (nodes[i] - nodes[m]))
    return table, weights


def two_parts(matrix):
    upper = matrix.astype(np.float32).astype(jnp.bfloat16)
    lower = (matrix - upper.astype(np.float64)).astype(np.float32).astype(jnp.bfloat16)
    return upper, lower


@functools.lru_cache(maxsize=None)
def operators():
    table, weights = gll_tables()
    eye4, eye8 = np.eye(4), np.eye(8)
    along_cycle = np.kron(eye4, table.T)
    along_rows = np.kron(table.T, eye4)
    grad = np.concatenate([np.kron(eye8, along_cycle), np.kron(eye8, along_rows)], axis=1)
    weight = np.diag(np.outer(weights, weights).reshape(16))
    div = np.concatenate(
        [np.kron(eye8, along_cycle @ weight), np.kron(eye8, along_rows @ weight)], axis=0
    )
    join = np.eye(256)
    for place in range(15):
        for j in range(4):
            low, high = place * 16 + 4 * j + 3, place * 16 + 16 + 4 * j
            join[low, high] = 1.0
            join[high, low] = 1.0
    both = np.zeros((512, 256))
    both[:256, :128] = div
    both[256:, 128:] = div
    div_join = both @ join
    grad_hi, grad_lo = two_parts(grad)
    div_hi, div_lo = two_parts(div_join)
    return np.concatenate(
        [grad_hi, grad_hi, grad_lo, div_hi, div_lo, join.astype(jnp.bfloat16)], axis=0
    )


def dot(left, right):
    return jnp.dot(left, right, preferred_element_type=F32)


def dot_last(left, right):
    return lax.dot_general(left, right, (((1,), (1,)), ((), ())), preferred_element_type=F32)


def halves(value):
    upper = value.astype(BF16)
    lower = (value - upper.astype(F32)).astype(BF16)
    return upper, lower


def lane_iota(shape):
    return lax.broadcasted_iota(jnp.int32, shape, 1)


def row_iota(shape):
    return lax.broadcasted_iota(jnp.int32, shape, 0)


def one_step(local, index):
    hit = (row_iota((ELEMS_DEV, ELEMS_DEV)) == index) & local
    return hit.astype(F32).astype(BF16)


def wide(local):
    return jnp.broadcast_to(local.astype(F32), (8, ELEMS_DEV))


def chain_length(local, index, doublings):
    length = wide(local)
    step = one_step(local, index)
    for k in range(doublings):
        length = length + dot(length.astype(BF16), step)
        if k + 1 < doublings:
            step = dot(step, step).astype(BF16)
    return length


def local_lists(near):
    base = (lax.axis_index("curve") * N_COL + lax.axis_index("col")) * ELEMS_DEV
    index = near - base
    return index, (index >= 0) & (index < ELEMS_DEV)


def over_points(element_values):
    shape = (ELEMS_DEV, POINTS_DEV)
    first = row_iota(shape) * 16
    spread = (lane_iota(shape) >= first) & (lane_iota(shape) < first + 16)
    spread = spread.astype(F32).astype(BF16)
    return dot(element_values.astype(BF16), spread)[0:1].astype(jnp.int32)


def three_parts(value):
    first = value.astype(BF16)
    rest = value - first.astype(F32)
    second = rest.astype(BF16)
    return first, second, (rest - second.astype(F32)).astype(BF16)


def strip_kernel(
    state_ref, jacobian_ref, coriolis_ref, metric_ref, near_ref, slot_ref, far_ref, close_ref,
    values_ref, near, jac, cor, metric, slot, state, sems
):
    copies = [
        pltpu.make_async_copy(source, target, sems.at[i])
        for i, (source, target) in enumerate(
            [
                (near_ref, near),
                (state_ref, state),
                (jacobian_ref, jac),
                (coriolis_ref, cor),
                (metric_ref, metric),
                (slot_ref, slot),
            ]
        )
    ]
    for copy in copies:
        copy.start()
    copies[0].wait()
    index, local = local_lists(near[...])
    lower = wide(local[2:3])
    row = lower + dot(lower.astype(BF16), one_step(local[2:3], index[2:3])) + wide(~local[3:4])
    sides = []
    for side in range(2):
        here, there = local[side : side + 1], index[side : side + 1]
        second = dot(wide(here).astype(BF16), one_step(here, there))
        edge = wide(~here)
        sides.append((edge, wide(here) * (1.0 - second)))
    (first, second), (last, second_last) = sides
    unit = (first + second) * (2.0 * row + 1.0 + second)
    unit = unit + (last + second_last) * (2.0 * row + 9.0 + last)
    lane = (over_points(unit) - 1) * 16 + lane_iota((1, POINTS_DEV)) % 16
    row16 = row_iota((2 * LANES, POINTS_DEV)).astype(jnp.int16)
    hits = jnp.where(row16 == lane.astype(jnp.int16), jnp.bfloat16(1), jnp.bfloat16(0))
    for copy in copies[1:]:
        copy.wait()
    values = jnp.concatenate(
        [
            state[...].reshape(STATE, POINTS_DEV),
            jac[...].reshape(1, POINTS_DEV),
            cor[...].reshape(1, POINTS_DEV),
            metric[...],
            slot[...].astype(F32).reshape(1, POINTS_DEV),
            jnp.zeros((1, POINTS_DEV), F32),
        ],
        axis=0,
    )
    values_ref[0:TILE, :] = values
    values_ref[TILE:, 0:ELEMS_DEV] = jnp.where(local, index, -1).astype(F32)
    parts = dot_last(jnp.concatenate(halves(values), axis=0), hits)
    strips = parts[:TILE] + parts[TILE:]
    even = lax.rem(lax.axis_index("col"), 2) == 0
    to_left, to_right = strips[:, :LANES], strips[:, LANES:]
    far_ref[...] = jnp.where(even, to_left, to_right)
    close_ref[...] = jnp.where(even, to_right, to_left)


def arrange_kernel(values_ref, low_ref, high_ref, hits_ref):
    index = values_ref[TILE:, 0:ELEMS_DEV].astype(jnp.int32)
    local = index >= 0
    place = chain_length(local[0:1], index[0:1], 4)
    row = chain_length(local[2:3], index[2:3], 2)
    target = over_points(row * 16.0 + place + 2.0) * 16 + lane_iota((1, POINTS_DEV)) % 16
    row16 = row_iota((1024, POINTS_DEV)).astype(jnp.int16)
    hits = jnp.where(row16 == target.astype(jnp.int16), jnp.bfloat16(1), jnp.bfloat16(0))
    hits_ref[...] = hits
    parts = dot_last(jnp.concatenate(halves(values_ref[0:TILE, :]), axis=0), hits)
    ordered = parts[:TILE] + parts[TILE:]
    for r in range(4):
        for g in range(2):
            block = ordered[:, (2 * r + g) * LANES : (2 * r + g + 1) * LANES]
            ref = low_ref if r < 2 else high_ref
            start = ((r % 2) * 2 + g) * TILE
            ref[start : start + TILE, :] = block


def turned(block, by):
    by = by % LANES
    return block if by == 0 else pltpu.roll(block, by, 1)


def margin_kernel(
    low_in, high_in, from_far, from_close, first_ref, second_ref, low_ref, high_ref
):
    lane = lane_iota((TILE, LANES))
    even = lax.rem(lax.axis_index("col"), 2) == 0
    from_left = jnp.where(even, from_far[...], from_close[...])
    from_right = jnp.where(even, from_close[...], from_far[...])
    halves_of_rows = []
    for source, start_row in ((low_in, 0), (high_in, 2)):
        blocks = []
        for r in range(2):
            turn = start_row + r
            start = r * 2 * TILE
            blocks.append(
                jnp.where(lane < 32, turned(from_left, -32 * turn), source[start : start + TILE, :])
            )
            start += TILE
            blocks.append(
                jnp.where(
                    lane >= 96, turned(from_right, 96 - 32 * turn), source[start : start + TILE, :]
                )
            )
        halves_of_rows.append(jnp.concatenate(blocks, axis=0))
    low, high = halves_of_rows
    low_ref[...] = low
    high_ref[...] = high
    even = lax.rem(lax.axis_index("curve"), 2) == 0
    first_ref[...] = jnp.where(even, high, low)
    second_ref[...] = jnp.where(even, low, high)


def send_lists(slots):
    square = (LANES, LANES)
    upto = (row_iota(square) <= lane_iota(square)).astype(F32)
    count = jnp.concatenate([upto, jnp.ones(square, F32)], axis=1).astype(BF16)
    lane = lane_iota((1, LANES))
    chosen, devices, withins, owns = [], [], [], []
    for i, slot in enumerate(slots):
        own = lane >= 32 if i % 2 == 0 else lane < 96
        device = jnp.where(own, jnp.floor((slot + 0.5) * (1.0 / POINTS_DEV)), -1.0)
        wanted = jnp.broadcast_to(device.astype(jnp.int32), (N_COL, LANES))
        chosen.append((wanted == row_iota((N_COL, LANES))).astype(F32))
        devices.append(device)
        withins.append(slot - device * POINTS_DEV)
        owns.append(own)
    counted = dot(jnp.concatenate(chosen, axis=0).astype(BF16), count)
    before = jnp.zeros((N_COL, LANES), F32)
    lists = []
    for i, (device, within, own) in enumerate(zip(devices, withins, owns)):
        rows = counted[i * N_COL : (i + 1) * N_COL]
        rank = jnp.sum((rows[:, :LANES] + before) * chosen[i], axis=0, keepdims=True) - 1.0
        before = before + rows[:, LANES:]
        third = (rank >= CAP_ROWS).astype(F32) + (rank >= 2 * CAP_ROWS).astype(F32)
        line = device * CAP_ROWS + rank - third * CAP_ROWS
        parts = [jnp.where(own & (third == float(k)), line + 1.0, 0.0) for k in range(3)]
        filler = jnp.zeros((4, LANES), F32)
        lists.append(
            jnp.concatenate(parts + [jnp.where(own, within + 1.0, 0.0), filler], axis=0)
        )
    return jnp.concatenate(lists, axis=1)


def fluxes(slope, coefficients):
    along_cycle, along_rows = slope[:, :LANES], slope[:, LANES:]
    caa, cab, cbb = coefficients
    return caa * along_cycle + cab * along_rows, cab * along_cycle + cbb * along_rows


def gradient(values, matrices):
    upper, lower = halves(values)
    return dot(jnp.concatenate([upper, lower], axis=1), matrices[0:256, :]) + dot(
        upper, matrices[256:384, :]
    )


def both_parts(upper, lower, matrix):
    count = upper.shape[0]
    result = dot(jnp.concatenate([upper, lower], axis=0), matrix)
    return result[:count] + result[count:]


def divergence_joined(values, matrices):
    upper, lower = halves(values)
    return both_parts(upper, lower, matrices[384:896, :]) + dot(upper, matrices[896:1408, :])


def rows_joined(below, here, above, low_mask, high_mask):
    parts = []
    for g in range(2):
        part = slice(g * LANES, (g + 1) * LANES)
        parts.append(
            here[:, part]
            + low_mask * turned(below[:, part], -12)
            + high_mask * turned(above[:, part], 12)
        )
    return parts


def row_starts(rows):
    slope, flux, plain = {}, {}, {}
    at = [0, 0, 0]
    for r in rows:
        lean = r in (0, 7)
        for g in range(2):
            slope[r, g] = at[0]
            at[0] += STATE if lean else TILE
        flux[r] = at[1]
        at[1] += STATE if lean else STATE + 16
        plain[r] = at[2]
        at[2] += 8 if lean else 32
    return slope, flux, plain, at


def local_terms(rows, tile, matrices, slopes, flux, plain, coefs, coefs_at):
    slope_at, flux_at, plain_at, _ = row_starts(rows)
    cells = [(r, g) for r in rows for g in range(2)]
    stacked = []
    for r, g in cells:
        stacked.append(tile(r, g, 0, STATE))
        if r not in (0, 7):
            zonal, meridional = tile(r, g, 0, 8), tile(r, g, 8, 8)
            energy = 0.5 * (zonal * zonal + meridional * meridional) + tile(r, g, 16, 8)
            stacked.append(energy)
    slopes[...] = gradient(jnp.concatenate(stacked, axis=0), matrices)
    lane = lane_iota((8, LANES))
    inner_i = (lane % 4 == 1) | (lane % 4 == 2)
    inner_j = (lane // 4 % 4 == 1) | (lane // 4 % 4 == 2)
    weight = jnp.where(inner_i, 5.0 / 6.0, 1.0 / 6.0) * jnp.where(inner_j, 5.0 / 6.0, 1.0 / 6.0)
    for r, g in cells:

        def line(k):
            return jnp.broadcast_to(tile(r, g, STATE + k, 1), (8, LANES))

        jacobian, coriolis = line(0), line(1)
        m11, m12, m21, m22 = 1.0 + line(2), line(3), line(4), 1.0 + line(5)
        caa = jacobian * (m11 * m11 + m12 * m12)
        cab = jacobian * (m11 * m21 + m12 * m22)
        cbb = jacobian * (m21 * m21 + m22 * m22)
        at = coefs_at(r, g)
        if at is not None:
            coefs[at : at + 8, :] = caa
            coefs[at + 8 : at + 16, :] = cab
            coefs[at + 16 : at + 24, :] = cbb
        mass = jacobian * weight
        at = slope_at[r, g]
        first = slice(g * 2 * LANES, (g * 2 + 1) * LANES)
        second = slice((g * 2 + 1) * LANES, (g * 2 + 2) * LANES)
        part = slice(g * LANES, (g + 1) * LANES)
        to, direct = flux_at[r], plain_at[r]
        for f in range(FIELDS):
            one, two = fluxes(slopes[at + 8 * f : at + 8 * f + 8, :], (caa, cab, cbb))
            flux[to + 8 * f : to + 8 * f + 8, first] = one
            flux[to + 8 * f : to + 8 * f + 8, second] = two
        plain[direct : direct + 8, part] = mass
        if r in (0, 7):
            continue
        zonal, meridional = tile(r, g, 0, 8), tile(r, g, 8, 8)
        flow1 = jacobian * (m11 * zonal + m12 * meridional)
        flow2 = jacobian * (m21 * zonal + m22 * meridional)
        for k in range(2):
            carried = tile(r, g, 24 + 8 * k, 8)
            flux[to + 40 + 8 * k : to + 48 + 8 * k, first] = carried * flow1
            flux[to + 40 + 8 * k : to + 48 + 8 * k, second] = carried * flow2
        ea, eb = slopes[at + 40 : at + 48, :LANES], slopes[at + 40 : at + 48, LANES:]
        ta, tb = slopes[at + 16 : at + 24, :LANES], slopes[at + 16 : at + 24, LANES:]
        plain[direct + 8 : direct + 16, part] = mass * (
            coriolis * meridional - (m11 * ea + m21 * eb)
        )
        plain[direct + 16 : direct + 24, part] = -mass * (
            coriolis * zonal + (m12 * ea + m22 * eb)
        )
        plain[direct + 24 : direct + 32, part] = -mass * (
            zonal * (m11 * ta + m21 * tb) + meridional * (m12 * ta + m22 * tb)
        )
    spread = divergence_joined(flux[...], matrices)
    upper, lower = halves(plain[...])
    return spread, both_parts(upper, lower, matrices[1408:1664, :])


def face_masks():
    lane = lane_iota((1, LANES)) % 16
    return (lane < 4).astype(F32), (lane >= 12).astype(F32)


def repeated(block):
    return jnp.concatenate([block] * FIELDS, axis=0)


def second_laplacian(rows, smoothing, inverse, coefficients, matrices):
    smooth = [smoothing[r][g] * repeated(inverse[r, g]) for r in rows for g in range(2)]
    again = gradient(jnp.concatenate(smooth, axis=0), matrices)
    flat = []
    for n, r in enumerate(rows):
        parts = []
        for g in range(2):
            triple = tuple(repeated(coefficients(r, g, k)) for k in range(3))
            start = (2 * n + g) * STATE
            parts += list(fluxes(again[start : start + STATE, :], triple))
        flat.append(jnp.concatenate(parts, axis=1))
    return divergence_joined(jnp.concatenate(flat, axis=0), matrices)


def mass_inverse(mass_sum):
    return 1.0 / jnp.where(mass_sum > 0.0, mass_sum, 1.0)


def advanced(state, straight, carried, inverse):
    return state + (TIME_STEP * jnp.concatenate([straight, -carried], axis=0)) * repeated(inverse)


OWN_ROWS = (2, 3, 4, 5)
OUTER_ROWS = (0, 1, 6, 7)
MIDDLE_ROWS = (3, 4)
EDGE_ROWS = (1, 2, 5, 6)


def inner_kernel(
    low_ref,
    high_ref,
    matrices,
    lists_ref,
    spread_ref,
    direct_ref,
    coefs,
    picks_ref,
    middle_ref,
    damped_ref,
    inverse_ref,
    slopes,
    flux,
    plain,
):
    def tile(r, g, start=0, size=TILE):
        offset = ((r % 2) * 2 + g) * TILE + start
        return (low_ref if r < 4 else high_ref)[offset : offset + size, :]

    def coefs_at(r, g):
        return (2 * (r - 2) + g) * 24

    lists = send_lists([tile(r, g, STATE + 6, 1) for r in OWN_ROWS for g in range(2)])
    lists_ref[...] = lists
    line = (lists[0:1] + lists[1:2] + lists[2:3]).astype(jnp.int32) - 1
    row16 = row_iota((POINTS_DEV, 1024)).astype(jnp.int16)
    picks_ref[...] = jnp.where(
        row16 == line.astype(jnp.int16), jnp.bfloat16(1), jnp.bfloat16(0)
    )
    spread, direct = local_terms(
        OWN_ROWS, tile, matrices, slopes, flux, plain, coefs, coefs_at
    )
    spread_ref[...] = spread
    direct_ref[...] = direct
    masks = face_masks()

    def joined(value, size, r, start, count):
        def rows(k):
            at = (k - 2) * size + start
            return value[at : at + count, :]

        return rows_joined(rows(r - 1), rows(r), rows(r + 1), *masks)

    inverse, smoothing = {}, {}
    for r in MIDDLE_ROWS:
        mass_sum = joined(direct, 32, r, 0, 8)
        smoothing[r] = joined(spread, 56, r, 0, STATE)
        straight = joined(direct, 32, r, 8, 24)
        carried = joined(spread, 56, r, STATE, 16)
        for g in range(2):
            inverse[r, g] = mass_inverse(mass_sum[g])
            at = 2 * (r - 3) + g
            inverse_ref[8 * at : 8 * at + 8, :] = inverse[r, g]
            middle_ref[STATE * at : STATE * at + STATE, :] = advanced(
                tile(r, g, 0, STATE), straight[g], carried[g], inverse[r, g]
            )

    def coefficients(r, g, k):
        return coefs[coefs_at(r, g) + 8 * k : coefs_at(r, g) + 8 * k + 8, :]

    damped_ref[...] = second_laplacian(MIDDLE_ROWS, smoothing, inverse, coefficients, matrices)


def section_kernel(
    first_far_ref,
    second_far_ref,
    low_ref,
    high_ref,
    lists_ref,
    picks_ref,
    matrices,
    inner_spread,
    inner_direct,
    inner_coefs,
    middle_ref,
    middle_damped,
    middle_inverse,
    whole_ref,
    send_ref,
    outside,
    slopes,
    flux,
    plain,
    outer_coefs,
):
    even = lax.rem(lax.axis_index("curve"), 2) == 0
    outside[0] = jnp.where(even, second_far_ref[...], first_far_ref[...])
    outside[1] = jnp.where(even, first_far_ref[...], second_far_ref[...])

    def tile(r, g, start=0, size=TILE):
        offset = ((r % 2) * 2 + g) * TILE + start
        if r in OUTER_ROWS:
            return outside[r // 6, offset : offset + size, :]
        return (low_ref if r < 4 else high_ref)[offset : offset + size, :]

    outer_spread, outer_direct = local_terms(
        OUTER_ROWS,
        tile,
        matrices,
        slopes,
        flux,
        plain,
        outer_coefs,
        lambda r, g: {1: 24 * g, 6: 48 + 24 * g}.get(r),
    )
    masks = face_masks()
    _, outer_flux_at, outer_plain_at, _ = row_starts(OUTER_ROWS)
    _, inner_flux_at, inner_plain_at, _ = row_starts(OWN_ROWS)

    def joined(spread, r, start, count):
        def rows(k):
            if k in OUTER_ROWS:
                at = (outer_flux_at if spread else outer_plain_at)[k] + start
                return (outer_spread if spread else outer_direct)[at : at + count, :]
            at = (inner_flux_at if spread else inner_plain_at)[k] + start
            return (inner_spread if spread else inner_direct)[at : at + count, :]

        return rows_joined(rows(r - 1), rows(r), rows(r + 1), *masks)

    def coefficients(r, g, k):
        if r in OUTER_ROWS:
            at = (0 if r == 1 else 48) + 24 * g + 8 * k
            return outer_coefs[at : at + 8, :]
        at = (2 * (r - 2) + g) * 24 + 8 * k
        return inner_coefs[at : at + 8, :]

    inverse, smoothing = {}, {}
    for r in EDGE_ROWS:
        mass_sum = joined(False, r, 0, 8)
        smoothing[r] = joined(True, r, 0, STATE)
        for g in range(2):
            inverse[r, g] = mass_inverse(mass_sum[g])
    for r in MIDDLE_ROWS:
        for g in range(2):
            at = 8 * (2 * (r - 3) + g)
            inverse[r, g] = middle_inverse[at : at + 8, :]
    damped = second_laplacian(EDGE_ROWS, smoothing, inverse, coefficients, matrices)

    def damped_row(r):
        if r in MIDDLE_ROWS:
            return middle_damped[(r - 3) * STATE : (r - 2) * STATE, :]
        at = EDGE_ROWS.index(r) * STATE
        return damped[at : at + STATE, :]

    ordered = []
    for r in OWN_ROWS:
        damping = rows_joined(damped_row(r - 1), damped_row(r), damped_row(r + 1), *masks)
        if r not in MIDDLE_ROWS:
            straight = joined(False, r, 8, 24)
            carried = joined(True, r, STATE, 16)
        for g in range(2):
            if r in MIDDLE_ROWS:
                at = STATE * (2 * (r - 3) + g)
                base = middle_ref[at : at + STATE, :]
            else:
                base = advanced(tile(r, g, 0, STATE), straight[g], carried[g], inverse[r, g])
            ordered.append(
                base - ((TIME_STEP * HYPER_NU) * damping[g]) * repeated(inverse[r, g])
            )
    whole = jnp.concatenate(ordered, axis=1)
    whole_ref[...] = whole
    shares = [(lists_ref[k : k + 1, :] > 0.0).astype(F32) for k in range(3)]
    slots = [jnp.broadcast_to(lists_ref[3:4, :] * shares[k], (8, 1024)) for k in range(3)]
    row = row_iota((8, 1024))
    slot_rows = sum(jnp.where(row == k, slots[k], 0.0) for k in range(3))
    columns = jnp.concatenate([whole * share for share in shares] + [slot_rows], axis=0)
    upper, lower = halves(columns)
    sent = dot_last(picks_ref[...], jnp.concatenate([upper, lower], axis=0))
    send_ref[...] = sent[:, :LANES] + sent[:, LANES:]


def receive_kernel(
    received_ref, whole_ref, hits_ref, updated_ref, physics_ref, updated, pieces, sems
):
    whole = whole_ref[...]
    upper = whole.astype(BF16).astype(F32)
    restored = dot(jnp.concatenate([upper, whole - upper], axis=0).astype(BF16), hits_ref[...])
    updated[...] = restored[:STATE] + restored[STATE:]
    copies = [pltpu.make_async_copy(updated, updated_ref, sems.at[3])]
    copies[0].start()
    turned_over = received_ref[...].T
    upper, lower = halves(turned_over)
    places = slice(3 * STATE, 3 * STATE + 3)
    slot = turned_over[places, :].astype(jnp.int32) - 1
    slots = [slot[k : k + 1].astype(jnp.int16) for k in range(3)]
    both = jnp.concatenate([upper, lower], axis=0)
    count = 2 * LANES
    for start in range(0, POINTS_DEV, count):
        row = (row_iota((count, POINTS_DEV)) + start).astype(jnp.int16)
        hits = (row == slots[0]) | (row == slots[1]) | (row == slots[2])
        rows = dot_last(both, jnp.where(hits, jnp.bfloat16(1), jnp.bfloat16(0)))
        rows = rows[:LANES] + rows[LANES:]
        own = rows[places, :] == (lane_iota((3, count)) + (start + 1)).astype(F32)
        piece = start // count
        pieces[piece] = jnp.where(
            own[0:1],
            rows[:STATE],
            jnp.where(own[1:2], rows[STATE : 2 * STATE], rows[2 * STATE : 3 * STATE]),
        )
        copies.append(
            pltpu.make_async_copy(
                pieces.at[piece], physics_ref.at[:, pl.ds(start, count)], sems.at[piece]
            )
        )
        copies[-1].start()
    for copy in copies:
        copy.wait()


def call(kernel, shapes, scratch=(), flops=0, moved=0, vmem=VMEM_LIMIT, **specs):
    return pl.pallas_call(
        kernel,
        out_shape=[
            jax.ShapeDtypeStruct(*s) if isinstance(s, tuple) else s for s in shapes
        ],
        scratch_shapes=list(scratch),
        **specs,
        compiler_params=pltpu.CompilerParams(vmem_limit_bytes=vmem),
        cost_estimate=pl.CostEstimate(flops=flops, bytes_accessed=moved, transcendentals=0),
    )


def swaps(count, pairs_from):
    route = []
    for i in range(pairs_from, count - 1, 2):
        route += [(i, i + 1), (i + 1, i)]
    return route


def body(
    evolving_state_array, point_id, neighbours, jacobian, inverse_metric, coriolis, column_slot
):
    anywhere = pl.BlockSpec(memory_space=pltpu.HBM)
    half = ((4 * TILE, LANES), F32)
    strip = ((TILE, LANES), F32)
    values_shape = ((TILE + 8, POINTS_DEV), F32)
    far, close, values = call(
        strip_kernel,
        [pltpu.VMEM(*strip), pltpu.VMEM(*strip), pltpu.VMEM(*values_shape)],
        scratch=[
            pltpu.VMEM((8, ELEMS_DEV), jnp.int32),
            pltpu.VMEM((POINTS_DEV,), F32),
            pltpu.VMEM((POINTS_DEV,), F32),
            pltpu.VMEM((4, POINTS_DEV), F32),
            pltpu.VMEM((POINTS_DEV,), jnp.int32),
            pltpu.VMEM((FIELDS, LEV, POINTS_DEV), F32),
            pltpu.SemaphoreType.DMA((6,)),
        ],
        in_specs=[anywhere] * 6,
        vmem=64 * 1024 * 1024 - 524288,
    )(evolving_state_array, jacobian, coriolis, inverse_metric, neighbours, column_slot)
    cols, rows = lax.axis_size("col"), lax.axis_size("curve")
    from_far = lax.ppermute(far, "col", swaps(cols, 1) + [(cols - 1, 0), (0, cols - 1)])
    from_close = lax.ppermute(close, "col", swaps(cols, 0))
    low, high, hits = call(
        arrange_kernel,
        [half, half, pltpu.VMEM((1024, POINTS_DEV), BF16)],
        flops=400_000_000,
        moved=1_000_000,
    )(values)
    first, second, low, high = call(margin_kernel, [half] * 4)(low, high, from_far, from_close)
    second_far = lax.ppermute(second, "curve", swaps(rows, 1))
    first_far = lax.ppermute(first, "curve", swaps(rows, 0))
    matrices = jnp.asarray(operators())
    def scratch(rows):
        slope_rows, flux_rows, plain_rows = row_starts(rows)[3]
        return [
            pltpu.VMEM((slope_rows, 2 * LANES), F32),
            pltpu.VMEM((flux_rows, 4 * LANES), F32),
            pltpu.VMEM((plain_rows, 2 * LANES), F32),
        ]

    inner = call(
        inner_kernel,
        [
            ((8, 1024), F32),
            ((4 * 56, 2 * LANES), F32),
            ((4 * 32, 2 * LANES), F32),
            ((8 * 24, LANES), F32),
            ((POINTS_DEV, 1024), BF16),
            ((4 * STATE, LANES), F32),
            ((2 * STATE, 2 * LANES), F32),
            ((4 * 8, LANES), F32),
        ],
        scratch=scratch(OWN_ROWS),
        flops=400_000_000,
        moved=1_000_000,
    )(low, high, matrices)
    lists, spread, direct, coefs, picks, middle, middle_damped, middle_inverse = inner
    whole, sent = call(
        section_kernel,
        [((STATE, 1024), F32), ((POINTS_DEV, LANES), F32)],
        scratch=[pltpu.VMEM((2, 4 * TILE, LANES), F32)]
        + scratch(OUTER_ROWS)
        + [pltpu.VMEM((4 * 24, LANES), F32)],
    )(
        first_far,
        second_far,
        low,
        high,
        lists,
        picks,
        matrices,
        spread,
        direct,
        coefs,
        middle,
        middle_damped,
        middle_inverse,
    )
    received = lax.all_to_all(sent, "col", split_axis=0, concat_axis=0, tiled=True)
    updated, physics = call(
        receive_kernel,
        [((STATE, POINTS_DEV), F32)] * 2,
        scratch=[
            pltpu.VMEM((STATE, POINTS_DEV), F32),
            pltpu.VMEM((3, STATE, 2 * LANES), F32),
            pltpu.SemaphoreType.DMA((4,)),
        ],
        in_specs=[pl.BlockSpec(memory_space=pltpu.VMEM)] * 3,
        out_specs=[anywhere] * 2,
    )(received, whole, hits)
    shape = evolving_state_array.shape
    return updated.reshape(shape), physics.reshape(shape)


def solution(mesh):
    split = ("curve", "col")
    return jax.shard_map(
        body,
        mesh=mesh,
        in_specs=(
            P(None, None, split),
            P(split),
            P(None, split),
            P(split),
            P(None, split),
            P(split),
            P(split),
        ),
        out_specs=(P(None, None, split), P(None, None, split)),
        check_vma=False,
    )
```
